32 devices in a mesh: grp: 2 (over x), ap: 16 (over z, y, core).
Axes of the slice: x: 2, y: 2, z: 4, core: 2. Of those that a mesh axis runs over, the one named last changes fastest.
Arguments:
- raw_echo: bfloat16 [2, 4096, 1024], P(None, 'ap', 'grp'), parts along dimension 2, may hold values from -6 to 6
- range_filter: float32 [2, 4096], replicated, may hold values from -4.2 to 4.2
- range_offsets: int32 [1024], P(('grp', 'ap')), parts along dimension 0, may hold values from 0 to 4095
- interp_weight: bfloat16 [2, 2, 2, 256, 128], replicated, may hold values from -0.25 to 0.25
- phase_rate: float32 [2], replicated, may hold values from 2 to 12
Outputs:
- focused: float32 [2, 1024, 32768], P(None, None, ('grp', 'ap')), parts along dimension 2
The draws below stay inside these ranges and needn't reach their ends.
There are 2 independent parts, one for each index of `grp`. The reference program is written for one: setup_inputs(seed, part) draws one part's arguments, and reference() takes and returns one part's arrays. A program takes and returns all parts, laid end to end along the dimension named above; an argument that names none is the same for every part. Nothing has to cross between parts.
All inputs are finite; a program needn't handle non-finite values.
Results may differ from the reference program's by a relative error of at most 0.012.
Values may be sent and summed in bfloat16 or wider, within the bound.
No kernel may reach another device: no remote copies, remote signals or barrier semaphores. Data moves between devices by JAX's collectives and lax.ppermute only.
A program may use at most 128 MiB of HBM per device.

```python
import math
import jax
import jax.numpy as jnp
from jax import lax

R = 4096
A0 = 256
AB = 128
SECTIONS = 2
PULSE_DEV = 32
P_SIZE = 512
MEMBERS = 4
GROUPS = 4
A_OUT = 1024


def with_ends(entries, stream_key, low, top_value):
    index_at = [jax.random.randint(jax.random.fold_in(stream_key, axis), (), 0, length) for axis, length in enumerate(entries.shape)]
    main_axis = entries.shape.index(max(entries.shape))
    beside = index_at[:main_axis] + [(index_at[main_axis] + 1) % entries.shape[main_axis]] + index_at[main_axis + 1:]
    return entries.at[tuple(index_at)].set(low).at[tuple(beside)].set(top_value)


def level_of(rng, extent, split, smallest, top_value):
    factor_of, own = 1.0, jax.random.fold_in(rng, 6)
    for dim, shards_of in split:
        heights = jnp.exp(jax.random.uniform(jax.random.fold_in(own, dim), (shards_of,), jnp.float32, smallest / len(split), top_value / len(split)))
        factor_of = factor_of * jnp.repeat(heights, extent[dim] // shards_of).reshape([-1 if axis == dim else 1 for axis in range(len(extent))])
    return factor_of


def scatter_about(rng, dims, scale, limit, pieces=(), held_as=jnp.bfloat16):
    result = jax.random.normal(rng, dims, jnp.float32) * scale
    if len(pieces) > 0:
        result = level_of(rng, dims, pieces, -0.22, 0.18) * result
    return jnp.clip(result, min=-limit, max=limit).astype(held_as)


def setup_inputs(seed: int = 0, part: int = 0) -> dict:
    keys = jax.random.split(jax.random.key(seed), 6)
    part_splits = jax.random.split(jax.random.fold_in(keys[5], part), 6)
    return {
        "raw_echo": scatter_about(part_splits[0], (2, R, P_SIZE), 1.0, 6.0, ((1, 16),)),
        "range_filter": scatter_about(keys[1], (2, R), 0.7, 4.2, (), jnp.float32),
        "range_offsets": with_ends(jax.random.randint(part_splits[2], (P_SIZE,), 0, R), jax.random.fold_in(part_splits[2], 1), 0, R - 1).astype(jnp.int32),
        "interp_weight": scatter_about(keys[3], (SECTIONS, 2, 2, 2 * AB, AB), (4 * AB) ** -0.5, 0.25),
        "phase_rate": jnp.clip(jnp.exp(jax.random.uniform(keys[4], (SECTIONS,), jnp.float32, math.log(2.0), math.log(12.0))), 2.0, 12.0),
    }


def steer_table(angle_count, pulse_count):
    angle_index = jnp.arange(angle_count, dtype=jnp.int32)[:, None]
    pulse_index = jnp.arange(pulse_count, dtype=jnp.int32)[None, :]
    turn_count = (angle_index + angle_count // 2) * pulse_index % angle_count
    angle_value = -2.0 * math.pi / angle_count * turn_count.astype(jnp.float32)
    scaling = 1.0 / math.sqrt(pulse_count)
    return jnp.stack([jnp.cos(angle_value) * scaling, jnp.sin(angle_value) * scaling]).astype(jnp.bfloat16)

def compress_all(raw_echo, range_filter, range_offsets):
    samples = lax.complex(raw_echo[0].astype(jnp.float32), raw_echo[1].astype(jnp.float32))
    spectrum = jnp.fft.fft(samples, axis=0)
    bin_index = jnp.arange(R, dtype=jnp.int32)
    turn_count = bin_index[:, None] * range_offsets[None, :] % R
    angle_value = -2.0 * math.pi / R * turn_count.astype(jnp.float32)
    shift_ramp = lax.complex(jnp.cos(angle_value), jnp.sin(angle_value))
    filter_spec = lax.complex(range_filter[0], range_filter[1])
    profile = jnp.fft.ifft(spectrum * filter_spec[:, None] * shift_ramp, axis=0)
    return jnp.stack([jnp.real(profile).T, jnp.imag(profile).T]).astype(jnp.bfloat16)

def focus_group(group_data, steering, interp_weight, phase_rate):
    values = group_data.astype(jnp.float32)
    steer_real = steering[0].astype(jnp.float32)
    steer_imag = steering[1].astype(jnp.float32)
    real_part = jnp.einsum('ap,spr->sar', steer_real, values[0]) - jnp.einsum('ap,spr->sar', steer_imag, values[1])
    imag_part = jnp.einsum('ap,spr->sar', steer_real, values[1]) + jnp.einsum('ap,spr->sar', steer_imag, values[0])
    images = jnp.stack([real_part, imag_part], axis=1).astype(jnp.bfloat16)
    for merge_step in range(SECTIONS):
        angle_count = images.shape[2]
        paired = images.reshape(-1, 2, 2, angle_count, R)
        products = []
        for child_index in range(2):
            weights = interp_weight[merge_step, child_index].astype(jnp.float32)
            blocked = paired[:, child_index].astype(jnp.float32).reshape(-1, 2, angle_count // AB, AB, R)
            real_part = jnp.einsum('pa,njar->njpr', weights[0], blocked[:, 0]) - jnp.einsum('pa,njar->njpr', weights[1], blocked[:, 1])
            imag_part = jnp.einsum('pa,njar->njpr', weights[0], blocked[:, 1]) + jnp.einsum('pa,njar->njpr', weights[1], blocked[:, 0])
            products.append(jnp.stack([real_part, imag_part], axis=1).reshape(-1, 2, 2 * angle_count, R))
        angle_pos = (jnp.arange(2 * angle_count, dtype=jnp.float32) + 0.5) / (2 * angle_count) - 0.5
        factor = 1.0 + jnp.arange(R, dtype=jnp.float32) / R
        phase_angle = phase_rate[merge_step] * angle_pos[:, None] * factor[None, :]
        cosine = jnp.cos(phase_angle)
        sine_term = jnp.sin(phase_angle)
        lower_term, upper_term = products
        summed = lower_term + upper_term
        differ = upper_term - lower_term
        merged = jnp.stack([cosine * summed[:, 0] - sine_term * differ[:, 1], cosine * summed[:, 1] + sine_term * differ[:, 0]], axis=1)
        images = merged.astype(jnp.bfloat16) if merge_step + 1 < SECTIONS else merged
    return images[0]

def reference(raw_echo, range_filter, range_offsets, interp_weight, phase_rate):
    compressed = compress_all(raw_echo, range_filter, range_offsets)
    grouped = jnp.moveaxis(compressed.reshape(2, GROUPS, MEMBERS, PULSE_DEV, R), 1, 0)
    steering = steer_table(A0, PULSE_DEV)
    focused = lax.map(lambda group_data: focus_group(group_data, steering, interp_weight, phase_rate), grouped)
    return jnp.transpose(focused, (1, 2, 0, 3)).reshape(2, A_OUT, GROUPS * R)
```

```python
import functools
import math

import jax
import jax.numpy as jnp
import ml_dtypes
import numpy as np
from jax import lax
from jax.experimental import pallas as pl
from jax.experimental.pallas import tpu as pltpu
from jax.sharding import PartitionSpec as P

A0 = 256
QUAD = 4
LANES = 128
FIRST = 16
TILE = 16


def as_real(matrix):
    top = np.concatenate([matrix.real, -matrix.imag], 1)
    low = np.concatenate([matrix.imag, matrix.real], 1)
    return np.concatenate([top, low], 0).astype(ml_dtypes.bfloat16)


def root(length, turns):
    return np.exp(-2j * np.pi / length * (turns % length))


def dft_tables(total):
    second = total // FIRST
    one = np.arange(FIRST)
    low = np.arange(TILE)
    k_one = one[:, None, None, None]
    l_row = low[None, :, None, None]
    n_one = one[None, None, :, None]
    l_col = low[None, None, None, :]
    same = l_row == l_col
    forward_one = root(FIRST, k_one * n_one) * root(total, l_row * k_one) * same
    forward_one = forward_one.reshape(FIRST * TILE, FIRST * TILE)
    two = np.arange(second)
    forward_two = root(second, two[:, None] * two[None, :])
    inverse_two = forward_two.conj()
    kept = np.arange(FIRST // QUAD)[:, None, None, None]
    inverse_one = (root(FIRST, kept * n_one) * root(total, l_col * n_one)).conj() * same
    inverse_one = inverse_one.reshape(FIRST // QUAD * TILE, FIRST * TILE)
    return [as_real(t) for t in (forward_one, forward_two, inverse_two, inverse_one)]


def steer_table(angle_count, pulse_count):
    angle_index = np.arange(angle_count)[:, None]
    pulse_index = np.arange(pulse_count)[None, :]
    value = root(angle_count, (angle_index + angle_count // 2) * pulse_index)
    value = value / math.sqrt(pulse_count)
    return np.stack([value.real, value.imag]).astype(ml_dtypes.bfloat16)


def unit(angle):
    return jnp.cos(angle), jnp.sin(angle)


def times(left, right):
    return (
        left[0] * right[0] - left[1] * right[1],
        left[0] * right[1] + left[1] * right[0],
    )


def spectrum_gain(range_filter, offsets, quarter, total):
    second = total // FIRST
    shift = offsets - quarter * (total // QUAD)
    k_one = jnp.arange(FIRST, dtype=jnp.int32)[:, None]
    k_two = jnp.arange(second, dtype=jnp.int32)[:, None]
    scale = -2.0 * math.pi / total
    part_one = unit(scale * (k_one * shift % total).astype(jnp.float32))
    part_two = unit(scale * (FIRST * k_two * shift % total).astype(jnp.float32))
    by_k = range_filter.reshape(2, second, FIRST).transpose(0, 2, 1) / total
    ramp = times(
        (part_one[0][:, None], part_one[1][:, None]),
        (part_two[0][None], part_two[1][None]),
    )
    return jnp.stack(times((by_k[0][:, :, None], by_k[1][:, :, None]), ramp))


def level_one_rows(weight, pulse_count):
    steer = jnp.asarray(steer_table(A0, pulse_count)).reshape(2, -1, weight.shape[3], pulse_count)
    dot = functools.partial(
        jnp.einsum, "cpj,bjq->bpcq", preferred_element_type=jnp.float32
    )
    real = dot(weight[:, 0], steer[0]) - dot(weight[:, 1], steer[1])
    imag = dot(weight[:, 0], steer[1]) + dot(weight[:, 1], steer[0])
    angles = real.shape[0] * real.shape[1]
    sign = jnp.array([1.0, -1.0], jnp.float32)[:, None]
    rows = []
    for factor in (1.0, sign):
        real_f = (real * factor).reshape(angles, 2 * pulse_count)
        imag_f = (imag * factor).reshape(angles, 2 * pulse_count)
        rows += [(real_f, -imag_f), (imag_f, real_f)]
    zero = jnp.zeros((angles, LANES - 2 * pulse_count), jnp.float32)
    first = [jnp.concatenate([a, zero, b, zero], 1) for a, b in rows]
    other = [jnp.concatenate([zero, a, zero, b], 1) for a, b in rows]
    return jnp.stack([jnp.stack(first), jnp.stack(other)]).astype(jnp.bfloat16)


def level_two_rows(weight):
    return jnp.concatenate(
        [
            jnp.concatenate([weight[:, 0], -weight[:, 1]], 2),
            jnp.concatenate([weight[:, 1], weight[:, 0]], 2),
        ],
        1,
    )


def phase_table(rate, angles, start, width, total):
    angle_pos = (jnp.arange(angles, dtype=jnp.float32) + 0.5) / angles - 0.5
    slope = (rate * angle_pos)[None, :, None]
    blocks = width // LANES
    block_start = (start + LANES * jnp.arange(blocks, dtype=jnp.int32)).astype(jnp.float32)
    coarse = unit(slope * (1.0 + block_start / total)[:, None, None])
    fine = unit(slope * (jnp.arange(LANES, dtype=jnp.float32) / total)[None, None, :])
    return jnp.stack(times(coarse, fine)).astype(jnp.bfloat16)


def kernel(
    count,
    total,
    place_ref,
    fone_ref,
    ftwo_ref,
    itwo_ref,
    ione_ref,
    gain_ref,
    rows_one_ref,
    rows_two_ref,
    phase_one_ref,
    phase_two_ref,
    *rest,
):
    pieces = rest[:count]
    out_ref, samples, partial_ref, folded, compressed, image, sem = rest[count:]
    groups = count // QUAD
    span = total // count
    second = total // FIRST
    chunks = second // TILE
    f32 = jnp.float32

    def dot(left, right):
        return jnp.dot(left, right, preferred_element_type=f32)

    @pl.when(pl.program_id(0) == 0)
    def _():
        group = place_ref[0]
        member = place_ref[1]
        copies = []
        for rel in range(QUAD):
            for step in range(groups):
                source = QUAD * lax.rem(group - step + groups, groups) + (member ^ rel)
                first_row = pl.multiple_of(source * span, span)
                copies.append(
                    pltpu.make_async_copy(
                        pieces[rel * groups + step],
                        samples.at[:, pl.ds(first_row, span), :],
                        sem,
                    )
                )
        for copy in copies:
            copy.start()
        for copy in copies:
            copy.wait()

        def chunk_of(part, chunk):
            picked = [
                samples[part, n_one * second + chunk * TILE : n_one * second + (chunk + 1) * TILE, :]
                for n_one in range(FIRST)
            ]
            return jnp.concatenate(picked, 0)

        half = FIRST * TILE
        for pair in range(chunks // 2):
            right = jnp.concatenate(
                [
                    jnp.concatenate([chunk_of(0, c), chunk_of(1, c)], 0)
                    for c in (2 * pair, 2 * pair + 1)
                ],
                1,
            )
            result = dot(fone_ref[...], right)
            for side in range(2):
                chunk = 2 * pair + side
                lanes = slice(side * LANES, (side + 1) * LANES)
                for k_one in range(FIRST):
                    real = result[k_one * TILE : (k_one + 1) * TILE, lanes]
                    imag = result[half + k_one * TILE : half + (k_one + 1) * TILE, lanes]
                    turn = -2.0 * math.pi * (TILE * chunk * k_one % total) / total
                    cosine, sine = math.cos(turn), math.sin(turn)
                    at = slice(chunk * TILE, (chunk + 1) * TILE)
                    partial_ref[k_one, 0, at, :] = (cosine * real - sine * imag).astype(jnp.bfloat16)
                    partial_ref[k_one, 1, at, :] = (cosine * imag + sine * real).astype(jnp.bfloat16)

        for pair in range(FIRST // 2):
            right = jnp.concatenate(
                [partial_ref[k].reshape(2 * second, LANES) for k in (2 * pair, 2 * pair + 1)], 1
            )
            result = dot(ftwo_ref[...], right)
            scaled = []
            for side in range(2):
                k_one = 2 * pair + side
                lanes = slice(side * LANES, (side + 1) * LANES)
                real, imag = result[:second, lanes], result[second:, lanes]
                gain_real, gain_imag = gain_ref[0, k_one], gain_ref[1, k_one]
                scaled.append(
                    jnp.concatenate(
                        [
                            (real * gain_real - imag * gain_imag).astype(jnp.bfloat16),
                            (real * gain_imag + imag * gain_real).astype(jnp.bfloat16),
                        ],
                        0,
                    )
                )
            result = dot(itwo_ref[...], jnp.concatenate(scaled, 1))
            for side in range(2):
                k_one = 2 * pair + side
                lanes = slice(side * LANES, (side + 1) * LANES)
                for chunk in range(chunks):
                    real = result[chunk * TILE : (chunk + 1) * TILE, lanes]
                    imag = result[second + chunk * TILE : second + (chunk + 1) * TILE, lanes]
                    turn = 2.0 * math.pi * (TILE * chunk * k_one % total) / total
                    cosine, sine = math.cos(turn), math.sin(turn)
                    at = slice(k_one * TILE, (k_one + 1) * TILE)
                    folded[chunk, 0, at, :] = (cosine * real - sine * imag).astype(jnp.bfloat16)
                    folded[chunk, 1, at, :] = (cosine * imag + sine * real).astype(jnp.bfloat16)

        kept = FIRST // QUAD
        for pair in range(chunks // 2):
            right = jnp.concatenate(
                [folded[c].reshape(2 * half, LANES) for c in (2 * pair, 2 * pair + 1)], 1
            )
            result = dot(ione_ref[...], right).astype(jnp.bfloat16)
            for side in range(2):
                chunk = 2 * pair + side
                lanes = slice(side * LANES, (side + 1) * LANES)
                for part in range(2):
                    for n_one in range(kept):
                        row = (part * kept + n_one) * TILE
                        compressed[
                            n_one * second + chunk * TILE : n_one * second + (chunk + 1) * TILE,
                            part * LANES : (part + 1) * LANES,
                        ] = result[row : row + TILE, lanes]

    width = out_ref.shape[2]
    blocks = width // LANES
    start = pl.multiple_of(pl.program_id(0) * width, width)
    columns = compressed[pl.ds(start, width), :]

    def phases(ref, rows):
        return [
            jnp.concatenate([ref[part, b, rows, :] for b in range(blocks)], 1).astype(f32)
            for part in range(2)
        ]

    block_angles = image.shape[3]
    for block in range(image.shape[1]):
        rows = slice(block * block_angles, (block + 1) * block_angles)
        cosine, sine = phases(phase_one_ref, rows)
        for pick in range(2):
            terms = [
                lax.dot_general(
                    rows_one_ref[pick, kind, rows, :],
                    columns,
                    (((1,), (1,)), ((), ())),
                    preferred_element_type=f32,
                )
                for kind in range(4)
            ]
            image[pick, block, 0] = (cosine * terms[0] + sine * terms[3]).astype(jnp.bfloat16)
            image[pick, block, 1] = (cosine * terms[1] - sine * terms[2]).astype(jnp.bfloat16)

    wide = rows_two_ref.shape[1] // 2
    for block in range(image.shape[1]):
        rows = slice(block * wide, (block + 1) * wide)
        cosine, sine = phases(phase_two_ref, rows)
        lower = dot(rows_two_ref[0], image[0, block].reshape(2 * block_angles, width))
        upper = dot(rows_two_ref[1], image[1, block].reshape(2 * block_angles, width))
        lower_real, lower_imag = lower[:wide], lower[wide:]
        upper_real, upper_imag = upper[:wide], upper[wide:]
        out_ref[0, rows, :] = cosine * (lower_real + upper_real) + sine * (lower_imag - upper_imag)
        out_ref[1, rows, :] = cosine * (lower_imag + upper_imag) + sine * (upper_real - lower_real)


def body(raw_echo, range_filter, range_offsets, interp_weight, phase_rate):
    count = lax.axis_size("ap")
    index = lax.axis_index("ap")
    total = range_filter.shape[1]
    pulse_count = range_offsets.shape[0]
    groups = count // QUAD
    group, member = index // QUAD, index % QUAD

    def move(value, target):
        return lax.ppermute(value, "ap", [(i, target(i)) for i in range(count)])

    def block_for(step):
        return lax.dynamic_slice_in_dim(
            raw_echo, (group + step) % groups * LANES, LANES, axis=2
        )

    own = [block_for(0)]
    for step in range(1, groups):
        own.append(move(block_for(step), lambda i, s=step: (i + QUAD * s) % count))
    across = [move(piece, lambda i: i ^ 2) for piece in own]
    beside = [move(piece, lambda i: i ^ 1) for piece in own]
    diagonal = [move(piece, lambda i: i ^ 1) for piece in across]
    pieces = own + beside + across + diagonal

    offset_near = jnp.stack([range_offsets, move(range_offsets, lambda i: i ^ 1)])
    offset_far = move(offset_near, lambda i: i ^ 2)
    offsets = jnp.concatenate([offset_near, offset_far])[
        jnp.arange(QUAD, dtype=jnp.int32) ^ member
    ].reshape(1, QUAD * pulse_count)

    gain = spectrum_gain(range_filter, offsets, member, total)
    rows_one = level_one_rows(interp_weight[0], pulse_count)
    rows_two = level_two_rows(interp_weight[1])
    width = total // QUAD
    start = member * width
    phase_one = phase_table(phase_rate[0], 2 * A0, start, width, total)
    phase_two = phase_table(phase_rate[1], 4 * A0, start, width, total)
    place = jnp.stack([group, member]).astype(jnp.int32)
    tables = [jnp.asarray(t) for t in dft_tables(total)]

    step_width = 256
    second = total // FIRST
    chunks = second // TILE

    def whole(array):
        return pl.BlockSpec(array.shape, lambda i, n=array.ndim: (0,) * n)

    def by_range(array):
        shape = array.shape[:1] + (step_width // LANES,) + array.shape[2:]
        return pl.BlockSpec(shape, lambda i: (0, i, 0, 0))

    bf16 = jnp.bfloat16
    return pl.pallas_call(
        functools.partial(kernel, count, total),
        grid=(width // step_width,),
        out_shape=jax.ShapeDtypeStruct((2, 4 * A0, width), jnp.float32),
        in_specs=[pl.BlockSpec(memory_space=pltpu.SMEM)]
        + [whole(a) for a in tables + [gain, rows_one, rows_two]]
        + [by_range(phase_one), by_range(phase_two)]
        + [pl.BlockSpec(memory_space=pl.ANY)] * len(pieces),
        out_specs=pl.BlockSpec((2, 4 * A0, step_width), lambda i: (0, 0, i)),
        scratch_shapes=[
            pltpu.VMEM((2, total, LANES), bf16),
            pltpu.VMEM((FIRST, 2, second, LANES), bf16),
            pltpu.VMEM((chunks, 2, FIRST * TILE, LANES), bf16),
            pltpu.VMEM((width, 2 * LANES), bf16),
            pltpu.VMEM((2, 4, 2, LANES, step_width), bf16),
            pltpu.SemaphoreType.DMA,
        ],
        compiler_params=pltpu.CompilerParams(vmem_limit_bytes=48 * 1024 * 1024),
    )(place, *tables, gain, rows_one, rows_two, phase_one, phase_two, *pieces)


def solution(mesh):
    placed = (P(None, "ap", "grp"), P(), P(("grp", "ap")), P(), P())
    return jax.shard_map(
        body, mesh=mesh, in_specs=placed, out_specs=P(None, None, ("grp", "ap")), check_vma=False
    )
```

```python
import functools
import math

import jax
import jax.numpy as jnp
import ml_dtypes
import numpy as np
from jax import lax
from jax.experimental import pallas as pl
from jax.experimental.pallas import tpu as pltpu
from jax.sharding import PartitionSpec as P

A0 = 256
QUAD = 4
LANES = 128
FIRST = 16
TILE = 16


def as_real(matrix):
    top = np.concatenate([matrix.real, -matrix.imag], 1)
    low = np.concatenate([matrix.imag, matrix.real], 1)
    return np.concatenate([top, low], 0).astype(ml_dtypes.bfloat16)


def root(length, turns):
    return np.exp(-2j * np.pi / length * (turns % length))


def dft_tables(total):
    second = total // FIRST
    one = np.arange(FIRST)
    low = np.arange(TILE)
    k_one = one[:, None, None, None]
    l_row = low[None, :, None, None]
    n_one = one[None, None, :, None]
    l_col = low[None, None, None, :]
    same = l_row == l_col
    forward_one = root(FIRST, k_one * n_one) * root(total, l_row * k_one) * same
    forward_one = forward_one.reshape(FIRST * TILE, FIRST * TILE)
    two = np.arange(second)
    forward_two = root(second, two[:, None] * two[None, :])
    inverse_two = forward_two.conj()
    kept = np.arange(FIRST // QUAD)[:, None, None, None]
    inverse_one = (root(FIRST, kept * n_one) * root(total, l_col * n_one)).conj() * same
    inverse_one = inverse_one.reshape(FIRST // QUAD * TILE, FIRST * TILE)
    return [as_real(t) for t in (forward_one, forward_two, inverse_two, inverse_one)]


def steer_table(angle_count, pulse_count):
    angle_index = np.arange(angle_count)[:, None]
    pulse_index = np.arange(pulse_count)[None, :]
    value = root(angle_count, (angle_index + angle_count // 2) * pulse_index)
    value = (value / math.sqrt(pulse_count)).astype(np.complex64)
    return value.real.astype(ml_dtypes.bfloat16), value.imag.astype(ml_dtypes.bfloat16)


def steer_blocks(pulse_count, child_angles):
    real, imag = steer_table(A0, pulse_count)
    real, imag = real[:child_angles], imag[:child_angles]
    table = np.zeros((2, 2, child_angles, 2, 2, 2, 2, 2, pulse_count), ml_dtypes.bfloat16)
    for pair in range(2):
        for child in range(2):
            spot = (pair, child)
            table[child, 0, :, pair, 0, 0, *spot] = real
            table[child, 0, :, pair, 0, 1, *spot] = -imag
            table[child, 1, :, pair, 0, 0, *spot] = -imag
            table[child, 1, :, pair, 0, 1, *spot] = -real
            table[child, 0, :, pair, 1, 0, *spot] = imag
            table[child, 0, :, pair, 1, 1, *spot] = real
            table[child, 1, :, pair, 1, 0, *spot] = real
            table[child, 1, :, pair, 1, 1, *spot] = -imag
    return table.reshape(4 * child_angles, 32 * pulse_count)


def small_unit(angle):
    square = angle * angle
    cosine = 1.0 + square * (-1 / 2 + square * (1 / 24 + square * (-1 / 720 + square / 40320)))
    sine = angle * (1.0 + square * (-1 / 6 + square * (1 / 120 + square * (-1 / 5040))))
    return cosine, sine


def unit(angle):
    quarter = jnp.floor(angle * (2.0 / math.pi) + 0.5)
    rest = angle - quarter * 1.5703125
    rest = rest - quarter * (math.pi / 2 - 1.5703125)
    cosine, sine = small_unit(rest)
    turn = quarter.astype(jnp.int32)
    odd = (turn & 1) == 1
    first = jnp.where(odd, sine, cosine)
    second = jnp.where(odd, cosine, sine)
    first = jnp.where(((turn + 1) & 2) == 2, -first, first)
    second = jnp.where((turn & 2) == 2, -second, second)
    return first, second


def times(left, right):
    return (
        left[0] * right[0] - left[1] * right[1],
        left[0] * right[1] + left[1] * right[0],
    )


def cut_kernel(place_ref, raw_ref, *outs):
    for step, out in enumerate(outs):
        first = pl.multiple_of((place_ref[0] ^ step) * LANES, LANES)
        out[...] = raw_ref[:, :, pl.ds(first, LANES)]


def phase_kernel(total, place_ref, rate_ref, one_ref, two_ref):
    start = (place_ref[1] * (total // QUAD)).astype(jnp.float32)
    size = (LANES, LANES)
    for level, ref in ((0, one_ref), (1, two_ref)):
        blocks, angles = ref.shape[1], ref.shape[2]
        rate = rate_ref[level]
        lane = lax.broadcasted_iota(jnp.int32, size, 1).astype(jnp.float32)
        factor = 1.0 + (lane + start) / total

        @pl.loop(0, angles // LANES)
        def _(part):
            row = lax.broadcasted_iota(jnp.int32, size, 0) + part * LANES
            slope = rate * ((row.astype(jnp.float32) + 0.5) / angles - 0.5)
            value = unit(slope * factor)
            step = unit(slope * (LANES / total))
            at = pl.ds(pl.multiple_of(part * LANES, LANES), LANES)
            for block in range(blocks):
                ref[0, block, at, :] = value[0].astype(jnp.bfloat16)
                ref[1, block, at, :] = value[1].astype(jnp.bfloat16)
                if block + 1 < blocks:
                    value = times(value, step)


def weight_kernel(pulse_count, weight_ref, steer_ref, one_ref, two_ref):
    joined = jnp.concatenate([weight_ref[0, c, part] for c in range(2) for part in range(2)], 1)
    parents = joined.shape[0]
    width = one_ref.shape[3]
    lane = lax.broadcasted_iota(jnp.int32, (parents, width), 1)
    odd_pulse = lane % 2 == 1
    odd_child = lane // pulse_count % 2 == 1
    for pair in range(2):
        for part in range(2):
            at = (pair * 2 + part) * width
            value = jnp.dot(
                joined, steer_ref[:, at : at + width], preferred_element_type=jnp.float32
            )
            for block in range(one_ref.shape[2] // parents):
                rows = slice(block * parents, (block + 1) * parents)
                turned = jnp.where(odd_pulse, -value, value) if block % 2 else value
                one_ref[pair, part, rows, :] = turned.astype(jnp.bfloat16)
                one_ref[pair, 2 + part, rows, :] = jnp.where(odd_child, -turned, turned).astype(
                    jnp.bfloat16
                )
    for child in range(2):
        real, imag = weight_ref[1, child, 0], weight_ref[1, child, 1]
        two_ref[child] = jnp.concatenate(
            [jnp.concatenate([real, -imag], 1), jnp.concatenate([imag, real], 1)], 0
        )


def gain_kernel(total, place_ref, offset_ref, filter_ref, out_ref):
    second = total // FIRST
    offsets = jnp.concatenate(
        [
            offset_ref[pl.ds(place_ref[1] ^ member, 1), :]
            for member in range(QUAD)
        ],
        1,
    )
    shift = offsets - place_ref[1] * (total // QUAD)
    scale = -2.0 * math.pi / total

    def ramp(rows, stride):
        k_index = stride * lax.broadcasted_iota(jnp.int32, (rows, LANES), 0)
        return unit(scale * ((k_index * shift) & (total - 1)).astype(jnp.float32))

    low, high = ramp(FIRST, 1), ramp(second, FIRST)
    for k_one in range(FIRST):
        row = (low[0][k_one : k_one + 1] * (1.0 / total), low[1][k_one : k_one + 1] * (1.0 / total))
        column = (filter_ref[0, :, k_one : k_one + 1], filter_ref[1, :, k_one : k_one + 1])
        value = times(times(high, row), column)
        out_ref[0, k_one] = value[0]
        out_ref[1, k_one] = value[1]


def kernel(
    count,
    total,
    place_ref,
    fone_ref,
    ftwo_ref,
    itwo_ref,
    ione_ref,
    gain_ref,
    rows_one_ref,
    rows_two_ref,
    phase_one_ref,
    phase_two_ref,
    *rest,
):
    pieces = rest[:count]
    out_ref, samples, partial_ref, folded, compressed, image, ready, sems = rest[count:]
    groups = count // QUAD
    span = total // count
    second = total // FIRST
    chunks = second // TILE
    f32 = jnp.float32

    def dot(left, right):
        return jnp.dot(left, right, preferred_element_type=f32)

    index = place_ref[0] * QUAD + place_ref[1]
    for number, piece in enumerate(pieces):
        source = index ^ number
        first_row = pl.multiple_of(source * span, span)
        samples[:, pl.ds(first_row, span), :] = piece[...]

    def chunk_of(part, chunk):
        picked = [
            samples[part, n_one * second + chunk * TILE : n_one * second + (chunk + 1) * TILE, :]
            for n_one in range(FIRST)
        ]
        return jnp.concatenate(picked, 0)

    half = FIRST * TILE
    for pair in range(chunks // 2):
        right = jnp.concatenate(
            [
                jnp.concatenate([chunk_of(0, c), chunk_of(1, c)], 0)
                for c in (2 * pair, 2 * pair + 1)
            ],
            1,
        )
        result = dot(fone_ref[...], right)
        for side in range(2):
            chunk = 2 * pair + side
            lanes = slice(side * LANES, (side + 1) * LANES)
            for k_one in range(FIRST):
                real = result[k_one * TILE : (k_one + 1) * TILE, lanes]
                imag = result[half + k_one * TILE : half + (k_one + 1) * TILE, lanes]
                turn = -2.0 * math.pi * (TILE * chunk * k_one % total) / total
                cosine, sine = math.cos(turn), math.sin(turn)
                at = slice(chunk * TILE, (chunk + 1) * TILE)
                partial_ref[k_one, 0, at, :] = (cosine * real - sine * imag).astype(jnp.bfloat16)
                partial_ref[k_one, 1, at, :] = (cosine * imag + sine * real).astype(jnp.bfloat16)

    for pair in range(FIRST // 2):
        right = jnp.concatenate(
            [partial_ref[k].reshape(2 * second, LANES) for k in (2 * pair, 2 * pair + 1)], 1
        )
        result = dot(ftwo_ref[...], right)
        scaled = []
        for side in range(2):
            k_one = 2 * pair + side
            lanes = slice(side * LANES, (side + 1) * LANES)
            real, imag = result[:second, lanes], result[second:, lanes]
            gain_real, gain_imag = gain_ref[0, k_one], gain_ref[1, k_one]
            scaled.append(
                jnp.concatenate(
                    [
                        (real * gain_real - imag * gain_imag).astype(jnp.bfloat16),
                        (real * gain_imag + imag * gain_real).astype(jnp.bfloat16),
                    ],
                    0,
                )
            )
        result = dot(itwo_ref[...], jnp.concatenate(scaled, 1))
        for side in range(2):
            k_one = 2 * pair + side
            lanes = slice(side * LANES, (side + 1) * LANES)
            for chunk in range(chunks):
                real = result[chunk * TILE : (chunk + 1) * TILE, lanes]
                imag = result[second + chunk * TILE : second + (chunk + 1) * TILE, lanes]
                turn = 2.0 * math.pi * (TILE * chunk * k_one % total) / total
                cosine, sine = math.cos(turn), math.sin(turn)
                at = slice(k_one * TILE, (k_one + 1) * TILE)
                folded[chunk, 0, at, :] = (cosine * real - sine * imag).astype(jnp.bfloat16)
                folded[chunk, 1, at, :] = (cosine * imag + sine * real).astype(jnp.bfloat16)

    kept = FIRST // QUAD
    for pair in range(chunks // 2):
        right = jnp.concatenate(
            [folded[c].reshape(2 * half, LANES) for c in (2 * pair, 2 * pair + 1)], 1
        )
        result = dot(ione_ref[...], right).astype(jnp.bfloat16)
        for side in range(2):
            chunk = 2 * pair + side
            lanes = slice(side * LANES, (side + 1) * LANES)
            for part in range(2):
                for n_one in range(kept):
                    row = (part * kept + n_one) * TILE
                    compressed[
                        n_one * second + chunk * TILE : n_one * second + (chunk + 1) * TILE,
                        part * LANES : (part + 1) * LANES,
                    ] = result[row : row + TILE, lanes]

    width = image.shape[4]
    blocks = width // LANES
    block_angles = image.shape[3]
    steps = compressed.shape[0] // width

    def out_copy(step):
        at = pl.ds(step * width, width)
        return pltpu.make_async_copy(
            ready.at[step % 2], out_ref.at[:, :, at], sems.at[step % 2]
        )

    for step in range(steps):
        slot = step % 2
        columns = compressed[step * width : (step + 1) * width, :]

        def phases(ref, rows):
            return [
                jnp.concatenate(
                    [ref[part, step * blocks + b, rows, :] for b in range(blocks)], 1
                ).astype(f32)
                for part in range(2)
            ]

        for block in range(image.shape[1]):
            rows = slice(block * block_angles, (block + 1) * block_angles)
            cosine, sine = phases(phase_one_ref, rows)
            for pick in range(2):
                terms = [
                    lax.dot_general(
                        rows_one_ref[pick, kind, rows, :],
                        columns,
                        (((1,), (1,)), ((), ())),
                        preferred_element_type=f32,
                    )
                    for kind in range(4)
                ]
                image[pick, block, 0] = (cosine * terms[0] + sine * terms[3]).astype(jnp.bfloat16)
                image[pick, block, 1] = (cosine * terms[1] - sine * terms[2]).astype(jnp.bfloat16)

        if step >= 2:
            out_copy(step - 2).wait()
        wide = rows_two_ref.shape[1] // 2
        for block in range(image.shape[1]):
            rows = slice(block * wide, (block + 1) * wide)
            cosine, sine = phases(phase_two_ref, rows)
            lower = dot(rows_two_ref[0], image[0, block].reshape(2 * block_angles, width))
            upper = dot(rows_two_ref[1], image[1, block].reshape(2 * block_angles, width))
            lower_real, lower_imag = lower[:wide], lower[wide:]
            upper_real, upper_imag = upper[:wide], upper[wide:]
            ready[slot, 0, rows, :] = cosine * (lower_real + upper_real) + sine * (
                lower_imag - upper_imag
            )
            ready[slot, 1, rows, :] = cosine * (lower_imag + upper_imag) + sine * (
                upper_real - lower_real
            )
        out_copy(step).start()
    for step in range(max(steps - 2, 0), steps):
        out_copy(step).wait()


def body(raw_echo, range_filter, range_offsets, interp_weight, phase_rate):
    count = lax.axis_size("ap")
    index = lax.axis_index("ap")
    total = range_filter.shape[1]
    pulse_count = range_offsets.shape[0]
    groups = count // QUAD
    width = total // QUAD
    step_width = 256
    second = total // FIRST
    chunks = second // TILE
    f32, bf16 = jnp.float32, jnp.bfloat16
    smem = pl.BlockSpec(memory_space=pltpu.SMEM)
    vmem = pl.BlockSpec(memory_space=pltpu.VMEM)
    far = pl.BlockSpec(memory_space=pl.ANY)
    place = jnp.stack([index // QUAD, index % QUAD]).astype(jnp.int32)

    def move(value, bits):
        return lax.ppermute(value, "ap", [(i, i ^ bits) for i in range(count)])

    def shape(dims, kind=bf16):
        return jax.ShapeDtypeStruct(dims, kind)

    small = pltpu.CompilerParams(vmem_limit_bytes=2 * 1024 * 1024)

    def cost(flops, moved):
        return pl.CostEstimate(flops=flops, bytes_accessed=moved, transcendentals=0)

    cut = pl.pallas_call(
        cut_kernel,
        out_shape=[shape((2, total // count, LANES))] * groups,
        in_specs=[smem, vmem],
        out_specs=[vmem] * groups,
        compiler_params=small,
    )(place, raw_echo)
    own = [cut[0]] + [move(cut[step], QUAD * step) for step in range(1, groups)]
    across = [move(piece, 2) for piece in own]
    beside = [move(piece, 1) for piece in own]
    diagonal = [move(piece, 1) for piece in across]
    pieces = [part for four in zip(own, beside, across, diagonal) for part in four]

    offset_near = jnp.stack([range_offsets, move(range_offsets, 1)])
    offsets = jnp.concatenate([offset_near, move(offset_near, 2)])

    phase_one, phase_two = pl.pallas_call(
        functools.partial(phase_kernel, total),
        out_shape=[
            shape((2, width // LANES, 2 * A0, LANES)),
            shape((2, width // LANES, 4 * A0, LANES)),
        ],
        in_specs=[smem, smem],
        out_specs=[vmem, vmem],
        cost_estimate=cost(2**30, 2**23),
        compiler_params=small,
    )(place, phase_rate)
    child_angles = interp_weight.shape[4]
    rows_one, rows_two = pl.pallas_call(
        functools.partial(weight_kernel, pulse_count),
        out_shape=[
            shape((2, 4, 2 * A0, 2 * LANES)),
            shape((2, 2 * interp_weight.shape[3], 2 * child_angles)),
        ],
        in_specs=[vmem, vmem],
        out_specs=[vmem, vmem],
        cost_estimate=cost(2**29, 2**22),
        compiler_params=small,
    )(interp_weight, jnp.asarray(steer_blocks(pulse_count, child_angles)))
    gain = pl.pallas_call(
        functools.partial(gain_kernel, total),
        out_shape=shape((2, FIRST, second, LANES), f32),
        in_specs=[smem, vmem, vmem],
        out_specs=vmem,
        cost_estimate=cost(2**28, 2**22),
        compiler_params=small,
    )(place, offsets, range_filter.reshape(2, second, FIRST))

    tables = [jnp.asarray(t) for t in dft_tables(total)]
    return pl.pallas_call(
        functools.partial(kernel, count, total),
        out_shape=shape((2, 4 * A0, width), f32),
        in_specs=[smem] + [vmem] * (9 + count),
        out_specs=far,
        scratch_shapes=[
            pltpu.VMEM((2, total, LANES), bf16),
            pltpu.VMEM((FIRST, 2, second, LANES), bf16),
            pltpu.VMEM((chunks, 2, FIRST * TILE, LANES), bf16),
            pltpu.VMEM((width, 2 * LANES), bf16),
            pltpu.VMEM((2, 4, 2, child_angles, step_width), bf16),
            pltpu.VMEM((2, 2, 4 * A0, step_width), f32),
            pltpu.SemaphoreType.DMA((2,)),
        ],
        compiler_params=pltpu.CompilerParams(vmem_limit_bytes=24 * 1024 * 1024),
    )(place, *tables, gain, rows_one, rows_two, phase_one, phase_two, *pieces)


def solution(mesh):
    placed = (P(None, "ap", "grp"), P(), P(("grp", "ap")), P(), P())
    return jax.shard_map(
        body, mesh=mesh, in_specs=placed, out_specs=P(None, None, ("grp", "ap")), check_vma=False
    )
```

```python
import functools
import math

import jax
import jax.numpy as jnp
import ml_dtypes
import numpy as np
from jax import lax
from jax.experimental import pallas as pl
from jax.experimental.pallas import tpu as pltpu
from jax.sharding import PartitionSpec as P

A0 = 256
QUAD = 4
LANES = 128
FIRST = 16
TILE = 16


def as_real(matrix):
    top = np.concatenate([matrix.real, -matrix.imag], 1)
    low = np.concatenate([matrix.imag, matrix.real], 1)
    return np.concatenate([top, low], 0).astype(ml_dtypes.bfloat16)


def by_tile(matrix):
    shaped = matrix.reshape(2, -1, TILE, matrix.shape[1])
    return shaped.transpose(1, 0, 2, 3).reshape(matrix.shape)


def root(length, turns):
    return np.exp(-2j * np.pi / length * (turns % length))


def dft_tables(total):
    second = total // FIRST
    one = np.arange(FIRST)
    low = np.arange(TILE)
    k_one = one[:, None, None, None]
    l_row = low[None, :, None, None]
    n_one = one[None, None, :, None]
    l_col = low[None, None, None, :]
    same = l_row == l_col
    forward_one = root(FIRST, k_one * n_one) * root(total, l_row * k_one) * same
    forward_one = forward_one.reshape(FIRST * TILE, FIRST * TILE)
    two = np.arange(second)
    forward_two = root(second, two[:, None] * two[None, :])
    inverse_two = forward_two.conj()
    kept = np.arange(FIRST // QUAD)[:, None, None, None]
    inverse_one = (root(FIRST, kept * n_one) * root(total, l_col * n_one)).conj() * same
    inverse_one = inverse_one.reshape(FIRST // QUAD * TILE, FIRST * TILE)
    one, two, three, four = (
        as_real(t) for t in (forward_one, forward_two, inverse_two, inverse_one)
    )
    return [by_tile(one), by_tile(two), by_tile(by_tile(three).T).T, four]


def turn_table(total):
    chunks = total // FIRST // TILE
    value = root(total, TILE * np.arange(chunks)[:, None] * np.arange(FIRST)[None, :]).conj()
    return np.stack([value.real, value.imag]).astype(np.float32)


def steer_table(angle_count, pulse_count):
    angle_index = np.arange(angle_count)[:, None]
    pulse_index = np.arange(pulse_count)[None, :]
    value = root(angle_count, (angle_index + angle_count // 2) * pulse_index)
    value = (value / math.sqrt(pulse_count)).astype(np.complex64)
    return value.real.astype(ml_dtypes.bfloat16), value.imag.astype(ml_dtypes.bfloat16)


def steer_blocks(pulse_count, child_angles):
    real, imag = steer_table(A0, pulse_count)
    real, imag = real[:child_angles], imag[:child_angles]
    table = np.zeros((2, 2, child_angles, 2, 2, 2, 2, 2, pulse_count), ml_dtypes.bfloat16)
    for pair in range(2):
        for child in range(2):
            spot = (pair, child)
            table[child, 0, :, pair, 0, 0, *spot] = real
            table[child, 0, :, pair, 0, 1, *spot] = -imag
            table[child, 1, :, pair, 0, 0, *spot] = -imag
            table[child, 1, :, pair, 0, 1, *spot] = -real
            table[child, 0, :, pair, 1, 0, *spot] = imag
            table[child, 0, :, pair, 1, 1, *spot] = real
            table[child, 1, :, pair, 1, 0, *spot] = real
            table[child, 1, :, pair, 1, 1, *spot] = -imag
    return table.reshape(4 * child_angles, 32 * pulse_count)


def small_unit(angle):
    square = angle * angle
    cosine = 1.0 + square * (-1 / 2 + square * (1 / 24 + square * (-1 / 720 + square / 40320)))
    sine = angle * (1.0 + square * (-1 / 6 + square * (1 / 120 + square * (-1 / 5040))))
    return cosine, sine


def unit(angle):
    quarter = jnp.floor(angle * (2.0 / math.pi) + 0.5)
    rest = angle - quarter * 1.5703125
    rest = rest - quarter * (math.pi / 2 - 1.5703125)
    cosine, sine = small_unit(rest)
    turn = quarter.astype(jnp.int32)
    odd = (turn & 1) == 1
    first = jnp.where(odd, sine, cosine)
    second = jnp.where(odd, cosine, sine)
    first = jnp.where(((turn + 1) & 2) == 2, -first, first)
    second = jnp.where((turn & 2) == 2, -second, second)
    return first, second


def times(left, right):
    return (
        left[0] * right[0] - left[1] * right[1],
        left[0] * right[1] + left[1] * right[0],
    )


def cut_kernel(place_ref, raw_ref, *outs):
    for step, out in enumerate(outs):
        first = pl.multiple_of((place_ref[0] ^ step) * LANES, LANES)
        out[...] = raw_ref[:, :, pl.ds(first, LANES)]


def phase_kernel(total, place_ref, rate_ref, one_ref, two_ref, done_ref):
    done_ref[0] = 1
    start = (place_ref[1] * (total // QUAD)).astype(jnp.float32)
    size = (LANES, LANES)
    for level, ref in ((0, one_ref), (1, two_ref)):
        blocks, angles = ref.shape[1], ref.shape[2]
        rate = rate_ref[level]
        lane = lax.broadcasted_iota(jnp.int32, size, 1).astype(jnp.float32)
        factor = 1.0 + (lane + start) / total

        @pl.loop(0, angles // LANES)
        def _(part):
            row = lax.broadcasted_iota(jnp.int32, size, 0) + part * LANES
            slope = rate * ((row.astype(jnp.float32) + 0.5) / angles - 0.5)
            value = unit(slope * factor)
            step = unit(slope * (LANES / total))
            at = pl.ds(pl.multiple_of(part * LANES, LANES), LANES)
            for block in range(blocks):
                ref[0, block, at, :] = value[0].astype(jnp.bfloat16)
                ref[1, block, at, :] = value[1].astype(jnp.bfloat16)
                if block + 1 < blocks:
                    value = times(value, step)


def weight_kernel(pulse_count, weight_ref, steer_ref, one_ref, two_ref, done_ref):
    done_ref[0] = 1
    joined = jnp.concatenate([weight_ref[0, c, part] for c in range(2) for part in range(2)], 1)
    parents = joined.shape[0]
    width = one_ref.shape[2]
    lane = lax.broadcasted_iota(jnp.int32, (parents, width), 1)
    odd_pulse = lane % 2 == 1
    odd_child = lane // pulse_count % 2 == 1
    children = one_ref.shape[1] // 8
    for pair in range(2):
        for part in range(2):
            at = (pair * 2 + part) * width
            value = jnp.dot(
                joined, steer_ref[:, at : at + width], preferred_element_type=jnp.float32
            )
            for turn in range(2):
                turned = jnp.where(odd_pulse, -value, value) if turn else value
                kinds = (turned, jnp.where(odd_child, -turned, turned))
                for kind, rows in enumerate(kinds):
                    rows = rows.astype(jnp.bfloat16)
                    for first in range(0, parents, TILE):
                        block, tile = divmod(first, children)
                        row = (tile // TILE * 8 + pair * 4 + kind * 2 + part) * TILE
                        one_ref[turn * (parents // children) + block, row : row + TILE, :] = rows[
                            first : first + TILE
                        ]
    for child in range(2):
        for tile in range(parents // TILE):
            at = slice(tile * TILE, (tile + 1) * TILE)
            real, imag = weight_ref[1, child, 0, at], weight_ref[1, child, 1, at]
            row = 2 * tile * TILE
            two_ref[child, row : row + TILE] = jnp.concatenate([real, -imag], 1)
            two_ref[child, row + TILE : row + 2 * TILE] = jnp.concatenate([imag, real], 1)


def gain_kernel(total, place_ref, offset_ref, filter_ref, out_ref, done_ref):
    done_ref[0] = 1
    second = total // FIRST
    offsets = jnp.concatenate(
        [
            offset_ref[pl.ds(place_ref[1] ^ member, 1), :]
            for member in range(QUAD)
        ],
        1,
    )
    shift = offsets - place_ref[1] * (total // QUAD)
    scale = -2.0 * math.pi / total

    def ramp(rows, stride):
        k_index = stride * lax.broadcasted_iota(jnp.int32, (rows, LANES), 0)
        return unit(scale * ((k_index * shift) & (total - 1)).astype(jnp.float32))

    low, high = ramp(FIRST, 1), ramp(second, FIRST)
    for k_one in range(FIRST):
        row = (low[0][k_one : k_one + 1] * (1.0 / total), low[1][k_one : k_one + 1] * (1.0 / total))
        column = (filter_ref[0, :, k_one : k_one + 1], filter_ref[1, :, k_one : k_one + 1])
        value = times(times(high, row), column)
        out_ref[0, k_one] = value[0]
        out_ref[1, k_one] = value[1]


LOADED = 9


def kernel(count, total, place_ref, turn_ref, *rest):
    sources, rest = rest[:LOADED], rest[LOADED:]
    pieces, out_ref, rest = rest[:count], rest[count], rest[count + 1 :]
    held, rest = rest[:LOADED], rest[LOADED:]
    samples, partial_ref, folded, compressed, image, ready, load_sems, sems = rest
    fone_ref, gain_ref, ftwo_ref, itwo_ref, ione_ref = held[:5]
    rows_one_ref, phase_one_ref, rows_two_ref, phase_two_ref = held[5:]
    loads = [
        pltpu.make_async_copy(source, target, load_sems.at[number])
        for number, (source, target) in enumerate(zip(sources, held))
    ]
    for load in loads:
        load.start()

    span = total // count
    second = total // FIRST
    chunks = second // TILE
    kept = FIRST // QUAD
    half = FIRST * TILE
    f32, bf16 = jnp.float32, jnp.bfloat16

    def dot(left, right):
        return jnp.dot(left, right, preferred_element_type=f32)

    def turned(real, imag, chunk, k_one, sign):
        cosine, sine = turn_ref[0, chunk, k_one], turn_ref[1, chunk, k_one] * sign
        return (
            (cosine * real - sine * imag).astype(bf16),
            (cosine * imag + sine * real).astype(bf16),
        )

    index = place_ref[0] * QUAD + place_ref[1]
    tiles = span // TILE
    per_row = chunks // tiles
    for number, piece in enumerate(pieces):
        source = index ^ number
        first_tile = pl.multiple_of(source % per_row * tiles, tiles)
        samples[:, source // per_row, pl.ds(first_tile, tiles)] = piece[...].reshape(
            2, tiles, TILE, LANES
        )

    loads[0].wait()

    @pl.loop(0, chunks // 2, unroll=True)
    def _(pair):
        right = jnp.concatenate(
            [samples[:, :, 2 * pair + side].reshape(2 * half, LANES) for side in range(2)], 1
        )
        result = dot(fone_ref[...], right)
        for side in range(2):
            chunk = 2 * pair + side
            lanes = slice(side * LANES, (side + 1) * LANES)
            for k_one in range(FIRST):
                row = 2 * k_one * TILE
                real = result[row : row + TILE, lanes]
                imag = result[row + TILE : row + 2 * TILE, lanes]
                real, imag = turned(real, imag, chunk, k_one, -1.0)
                partial_ref[k_one, 0, chunk] = real
                partial_ref[k_one, 1, chunk] = imag

    for load in loads[1:4]:
        load.wait()

    @pl.loop(0, FIRST // 2, unroll=True)
    def _(pair):
        right = jnp.concatenate(
            [partial_ref[2 * pair + side].reshape(2 * second, LANES) for side in range(2)], 1
        )
        result = dot(ftwo_ref[...], right)
        scaled = []
        for side in range(2):
            k_one = 2 * pair + side
            lanes = slice(side * LANES, (side + 1) * LANES)
            parts = []
            for chunk in range(chunks):
                row = 2 * chunk * TILE
                at = slice(chunk * TILE, (chunk + 1) * TILE)
                real = result[row : row + TILE, lanes]
                imag = result[row + TILE : row + 2 * TILE, lanes]
                gain_real, gain_imag = gain_ref[0, k_one, at], gain_ref[1, k_one, at]
                parts.append((real * gain_real - imag * gain_imag).astype(bf16))
                parts.append((real * gain_imag + imag * gain_real).astype(bf16))
            scaled.append(jnp.concatenate(parts, 0))
        result = dot(itwo_ref[...], jnp.concatenate(scaled, 1))
        for side in range(2):
            k_one = 2 * pair + side
            lanes = slice(side * LANES, (side + 1) * LANES)
            for chunk in range(chunks):
                row = 2 * chunk * TILE
                real = result[row : row + TILE, lanes]
                imag = result[row + TILE : row + 2 * TILE, lanes]
                real, imag = turned(real, imag, chunk, k_one, 1.0)
                folded[chunk, 0, k_one] = real
                folded[chunk, 1, k_one] = imag

    for load in loads[4:]:
        load.wait()

    @pl.loop(0, chunks // 2, unroll=True)
    def _(pair):
        right = jnp.concatenate(
            [folded[2 * pair + side].reshape(2 * half, LANES) for side in range(2)], 1
        )
        result = dot(ione_ref[...], right).astype(bf16)
        for side in range(2):
            lanes = slice(side * LANES, (side + 1) * LANES)
            for part in range(2):
                for n_one in range(kept):
                    row = (part * kept + n_one) * TILE
                    compressed[n_one, 2 * pair + side, :, part * LANES : (part + 1) * LANES] = (
                        result[row : row + TILE, lanes]
                    )

    width = image.shape[4]
    blocks = width // LANES
    block_angles = image.shape[3]
    angle_blocks = image.shape[1]
    wide = rows_two_ref.shape[1] // 2
    steps = total // QUAD // width
    per_step = second // width

    def out_copy(step, slot):
        at = pl.ds(pl.multiple_of(step * width, width), width)
        return pltpu.make_async_copy(ready.at[slot], out_ref.at[:, :, at], sems.at[slot])

    @pl.loop(0, steps)
    def _(step):
        slot = step % 2
        tiles_wide = width // TILE
        first_tile = pl.multiple_of(step % per_step * tiles_wide, tiles_wide)
        columns = compressed[step // per_step, pl.ds(first_tile, tiles_wide)].reshape(
            width, 2 * LANES
        )

        def phases(ref, rows):
            return [
                jnp.concatenate(
                    [ref[part, step * blocks + b, rows, :] for b in range(blocks)], 1
                ).astype(f32)
                for part in range(2)
            ]

        for block in range(angle_blocks):
            result = lax.dot_general(
                rows_one_ref[block],
                columns,
                (((1,), (1,)), ((), ())),
                preferred_element_type=f32,
            )
            for tile in range(block_angles // TILE):
                at = slice(tile * TILE, (tile + 1) * TILE)
                cosine, sine = phases(
                    phase_one_ref, pl.ds(block * block_angles + tile * TILE, TILE)
                )
                for pick in range(2):
                    terms = [
                        result[row : row + TILE]
                        for row in [((tile * 2 + pick) * 4 + kind) * TILE for kind in range(4)]
                    ]
                    image[pick, block, 0, at] = (cosine * terms[0] + sine * terms[3]).astype(bf16)
                    image[pick, block, 1, at] = (cosine * terms[1] - sine * terms[2]).astype(bf16)

        @pl.when(step >= 2)
        def _():
            out_copy(step - 2, slot).wait()

        for block in range(angle_blocks):
            lower = dot(rows_two_ref[0], image[0, block].reshape(2 * block_angles, width))
            upper = dot(rows_two_ref[1], image[1, block].reshape(2 * block_angles, width))
            for tile in range(wide // TILE):
                rows = pl.ds(block * wide + tile * TILE, TILE)
                cosine, sine = phases(phase_two_ref, rows)
                real = slice(2 * tile * TILE, (2 * tile + 1) * TILE)
                imag = slice((2 * tile + 1) * TILE, (2 * tile + 2) * TILE)
                ready[slot, 0, rows, :] = cosine * (lower[real] + upper[real]) + sine * (
                    lower[imag] - upper[imag]
                )
                ready[slot, 1, rows, :] = cosine * (lower[imag] + upper[imag]) + sine * (
                    upper[real] - lower[real]
                )
        out_copy(step, slot).start()

    for step in range(max(steps - 2, 0), steps):
        out_copy(step, step % 2).wait()


def hold_kernel(*refs):
    pass


def hold(value, *flags):
    far = pl.BlockSpec(memory_space=pl.ANY)
    return pl.pallas_call(
        hold_kernel,
        out_shape=jax.ShapeDtypeStruct(value.shape, value.dtype),
        in_specs=[far] + [pl.BlockSpec(memory_space=pltpu.SMEM)] * len(flags),
        out_specs=far,
        input_output_aliases={0: 0},
        compiler_params=pltpu.CompilerParams(vmem_limit_bytes=1024 * 1024),
    )(value, *flags)


def focus(place, turns, tables, gain, rows_one, rows_two, phase_one, phase_two, pieces):
    count = len(pieces)
    total = phase_one.shape[1] * phase_one.shape[3] * QUAD
    second = total // FIRST
    chunks = second // TILE
    step_width = 256
    bf16, f32 = jnp.bfloat16, jnp.float32
    smem = pl.BlockSpec(memory_space=pltpu.SMEM)
    vmem = pl.BlockSpec(memory_space=pltpu.VMEM)
    parents, children = rows_two.shape[1] // 2, rows_two.shape[2] // 2
    angle_blocks = rows_one.shape[0]
    fone, ftwo, itwo, ione = tables
    sources = [fone, gain, ftwo, itwo, ione, rows_one, phase_one, rows_two, phase_two]
    far = pl.BlockSpec(memory_space=pl.ANY)
    return pl.pallas_call(
        functools.partial(kernel, count, total),
        out_shape=jax.ShapeDtypeStruct((2, angle_blocks * parents, total // QUAD), f32),
        in_specs=[smem, smem] + [far] * len(sources) + [vmem] * count,
        out_specs=far,
        scratch_shapes=[pltpu.VMEM(source.shape, source.dtype) for source in sources]
        + [
            pltpu.VMEM((2, FIRST, chunks, TILE, LANES), bf16),
            pltpu.VMEM((FIRST, 2, chunks, TILE, LANES), bf16),
            pltpu.VMEM((chunks, 2, FIRST, TILE, LANES), bf16),
            pltpu.VMEM((FIRST // QUAD, chunks, TILE, 2 * LANES), bf16),
            pltpu.VMEM((2, angle_blocks, 2, children, step_width), bf16),
            pltpu.VMEM((2, 2, angle_blocks * parents, step_width), f32),
            pltpu.SemaphoreType.DMA((LOADED,)),
            pltpu.SemaphoreType.DMA((2,)),
        ],
        compiler_params=pltpu.CompilerParams(vmem_limit_bytes=50 * 1024 * 1024),
    )(place, turns, *sources, *pieces)


def body(raw_echo, range_filter, range_offsets, interp_weight, phase_rate):
    count = lax.axis_size("ap")
    index = lax.axis_index("ap")
    total = range_filter.shape[1]
    pulse_count = range_offsets.shape[0]
    groups = count // QUAD
    width = total // QUAD
    second = total // FIRST
    f32, bf16 = jnp.float32, jnp.bfloat16
    smem = pl.BlockSpec(memory_space=pltpu.SMEM)
    vmem = pl.BlockSpec(memory_space=pltpu.VMEM)
    place = jnp.stack([index // QUAD, index % QUAD]).astype(jnp.int32)

    def move(value, bits):
        return lax.ppermute(value, "ap", [(i, i ^ bits) for i in range(count)])

    def shape(dims, kind=bf16):
        return jax.ShapeDtypeStruct(dims, kind)

    flag = shape((1,), jnp.int32)
    small = pltpu.CompilerParams(vmem_limit_bytes=2 * 1024 * 1024)

    def cost(flops, moved):
        return pl.CostEstimate(flops=flops, bytes_accessed=moved, transcendentals=0)

    cut = pl.pallas_call(
        cut_kernel,
        out_shape=[shape((2, total // count, LANES))] * groups,
        in_specs=[smem, vmem],
        out_specs=[vmem] * groups,
        compiler_params=small,
    )(place, raw_echo)
    offset_near = jnp.stack([range_offsets, move(range_offsets, 1)])
    offsets = jnp.concatenate([offset_near, move(offset_near, 2)])

    phase_one, phase_two, phase_done = pl.pallas_call(
        functools.partial(phase_kernel, total),
        out_shape=[
            shape((2, width // LANES, 2 * A0, LANES)),
            shape((2, width // LANES, 4 * A0, LANES)),
            flag,
        ],
        in_specs=[smem, smem],
        out_specs=[vmem, vmem, smem],
        cost_estimate=cost(2**30, 2**23),
        compiler_params=small,
    )(place, phase_rate)
    child_angles = interp_weight.shape[4]
    rows_one, rows_two, weight_done = pl.pallas_call(
        functools.partial(weight_kernel, pulse_count),
        out_shape=[
            shape((2 * A0 // child_angles, 8 * child_angles, 2 * LANES)),
            shape((2, 2 * interp_weight.shape[3], 2 * child_angles)),
            flag,
        ],
        in_specs=[vmem, vmem],
        out_specs=[vmem, vmem, smem],
        cost_estimate=cost(2**29, 2**22),
        compiler_params=small,
    )(interp_weight, jnp.asarray(steer_blocks(pulse_count, child_angles)))
    gain, gain_done = pl.pallas_call(
        functools.partial(gain_kernel, total),
        out_shape=[shape((2, FIRST, second, LANES), f32), flag],
        in_specs=[smem, vmem, vmem],
        out_specs=[vmem, smem],
        cost_estimate=cost(2**28, 2**22),
        compiler_params=small,
    )(place, offsets, range_filter.reshape(2, second, FIRST))

    tables = [jnp.asarray(t) for t in dft_tables(total)]
    turns = jnp.asarray(turn_table(total))

    own = [cut[0]] + [move(cut[step], QUAD * step) for step in range(1, groups)]
    own[1] = hold(own[1], phase_done, weight_done)
    if groups > 2:
        own[2] = hold(own[2], gain_done)
    across = [move(piece, 2) for piece in own]
    beside = [move(piece, 1) for piece in own]
    diagonal = [move(piece, 1) for piece in across]
    pieces = [part for four in zip(own, beside, across, diagonal) for part in four]
    return focus(place, turns, tables, gain, rows_one, rows_two, phase_one, phase_two, pieces)


def solution(mesh):
    placed = (P(None, "ap", "grp"), P(), P(("grp", "ap")), P(), P())
    return jax.shard_map(
        body, mesh=mesh, in_specs=placed, out_specs=P(None, None, ("grp", "ap")), check_vma=False
    )
```

```python
import functools
import math

import jax
import jax.numpy as jnp
import ml_dtypes
import numpy as np
from jax import lax
from jax.experimental import pallas as pl
from jax.experimental.pallas import tpu as pltpu
from jax.sharding import PartitionSpec as P

A0 = 256
QUAD = 4
LANES = 128
FIRST = 16
TILE = 16


def as_real(matrix):
    top = np.concatenate([matrix.real, -matrix.imag], 1)
    low = np.concatenate([matrix.imag, matrix.real], 1)
    return np.concatenate([top, low], 0).astype(ml_dtypes.bfloat16)


def by_tile(matrix):
    shaped = matrix.reshape(2, -1, TILE, matrix.shape[1])
    return shaped.transpose(1, 0, 2, 3).reshape(matrix.shape)


def root(length, turns):
    return np.exp(-2j * np.pi / length * (turns % length))


def dft_tables(total):
    second = total // FIRST
    one = np.arange(FIRST)
    low = np.arange(TILE)
    k_one = one[:, None, None, None]
    l_row = low[None, :, None, None]
    n_one = one[None, None, :, None]
    l_col = low[None, None, None, :]
    same = l_row == l_col
    forward_one = root(FIRST, k_one * n_one) * root(total, l_row * k_one) * same
    forward_one = forward_one.reshape(FIRST * TILE, FIRST * TILE)
    two = np.arange(second)
    forward_two = root(second, two[:, None] * two[None, :])
    inverse_two = forward_two.conj()
    kept = np.arange(FIRST // QUAD)[:, None, None, None]
    inverse_one = (root(FIRST, kept * n_one) * root(total, l_col * n_one)).conj() * same
    inverse_one = inverse_one.reshape(FIRST // QUAD * TILE, FIRST * TILE)
    one, two, three, four = (
        as_real(t) for t in (forward_one, forward_two, inverse_two, inverse_one)
    )
    return [by_tile(one), by_tile(two), by_tile(by_tile(three).T).T, four]


def turn_table(total):
    chunks = total // FIRST // TILE
    value = root(total, TILE * np.arange(chunks)[:, None] * np.arange(FIRST)[None, :]).conj()
    return np.stack([value.real, value.imag]).astype(np.float32)


def steer_table(angle_count, pulse_count):
    angle_index = np.arange(angle_count)[:, None]
    pulse_index = np.arange(pulse_count)[None, :]
    value = root(angle_count, (angle_index + angle_count // 2) * pulse_index)
    value = (value / math.sqrt(pulse_count)).astype(np.complex64)
    return value.real.astype(ml_dtypes.bfloat16), value.imag.astype(ml_dtypes.bfloat16)


def steer_blocks(pulse_count, child_angles):
    real, imag = steer_table(A0, pulse_count)
    real, imag = real[:child_angles], imag[:child_angles]
    table = np.zeros((2, 2, child_angles, 2, 2, 2, 2, 2, pulse_count), ml_dtypes.bfloat16)
    for pair in range(2):
        for child in range(2):
            spot = (pair, child)
            table[child, 0, :, pair, 0, 0, *spot] = real
            table[child, 0, :, pair, 0, 1, *spot] = -imag
            table[child, 1, :, pair, 0, 0, *spot] = -imag
            table[child, 1, :, pair, 0, 1, *spot] = -real
            table[child, 0, :, pair, 1, 0, *spot] = imag
            table[child, 0, :, pair, 1, 1, *spot] = real
            table[child, 1, :, pair, 1, 0, *spot] = real
            table[child, 1, :, pair, 1, 1, *spot] = -imag
    return table.reshape(4 * child_angles, 32 * pulse_count)


def small_unit(angle):
    square = angle * angle
    cosine = 1.0 + square * (-1 / 2 + square * (1 / 24 + square * (-1 / 720 + square / 40320)))
    sine = angle * (1.0 + square * (-1 / 6 + square * (1 / 120 + square * (-1 / 5040))))
    return cosine, sine


def unit(angle):
    quarter = jnp.floor(angle * (2.0 / math.pi) + 0.5)
    rest = angle - quarter * 1.5703125
    rest = rest - quarter * (math.pi / 2 - 1.5703125)
    cosine, sine = small_unit(rest)
    turn = quarter.astype(jnp.int32)
    odd = (turn & 1) == 1
    first = jnp.where(odd, sine, cosine)
    second = jnp.where(odd, cosine, sine)
    first = jnp.where(((turn + 1) & 2) == 2, -first, first)
    second = jnp.where((turn & 2) == 2, -second, second)
    return first, second


def times(left, right):
    return (
        left[0] * right[0] - left[1] * right[1],
        left[0] * right[1] + left[1] * right[0],
    )


def cut_kernel(place_ref, raw_ref, *outs):
    for step, out in enumerate(outs):
        first = pl.multiple_of((place_ref[0] ^ step) * LANES, LANES)
        out[...] = raw_ref[:, :, pl.ds(first, LANES)]


def phase_rows(ref, rate, start, total):
    size = (LANES, LANES)
    blocks, angles = ref.shape[1], ref.shape[2]
    lane = lax.broadcasted_iota(jnp.int32, size, 1).astype(jnp.float32)
    factor = 1.0 + (lane + start) / total

    @pl.loop(0, angles // LANES)
    def _(part):
        row = lax.broadcasted_iota(jnp.int32, size, 0) + part * LANES
        slope = rate * ((row.astype(jnp.float32) + 0.5) / angles - 0.5)
        value = unit(slope * factor)
        step = small_unit(slope * (LANES / total))
        at = pl.ds(pl.multiple_of(part * LANES, LANES), LANES)
        for block in range(blocks):
            ref[0, block, at, :] = value[0].astype(jnp.bfloat16)
            ref[1, block, at, :] = value[1].astype(jnp.bfloat16)
            if block + 1 < blocks:
                value = times(value, step)


def weight_rows(pulse_count, weight_ref, steer_ref, one_ref, two_ref):
    joined = jnp.concatenate([weight_ref[0, c, part] for c in range(2) for part in range(2)], 1)
    parents = joined.shape[0]
    width = one_ref.shape[2]
    lane = lax.broadcasted_iota(jnp.int32, (parents, width), 1)
    odd_pulse = lane % 2 == 1
    odd_child = lane // pulse_count % 2 == 1
    children = one_ref.shape[1] // 8
    for pair in range(2):
        for part in range(2):
            at = (pair * 2 + part) * width
            value = jnp.dot(
                joined, steer_ref[:, at : at + width], preferred_element_type=jnp.float32
            )
            for turn in range(2):
                turned = jnp.where(odd_pulse, -value, value) if turn else value
                kinds = (turned, jnp.where(odd_child, -turned, turned))
                for kind, rows in enumerate(kinds):
                    rows = rows.astype(jnp.bfloat16)
                    for first in range(0, parents, TILE):
                        block, tile = divmod(first, children)
                        row = (tile // TILE * 8 + pair * 4 + kind * 2 + part) * TILE
                        one_ref[turn * (parents // children) + block, row : row + TILE, :] = rows[
                            first : first + TILE
                        ]
    for child in range(2):
        for tile in range(parents // TILE):
            at = slice(tile * TILE, (tile + 1) * TILE)
            real, imag = weight_ref[1, child, 0, at], weight_ref[1, child, 1, at]
            row = 2 * tile * TILE
            two_ref[child, row : row + TILE] = jnp.concatenate([real, -imag], 1)
            two_ref[child, row + TILE : row + 2 * TILE] = jnp.concatenate([imag, real], 1)


def table_kernel(pulse_count, total, place_ref, rate_ref, near_ref, *refs):
    sources, targets, done_ref = refs[:2], refs[2:6], refs[6]
    inputs, held, sems = refs[7:9], refs[9:13], refs[13]
    loads = [
        pltpu.make_async_copy(source, ref, sems.at[spot])
        for spot, (source, ref) in enumerate(zip(sources, inputs))
    ]
    stores = [
        pltpu.make_async_copy(ref, target, sems.at[spot + 2])
        for spot, (ref, target) in enumerate(zip(held, targets))
    ]
    for load in loads:
        load.start()
    start = (place_ref[1] * (total // QUAD)).astype(jnp.float32)
    phase_rows(held[3], rate_ref[1], start, total)
    stores[3].start()
    phase_rows(held[2], rate_ref[0], start, total)
    stores[2].start()
    for load in loads:
        load.wait()
    weight_rows(pulse_count, *inputs, *held[:2])
    stores[0].start()
    stores[1].start()
    done_ref[0] = 1
    for store in stores:
        store.wait()


def gain_kernel(total, place_ref, offset_ref, filter_ref, out_ref, done_ref):
    done_ref[0] = 1
    second = total // FIRST
    offsets = jnp.concatenate(
        [
            offset_ref[pl.ds(place_ref[1] ^ member, 1), :]
            for member in range(QUAD)
        ],
        1,
    )
    shift = offsets - place_ref[1] * (total // QUAD)
    scale = -2.0 * math.pi / total

    def ramp(rows, stride):
        k_index = stride * lax.broadcasted_iota(jnp.int32, (rows, LANES), 0)
        return unit(scale * ((k_index * shift) & (total - 1)).astype(jnp.float32))

    low, high = ramp(FIRST, 1), ramp(second, FIRST)
    for k_one in range(FIRST):
        row = (low[0][k_one : k_one + 1] * (1.0 / total), low[1][k_one : k_one + 1] * (1.0 / total))
        column = (filter_ref[0, :, k_one : k_one + 1], filter_ref[1, :, k_one : k_one + 1])
        value = times(times(high, row), column)
        out_ref[0, k_one] = value[0].astype(jnp.bfloat16)
        out_ref[1, k_one] = value[1].astype(jnp.bfloat16)


def packs_of(packs):
    single = (len(packs) - 2) // 2
    return zip((0, 1, *[2] * single, *[3] * single), packs)


def kernel(count, total, place_ref, turn_ref, *rest):
    fone_ref, ftwo_ref, itwo_ref, ione_ref = rest[:4]
    sources, packs, out_ref, rest = rest[4:9], rest[9:-14], rest[-14], rest[-13:]
    held, rest = rest[:5], rest[5:]
    gain_ref, rows_one_ref, rows_two_ref, phase_one_ref, phase_two_ref = held
    samples, partial_ref, folded, compressed, image, ready, load_sems, sems = rest
    loads = [
        pltpu.make_async_copy(source, ref, load_sems.at[spot])
        for spot, (source, ref) in enumerate(zip(sources, held))
    ]
    for load in loads:
        load.start()

    span = total // count
    second = total // FIRST
    chunks = second // TILE
    kept = FIRST // QUAD
    half = FIRST * TILE
    f32, bf16 = jnp.float32, jnp.bfloat16

    def dot(left, right):
        return jnp.dot(left, right, preferred_element_type=f32)

    def turned(real, imag, chunk, k_one, sign):
        cosine, sine = turn_ref[0, chunk, k_one], turn_ref[1, chunk, k_one] * sign
        return (
            (cosine * real - sine * imag).astype(bf16),
            (cosine * imag + sine * real).astype(bf16),
        )

    index = place_ref[0] * QUAD + place_ref[1]
    tiles = span // TILE
    per_row = chunks // tiles
    number = [0] * QUAD
    for rel, pack in packs_of(packs):
        for spot in range(math.prod(pack.shape[:-3])):
            source = index ^ (QUAD * number[rel] + rel)
            number[rel] += 1
            first_tile = pl.multiple_of(source % per_row * tiles, tiles)
            samples[:, source // per_row, pl.ds(first_tile, tiles)] = (pack[spot] if len(pack.shape) == 4 else pack[...]).reshape(
                2, tiles, TILE, LANES
            )

    @pl.loop(0, chunks // 2, unroll=True)
    def _(pair):
        right = jnp.concatenate(
            [samples[:, :, 2 * pair + side].reshape(2 * half, LANES) for side in range(2)], 1
        )
        result = dot(fone_ref[...], right)
        for side in range(2):
            chunk = 2 * pair + side
            lanes = slice(side * LANES, (side + 1) * LANES)
            for k_one in range(FIRST):
                row = 2 * k_one * TILE
                real = result[row : row + TILE, lanes]
                imag = result[row + TILE : row + 2 * TILE, lanes]
                real, imag = turned(real, imag, chunk, k_one, -1.0)
                partial_ref[k_one, 0, chunk] = real
                partial_ref[k_one, 1, chunk] = imag

    loads[0].wait()

    @pl.loop(0, FIRST // 2, unroll=True)
    def _(pair):
        right = jnp.concatenate(
            [partial_ref[2 * pair + side].reshape(2 * second, LANES) for side in range(2)], 1
        )
        result = dot(ftwo_ref[...], right)
        scaled = []
        for side in range(2):
            k_one = 2 * pair + side
            lanes = slice(side * LANES, (side + 1) * LANES)
            parts = []
            for chunk in range(chunks):
                row = 2 * chunk * TILE
                at = slice(chunk * TILE, (chunk + 1) * TILE)
                real = result[row : row + TILE, lanes]
                imag = result[row + TILE : row + 2 * TILE, lanes]
                gain_real = gain_ref[0, k_one, at].astype(f32)
                gain_imag = gain_ref[1, k_one, at].astype(f32)
                parts.append((real * gain_real - imag * gain_imag).astype(bf16))
                parts.append((real * gain_imag + imag * gain_real).astype(bf16))
            scaled.append(jnp.concatenate(parts, 0))
        result = dot(itwo_ref[...], jnp.concatenate(scaled, 1))
        for side in range(2):
            k_one = 2 * pair + side
            lanes = slice(side * LANES, (side + 1) * LANES)
            for chunk in range(chunks):
                row = 2 * chunk * TILE
                real = result[row : row + TILE, lanes]
                imag = result[row + TILE : row + 2 * TILE, lanes]
                real, imag = turned(real, imag, chunk, k_one, 1.0)
                folded[chunk, 0, k_one] = real
                folded[chunk, 1, k_one] = imag

    for load in loads[1:]:
        load.wait()

    @pl.loop(0, chunks // 2, unroll=True)
    def _(pair):
        right = jnp.concatenate(
            [folded[2 * pair + side].reshape(2 * half, LANES) for side in range(2)], 1
        )
        result = dot(ione_ref[...], right).astype(bf16)
        for side in range(2):
            lanes = slice(side * LANES, (side + 1) * LANES)
            for part in range(2):
                for n_one in range(kept):
                    row = (part * kept + n_one) * TILE
                    compressed[n_one, 2 * pair + side, :, part * LANES : (part + 1) * LANES] = (
                        result[row : row + TILE, lanes]
                    )

    width = image.shape[4]
    blocks = width // LANES
    block_angles = image.shape[3]
    angle_blocks = image.shape[1]
    wide = rows_two_ref.shape[1] // 2
    steps = total // QUAD // width
    per_step = second // width

    def out_copy(step, slot):
        at = pl.ds(pl.multiple_of(step * width, width), width)
        return pltpu.make_async_copy(ready.at[slot], out_ref.at[:, :, at], sems.at[slot])

    @pl.loop(0, steps)
    def _(step):
        slot = step % 2
        tiles_wide = width // TILE
        first_tile = pl.multiple_of(step % per_step * tiles_wide, tiles_wide)
        columns = compressed[step // per_step, pl.ds(first_tile, tiles_wide)].reshape(
            width, 2 * LANES
        )

        def phases(ref, rows):
            return [
                jnp.concatenate(
                    [ref[part, step * blocks + b, rows, :] for b in range(blocks)], 1
                ).astype(f32)
                for part in range(2)
            ]

        for block in range(angle_blocks):
            result = lax.dot_general(
                rows_one_ref[block],
                columns,
                (((1,), (1,)), ((), ())),
                preferred_element_type=f32,
            )
            for tile in range(block_angles // TILE):
                at = slice(tile * TILE, (tile + 1) * TILE)
                cosine, sine = phases(
                    phase_one_ref, pl.ds(block * block_angles + tile * TILE, TILE)
                )
                for pick in range(2):
                    terms = [
                        result[row : row + TILE]
                        for row in [((tile * 2 + pick) * 4 + kind) * TILE for kind in range(4)]
                    ]
                    image[pick, block, 0, at] = (cosine * terms[0] + sine * terms[3]).astype(bf16)
                    image[pick, block, 1, at] = (cosine * terms[1] - sine * terms[2]).astype(bf16)

        @pl.when(step >= 2)
        def _():
            out_copy(step - 2, slot).wait()

        for block in range(angle_blocks):
            lower = dot(rows_two_ref[0], image[0, block].reshape(2 * block_angles, width))
            upper = dot(rows_two_ref[1], image[1, block].reshape(2 * block_angles, width))
            for tile in range(wide // TILE):
                rows = pl.ds(block * wide + tile * TILE, TILE)
                cosine, sine = phases(phase_two_ref, rows)
                real = slice(2 * tile * TILE, (2 * tile + 1) * TILE)
                imag = slice((2 * tile + 1) * TILE, (2 * tile + 2) * TILE)
                ready[slot, 0, rows, :] = cosine * (lower[real] + upper[real]) + sine * (
                    lower[imag] - upper[imag]
                )
                ready[slot, 1, rows, :] = cosine * (lower[imag] + upper[imag]) + sine * (
                    upper[real] - lower[real]
                )
        out_copy(step, slot).start()

    for step in range(max(steps - 2, 0), steps):
        out_copy(step, step % 2).wait()


def hold_kernel(*refs):
    pass


def hold(value, *flags):
    far = pl.BlockSpec(memory_space=pl.ANY)
    return pl.pallas_call(
        hold_kernel,
        out_shape=jax.ShapeDtypeStruct(value.shape, value.dtype),
        in_specs=[far] + [pl.BlockSpec(memory_space=pltpu.SMEM)] * len(flags),
        out_specs=far,
        input_output_aliases={0: 0},
        cost_estimate=pl.CostEstimate(flops=1, bytes_accessed=1, transcendentals=0),
        compiler_params=pltpu.CompilerParams(vmem_limit_bytes=1024 * 1024),
    )(value, *flags)


def pack_kernel(*refs):
    for spot in range(refs[-1].shape[0]):
        refs[-1][spot] = refs[spot][...]


def pack(pieces, *flags):
    vmem = pl.BlockSpec(memory_space=pltpu.VMEM)
    return pl.pallas_call(
        pack_kernel,
        out_shape=jax.ShapeDtypeStruct((len(pieces), *pieces[0].shape), pieces[0].dtype),
        in_specs=[vmem] * len(pieces) + [pl.BlockSpec(memory_space=pltpu.SMEM)] * len(flags),
        out_specs=vmem,
        cost_estimate=pl.CostEstimate(flops=1, bytes_accessed=1, transcendentals=0),
        compiler_params=pltpu.CompilerParams(vmem_limit_bytes=1024 * 1024),
    )(*pieces, *flags)


def focus(place, turns, tables, made, packs):
    _, rows_one, rows_two, phase_one, _ = made
    count = QUAD * packs[0].shape[0]
    total = phase_one.shape[1] * phase_one.shape[3] * QUAD
    second = total // FIRST
    chunks = second // TILE
    step_width = 256
    bf16, f32 = jnp.bfloat16, jnp.float32
    smem = pl.BlockSpec(memory_space=pltpu.SMEM)
    vmem = pl.BlockSpec(memory_space=pltpu.VMEM)
    far = pl.BlockSpec(memory_space=pltpu.HBM)
    parents, children = rows_two.shape[1] // 2, rows_two.shape[2] // 2
    angle_blocks = rows_one.shape[0]
    return pl.pallas_call(
        functools.partial(kernel, count, total),
        out_shape=jax.ShapeDtypeStruct((2, angle_blocks * parents, total // QUAD), f32),
        in_specs=[smem, smem] + [vmem] * 4 + [far] * len(made) + [vmem] * len(packs),
        out_specs=far,
        scratch_shapes=[pltpu.VMEM(array.shape, bf16) for array in made]
        + [
            pltpu.VMEM((2, FIRST, chunks, TILE, LANES), bf16),
            pltpu.VMEM((FIRST, 2, chunks, TILE, LANES), bf16),
            pltpu.VMEM((chunks, 2, FIRST, TILE, LANES), bf16),
            pltpu.VMEM((FIRST // QUAD, chunks, TILE, 2 * LANES), bf16),
            pltpu.VMEM((2, angle_blocks, 2, children, step_width), bf16),
            pltpu.VMEM((2, 2, angle_blocks * parents, step_width), f32),
            pltpu.SemaphoreType.DMA((5,)),
            pltpu.SemaphoreType.DMA((2,)),
        ],
        compiler_params=pltpu.CompilerParams(vmem_limit_bytes=50 * 1024 * 1024),
    )(place, turns, *tables, *made, *packs)


def body(raw_echo, range_filter, range_offsets, interp_weight, phase_rate):
    count = lax.axis_size("ap")
    index = lax.axis_index("ap")
    total = range_filter.shape[1]
    pulse_count = range_offsets.shape[0]
    groups = count // QUAD
    width = total // QUAD
    second = total // FIRST
    f32, bf16 = jnp.float32, jnp.bfloat16
    smem = pl.BlockSpec(memory_space=pltpu.SMEM)
    vmem = pl.BlockSpec(memory_space=pltpu.VMEM)
    place = jnp.stack([index // QUAD, index % QUAD]).astype(jnp.int32)

    def move(value, bits):
        return lax.ppermute(value, "ap", [(i, i ^ bits) for i in range(count)])

    def shape(dims, kind=bf16):
        return jax.ShapeDtypeStruct(dims, kind)

    flag = shape((1,), jnp.int32)
    small = pltpu.CompilerParams(vmem_limit_bytes=2 * 1024 * 1024)

    def cost(flops, moved):
        return pl.CostEstimate(flops=flops, bytes_accessed=moved, transcendentals=0)

    cut = pl.pallas_call(
        cut_kernel,
        out_shape=[shape((2, total // count, LANES))] * groups,
        in_specs=[smem, vmem],
        out_specs=[vmem] * groups,
        compiler_params=small,
    )(place, raw_echo)
    offset_near = jnp.stack([range_offsets, move(range_offsets, 1)])
    offsets = jnp.concatenate([offset_near, move(offset_near, 2)])

    far = pl.BlockSpec(memory_space=pltpu.HBM)
    child_angles = interp_weight.shape[4]
    steer = jnp.asarray(steer_blocks(pulse_count, child_angles))
    made_shapes = [
        (2 * A0 // child_angles, 8 * child_angles, 2 * LANES),
        (2, 2 * interp_weight.shape[3], 2 * child_angles),
        (2, width // LANES, 2 * A0, LANES),
        (2, width // LANES, 4 * A0, LANES),
    ]
    *made, made_flag = pl.pallas_call(
        functools.partial(table_kernel, pulse_count, total),
        out_shape=[shape(dims) for dims in made_shapes] + [flag],
        in_specs=[smem, smem, vmem, far, far],
        out_specs=[far] * 4 + [smem],
        scratch_shapes=[
            pltpu.VMEM(dims, bf16) for dims in [interp_weight.shape, steer.shape, *made_shapes]
        ]
        + [pltpu.SemaphoreType.DMA((6,))],
        cost_estimate=cost(2**30, 2**23),
        compiler_params=pltpu.CompilerParams(vmem_limit_bytes=52 * 1024 * 1024),
    )(place, phase_rate, offset_near, interp_weight, steer)

    own = [cut[0]] + [move(cut[step], QUAD * step) for step in range(1, groups)]
    own[1] = hold(own[1], made_flag, offsets)
    gain, gain_flag = pl.pallas_call(
        functools.partial(gain_kernel, total),
        out_shape=[shape((2, FIRST, second, LANES)), flag],
        in_specs=[smem, vmem, vmem],
        out_specs=[vmem, smem],
        cost_estimate=cost(2**28, 2**22),
        compiler_params=small,
    )(place, offsets, range_filter.reshape(2, second, FIRST))
    if groups > 2:
        own[2] = hold(own[2], gain_flag)
    across = [move(piece, 2) for piece in own]
    mine = pack(own)
    beside = move(mine, 1)
    packs = [mine, beside, *across, *[move(piece, 1) for piece in across]]
    tables = [jnp.asarray(t) for t in dft_tables(total)]
    return focus(place, jnp.asarray(turn_table(total)), tables, [gain, *made], packs)


def solution(mesh):
    placed = (P(None, "ap", "grp"), P(), P(("grp", "ap")), P(), P())
    return jax.shard_map(
        body, mesh=mesh, in_specs=placed, out_specs=P(None, None, ("grp", "ap")), check_vma=False
    )
```

```python
import functools
import math

import jax
import jax.numpy as jnp
import ml_dtypes
import numpy as np
from jax import lax
from jax.experimental import pallas as pl
from jax.experimental.pallas import tpu as pltpu
from jax.sharding import PartitionSpec as P

A0 = 256
QUAD = 4
LANES = 128
FIRST = 16
TILE = 16


def as_real(matrix):
    top = np.concatenate([matrix.real, -matrix.imag], 1)
    low = np.concatenate([matrix.imag, matrix.real], 1)
    return np.concatenate([top, low], 0).astype(ml_dtypes.bfloat16)


def by_tile(matrix):
    shaped = matrix.reshape(2, -1, TILE, matrix.shape[1])
    return shaped.transpose(1, 0, 2, 3).reshape(matrix.shape)


def root(length, turns):
    return np.exp(-2j * np.pi / length * (turns % length))


def dft_tables(total):
    second = total // FIRST
    one = np.arange(FIRST)
    low = np.arange(TILE)
    k_one = one[:, None, None, None]
    l_row = low[None, :, None, None]
    n_one = one[None, None, :, None]
    l_col = low[None, None, None, :]
    same = l_row == l_col
    forward_one = root(FIRST, k_one * n_one) * root(total, l_row * k_one) * same
    forward_one = forward_one.reshape(FIRST * TILE, FIRST * TILE)
    two = np.arange(second)
    forward_two = root(second, two[:, None] * two[None, :])
    inverse_two = forward_two.conj()
    kept = np.arange(FIRST // QUAD)[:, None, None, None]
    inverse_one = (root(FIRST, kept * n_one) * root(total, l_col * n_one)).conj() * same
    inverse_one = inverse_one.reshape(FIRST // QUAD * TILE, FIRST * TILE)
    one, two, three, four = (
        as_real(t) for t in (forward_one, forward_two, inverse_two, inverse_one)
    )
    return [by_tile(one), by_tile(two), by_tile(by_tile(three).T).T, four]


def turn_table(total):
    chunks = total // FIRST // TILE
    value = root(total, TILE * np.arange(chunks)[:, None] * np.arange(FIRST)[None, :]).conj()
    return np.stack([value.real, value.imag]).astype(np.float32)


def steer_table(angle_count, pulse_count):
    angle_index = np.arange(angle_count)[:, None]
    pulse_index = np.arange(pulse_count)[None, :]
    value = root(angle_count, (angle_index + angle_count // 2) * pulse_index)
    value = (value / math.sqrt(pulse_count)).astype(np.complex64)
    return value.real.astype(ml_dtypes.bfloat16), value.imag.astype(ml_dtypes.bfloat16)


def steer_blocks(pulse_count, child_angles):
    real, imag = steer_table(A0, pulse_count)
    real, imag = real[:child_angles], imag[:child_angles]
    table = np.zeros((2, 2, child_angles, 2, 2, 2, 2, 2, pulse_count), ml_dtypes.bfloat16)
    for pair in range(2):
        for child in range(2):
            spot = (pair, child)
            table[child, 0, :, pair, 0, 0, *spot] = real
            table[child, 0, :, pair, 0, 1, *spot] = -imag
            table[child, 1, :, pair, 0, 0, *spot] = -imag
            table[child, 1, :, pair, 0, 1, *spot] = -real
            table[child, 0, :, pair, 1, 0, *spot] = imag
            table[child, 0, :, pair, 1, 1, *spot] = real
            table[child, 1, :, pair, 1, 0, *spot] = real
            table[child, 1, :, pair, 1, 1, *spot] = -imag
    return table.reshape(4 * child_angles, 32 * pulse_count)


def small_unit(angle):
    square = angle * angle
    cosine = 1.0 + square * (-1 / 2 + square * (1 / 24 + square * (-1 / 720 + square / 40320)))
    sine = angle * (1.0 + square * (-1 / 6 + square * (1 / 120 + square * (-1 / 5040))))
    return cosine, sine


def unit(angle):
    quarter = jnp.floor(angle * (2.0 / math.pi) + 0.5)
    rest = angle - quarter * 1.5703125
    rest = rest - quarter * (math.pi / 2 - 1.5703125)
    cosine, sine = small_unit(rest)
    turn = quarter.astype(jnp.int32)
    odd = (turn & 1) == 1
    first = jnp.where(odd, sine, cosine)
    second = jnp.where(odd, cosine, sine)
    first = jnp.where(((turn + 1) & 2) == 2, -first, first)
    second = jnp.where((turn & 2) == 2, -second, second)
    return first, second


def times(left, right):
    return (
        left[0] * right[0] - left[1] * right[1],
        left[0] * right[1] + left[1] * right[0],
    )


def cut_kernel(place_ref, raw_ref, *outs):
    for step, out in enumerate(outs):
        first = pl.multiple_of((place_ref[0] ^ step) * LANES, LANES)
        out[...] = raw_ref[:, :, pl.ds(first, LANES)]


def phase_rows(ref, rate, start, total):
    size = (LANES, LANES)
    blocks, angles = ref.shape[1], ref.shape[2]
    lane = lax.broadcasted_iota(jnp.int32, size, 1).astype(jnp.float32)
    factor = 1.0 + (lane + start) / total

    @pl.loop(0, angles // LANES)
    def _(part):
        row = lax.broadcasted_iota(jnp.int32, size, 0) + part * LANES
        slope = rate * ((row.astype(jnp.float32) + 0.5) / angles - 0.5)
        value = unit(slope * factor)
        step = small_unit(slope * (LANES / total))
        at = pl.ds(pl.multiple_of(part * LANES, LANES), LANES)
        for block in range(blocks):
            ref[0, block, at, :] = value[0].astype(jnp.bfloat16)
            ref[1, block, at, :] = value[1].astype(jnp.bfloat16)
            if block + 1 < blocks:
                value = times(value, step)


def weight_rows(pulse_count, weight_ref, steer_ref, one_ref, two_ref):
    joined = jnp.concatenate([weight_ref[0, c, part] for c in range(2) for part in range(2)], 1)
    parents = joined.shape[0]
    width = one_ref.shape[2]
    lane = lax.broadcasted_iota(jnp.int32, (parents, width), 1)
    odd_pulse = lane % 2 == 1
    odd_child = lane // pulse_count % 2 == 1
    children = one_ref.shape[1] // 8
    for pair in range(2):
        for part in range(2):
            at = (pair * 2 + part) * width
            value = jnp.dot(
                joined, steer_ref[:, at : at + width], preferred_element_type=jnp.float32
            )
            for turn in range(2):
                turned = jnp.where(odd_pulse, -value, value) if turn else value
                kinds = (turned, jnp.where(odd_child, -turned, turned))
                for kind, rows in enumerate(kinds):
                    rows = rows.astype(jnp.bfloat16)
                    for first in range(0, parents, TILE):
                        block, tile = divmod(first, children)
                        row = (tile // TILE * 8 + pair * 4 + kind * 2 + part) * TILE
                        one_ref[turn * (parents // children) + block, row : row + TILE, :] = rows[
                            first : first + TILE
                        ]
    for child in range(2):
        for tile in range(parents // TILE):
            at = slice(tile * TILE, (tile + 1) * TILE)
            real, imag = weight_ref[1, child, 0, at], weight_ref[1, child, 1, at]
            row = 2 * tile * TILE
            two_ref[child, row : row + TILE] = jnp.concatenate([real, -imag], 1)
            two_ref[child, row + TILE : row + 2 * TILE] = jnp.concatenate([imag, real], 1)


def table_kernel(pulse_count, total, place_ref, rate_ref, near_ref, *refs):
    sources, targets, done_ref = refs[:2], refs[2:6], refs[6]
    inputs, held, sems = refs[7:9], refs[9:13], refs[13]
    loads = [
        pltpu.make_async_copy(source, ref, sems.at[spot])
        for spot, (source, ref) in enumerate(zip(sources, inputs))
    ]
    stores = [
        pltpu.make_async_copy(ref, target, sems.at[spot + 2])
        for spot, (ref, target) in enumerate(zip(held, targets))
    ]
    for load in loads:
        load.start()
    start = (place_ref[1] * (total // QUAD)).astype(jnp.float32)
    phase_rows(held[3], rate_ref[1], start, total)
    stores[3].start()
    phase_rows(held[2], rate_ref[0], start, total)
    stores[2].start()
    for load in loads:
        load.wait()
    weight_rows(pulse_count, *inputs, *held[:2])
    stores[0].start()
    stores[1].start()
    done_ref[0] = 1
    for store in stores:
        store.wait()


def gain_kernel(total, place_ref, offset_ref, filter_ref, out_ref):
    second = total // FIRST
    offsets = jnp.concatenate(
        [
            offset_ref[pl.ds(place_ref[1] ^ member, 1), :]
            for member in range(QUAD)
        ],
        1,
    )
    shift = offsets - place_ref[1] * (total // QUAD)
    scale = -2.0 * math.pi / total

    def ramp(rows, stride):
        k_index = stride * lax.broadcasted_iota(jnp.int32, (rows, LANES), 0)
        return unit(scale * ((k_index * shift) & (total - 1)).astype(jnp.float32))

    low, high = ramp(FIRST, 1), ramp(second, FIRST)
    for k_one in range(FIRST):
        row = (low[0][k_one : k_one + 1] * (1.0 / total), low[1][k_one : k_one + 1] * (1.0 / total))
        column = (filter_ref[0, :, k_one : k_one + 1], filter_ref[1, :, k_one : k_one + 1])
        value = times(times(high, row), column)
        out_ref[0, k_one] = value[0].astype(jnp.bfloat16)
        out_ref[1, k_one] = value[1].astype(jnp.bfloat16)


def kernel(count, total, place_ref, turn_ref, *rest):
    fone_ref, ftwo_ref, itwo_ref, ione_ref, gain_ref = rest[:5]
    sources, pieces, out_ref, rest = rest[5:9], rest[9:-13], rest[-13], rest[-12:]
    held, rest = rest[:4], rest[4:]
    rows_one_ref, rows_two_ref, phase_one_ref, phase_two_ref = held
    samples, partial_ref, folded, compressed, image, ready, load_sems, sems = rest
    loads = [
        pltpu.make_async_copy(source, ref, load_sems.at[spot])
        for spot, (source, ref) in enumerate(zip(sources, held))
    ]
    for load in loads:
        load.start()

    span = total // count
    second = total // FIRST
    chunks = second // TILE
    kept = FIRST // QUAD
    half = FIRST * TILE
    f32, bf16 = jnp.float32, jnp.bfloat16

    def dot(left, right):
        return jnp.dot(left, right, preferred_element_type=f32)

    def turned(real, imag, chunk, k_one, sign):
        cosine, sine = turn_ref[0, chunk, k_one], turn_ref[1, chunk, k_one] * sign
        return (
            (cosine * real - sine * imag).astype(bf16),
            (cosine * imag + sine * real).astype(bf16),
        )

    index = place_ref[0] * QUAD + place_ref[1]
    tiles = span // TILE
    per_row = chunks // tiles
    for number, piece in enumerate(pieces):
        source = index ^ number
        first_tile = pl.multiple_of(source % per_row * tiles, tiles)
        samples[:, source // per_row, pl.ds(first_tile, tiles)] = piece[...].reshape(
            2, tiles, TILE, LANES
        )

    @pl.loop(0, chunks // 2, unroll=True)
    def _(pair):
        right = jnp.concatenate(
            [samples[:, :, 2 * pair + side].reshape(2 * half, LANES) for side in range(2)], 1
        )
        result = dot(fone_ref[...], right)
        for side in range(2):
            chunk = 2 * pair + side
            lanes = slice(side * LANES, (side + 1) * LANES)
            for k_one in range(FIRST):
                row = 2 * k_one * TILE
                real = result[row : row + TILE, lanes]
                imag = result[row + TILE : row + 2 * TILE, lanes]
                real, imag = turned(real, imag, chunk, k_one, -1.0)
                partial_ref[k_one, 0, chunk] = real
                partial_ref[k_one, 1, chunk] = imag

    @pl.loop(0, FIRST // 2, unroll=True)
    def _(pair):
        right = jnp.concatenate(
            [partial_ref[2 * pair + side].reshape(2 * second, LANES) for side in range(2)], 1
        )
        result = dot(ftwo_ref[...], right)
        scaled = []
        for side in range(2):
            k_one = 2 * pair + side
            lanes = slice(side * LANES, (side + 1) * LANES)
            parts = []
            for chunk in range(chunks):
                row = 2 * chunk * TILE
                at = slice(chunk * TILE, (chunk + 1) * TILE)
                real = result[row : row + TILE, lanes]
                imag = result[row + TILE : row + 2 * TILE, lanes]
                gain_real = gain_ref[0, k_one, at].astype(f32)
                gain_imag = gain_ref[1, k_one, at].astype(f32)
                parts.append((real * gain_real - imag * gain_imag).astype(bf16))
                parts.append((real * gain_imag + imag * gain_real).astype(bf16))
            scaled.append(jnp.concatenate(parts, 0))
        result = dot(itwo_ref[...], jnp.concatenate(scaled, 1))
        for side in range(2):
            k_one = 2 * pair + side
            lanes = slice(side * LANES, (side + 1) * LANES)
            for chunk in range(chunks):
                row = 2 * chunk * TILE
                real = result[row : row + TILE, lanes]
                imag = result[row + TILE : row + 2 * TILE, lanes]
                real, imag = turned(real, imag, chunk, k_one, 1.0)
                folded[chunk, 0, k_one] = real
                folded[chunk, 1, k_one] = imag

    for load in loads:
        load.wait()

    @pl.loop(0, chunks // 2, unroll=True)
    def _(pair):
        right = jnp.concatenate(
            [folded[2 * pair + side].reshape(2 * half, LANES) for side in range(2)], 1
        )
        result = dot(ione_ref[...], right).astype(bf16)
        for side in range(2):
            lanes = slice(side * LANES, (side + 1) * LANES)
            for part in range(2):
                for n_one in range(kept):
                    row = (part * kept + n_one) * TILE
                    compressed[n_one, 2 * pair + side, :, part * LANES : (part + 1) * LANES] = (
                        result[row : row + TILE, lanes]
                    )

    width = image.shape[4]
    blocks = width // LANES
    block_angles = image.shape[3]
    angle_blocks = image.shape[1]
    wide = rows_two_ref.shape[1] // 2
    steps = total // QUAD // width
    per_step = second // width

    def out_copy(step, slot):
        at = pl.ds(pl.multiple_of(step * width, width), width)
        return pltpu.make_async_copy(ready.at[slot], out_ref.at[:, :, at], sems.at[slot])

    @pl.loop(0, steps)
    def _(step):
        slot = step % 2
        tiles_wide = width // TILE
        first_tile = pl.multiple_of(step % per_step * tiles_wide, tiles_wide)
        columns = compressed[step // per_step, pl.ds(first_tile, tiles_wide)].reshape(
            width, 2 * LANES
        )

        def phases(ref, rows):
            return [
                jnp.concatenate(
                    [ref[part, step * blocks + b, rows, :] for b in range(blocks)], 1
                ).astype(f32)
                for part in range(2)
            ]

        for block in range(angle_blocks):
            result = lax.dot_general(
                rows_one_ref[block],
                columns,
                (((1,), (1,)), ((), ())),
                preferred_element_type=f32,
            )
            for tile in range(block_angles // TILE):
                at = slice(tile * TILE, (tile + 1) * TILE)
                cosine, sine = phases(
                    phase_one_ref, pl.ds(block * block_angles + tile * TILE, TILE)
                )
                for pick in range(2):
                    terms = [
                        result[row : row + TILE]
                        for row in [((tile * 2 + pick) * 4 + kind) * TILE for kind in range(4)]
                    ]
                    image[pick, block, 0, at] = (cosine * terms[0] + sine * terms[3]).astype(bf16)
                    image[pick, block, 1, at] = (cosine * terms[1] - sine * terms[2]).astype(bf16)

        @pl.when(step >= 2)
        def _():
            out_copy(step - 2, slot).wait()

        for block in range(angle_blocks):
            lower = dot(rows_two_ref[0], image[0, block].reshape(2 * block_angles, width))
            upper = dot(rows_two_ref[1], image[1, block].reshape(2 * block_angles, width))
            for tile in range(wide // TILE):
                rows = pl.ds(block * wide + tile * TILE, TILE)
                cosine, sine = phases(phase_two_ref, rows)
                real = slice(2 * tile * TILE, (2 * tile + 1) * TILE)
                imag = slice((2 * tile + 1) * TILE, (2 * tile + 2) * TILE)
                ready[slot, 0, rows, :] = cosine * (lower[real] + upper[real]) + sine * (
                    lower[imag] - upper[imag]
                )
                ready[slot, 1, rows, :] = cosine * (lower[imag] + upper[imag]) + sine * (
                    upper[real] - lower[real]
                )
        out_copy(step, slot).start()

    for step in range(max(steps - 2, 0), steps):
        out_copy(step, step % 2).wait()


def hold_kernel(*refs):
    pass


def hold(value, flag, after=None):
    far = pl.BlockSpec(memory_space=pl.ANY)
    others = [] if after is None else [after]
    return pl.pallas_call(
        hold_kernel,
        out_shape=jax.ShapeDtypeStruct(value.shape, value.dtype),
        in_specs=[far, pl.BlockSpec(memory_space=pltpu.SMEM)] + [far] * len(others),
        out_specs=far,
        input_output_aliases={0: 0},
        cost_estimate=pl.CostEstimate(flops=1, bytes_accessed=1, transcendentals=0),
        compiler_params=pltpu.CompilerParams(vmem_limit_bytes=1024 * 1024),
    )(value, flag, *others)


def focus(place, turns, tables, gain, made, pieces):
    rows_one, rows_two, phase_one, _ = made
    count = len(pieces)
    total = phase_one.shape[1] * phase_one.shape[3] * QUAD
    second = total // FIRST
    chunks = second // TILE
    step_width = 256
    bf16, f32 = jnp.bfloat16, jnp.float32
    smem = pl.BlockSpec(memory_space=pltpu.SMEM)
    vmem = pl.BlockSpec(memory_space=pltpu.VMEM)
    far = pl.BlockSpec(memory_space=pltpu.HBM)
    parents, children = rows_two.shape[1] // 2, rows_two.shape[2] // 2
    angle_blocks = rows_one.shape[0]
    return pl.pallas_call(
        functools.partial(kernel, count, total),
        out_shape=jax.ShapeDtypeStruct((2, angle_blocks * parents, total // QUAD), f32),
        in_specs=[smem, smem] + [vmem] * 5 + [far] * len(made) + [vmem] * len(pieces),
        out_specs=far,
        scratch_shapes=[pltpu.VMEM(array.shape, bf16) for array in made]
        + [
            pltpu.VMEM((2, FIRST, chunks, TILE, LANES), bf16),
            pltpu.VMEM((FIRST, 2, chunks, TILE, LANES), bf16),
            pltpu.VMEM((chunks, 2, FIRST, TILE, LANES), bf16),
            pltpu.VMEM((FIRST // QUAD, chunks, TILE, 2 * LANES), bf16),
            pltpu.VMEM((2, angle_blocks, 2, children, step_width), bf16),
            pltpu.VMEM((2, 2, angle_blocks * parents, step_width), f32),
            pltpu.SemaphoreType.DMA((4,)),
            pltpu.SemaphoreType.DMA((2,)),
        ],
        compiler_params=pltpu.CompilerParams(vmem_limit_bytes=46 * 1024 * 1024),
    )(place, turns, *tables, gain, *made, *pieces)


def body(raw_echo, range_filter, range_offsets, interp_weight, phase_rate):
    count = lax.axis_size("ap")
    index = lax.axis_index("ap")
    total = range_filter.shape[1]
    pulse_count = range_offsets.shape[0]
    groups = count // QUAD
    width = total // QUAD
    second = total // FIRST
    f32, bf16 = jnp.float32, jnp.bfloat16
    smem = pl.BlockSpec(memory_space=pltpu.SMEM)
    vmem = pl.BlockSpec(memory_space=pltpu.VMEM)
    place = jnp.stack([index // QUAD, index % QUAD]).astype(jnp.int32)

    def move(value, bits):
        return lax.ppermute(value, "ap", [(i, i ^ bits) for i in range(count)])

    def shape(dims, kind=bf16):
        return jax.ShapeDtypeStruct(dims, kind)

    flag = shape((1,), jnp.int32)
    small = pltpu.CompilerParams(vmem_limit_bytes=2 * 1024 * 1024)

    def cost(flops, moved):
        return pl.CostEstimate(flops=flops, bytes_accessed=moved, transcendentals=0)

    cut = pl.pallas_call(
        cut_kernel,
        out_shape=[shape((2, total // count, LANES))] * groups,
        in_specs=[smem, vmem],
        out_specs=[vmem] * groups,
        compiler_params=small,
    )(place, raw_echo)
    offset_near = jnp.stack([range_offsets, move(range_offsets, 1)])
    offsets = jnp.concatenate([offset_near, move(offset_near, 2)])

    far = pl.BlockSpec(memory_space=pltpu.HBM)
    child_angles = interp_weight.shape[4]
    steer = jnp.asarray(steer_blocks(pulse_count, child_angles))
    made_shapes = [
        (2 * A0 // child_angles, 8 * child_angles, 2 * LANES),
        (2, 2 * interp_weight.shape[3], 2 * child_angles),
        (2, width // LANES, 2 * A0, LANES),
        (2, width // LANES, 4 * A0, LANES),
    ]
    *made, made_flag = pl.pallas_call(
        functools.partial(table_kernel, pulse_count, total),
        out_shape=[shape(dims) for dims in made_shapes] + [flag],
        in_specs=[smem, smem, vmem, far, far],
        out_specs=[far] * 4 + [smem],
        scratch_shapes=[
            pltpu.VMEM(dims, bf16) for dims in [interp_weight.shape, steer.shape, *made_shapes]
        ]
        + [pltpu.SemaphoreType.DMA((6,))],
        cost_estimate=cost(2**30, 2**23),
        compiler_params=pltpu.CompilerParams(vmem_limit_bytes=52 * 1024 * 1024),
    )(place, phase_rate, offset_near, interp_weight, steer)

    own = [cut[0]] + [move(cut[step], QUAD * step) for step in range(1, groups)]
    across = [move(own[0], 2), move(own[1], 2)]
    if groups > 2:
        own[2] = hold(own[2], made_flag, after=across[1])
    else:
        made[0] = hold(made[0], made_flag)
    across += [move(piece, 2) for piece in own[2:]]
    beside = [move(piece, 1) for piece in own]
    diagonal = [move(piece, 1) for piece in across]
    gain = pl.pallas_call(
        functools.partial(gain_kernel, total),
        out_shape=shape((2, FIRST, second, LANES)),
        in_specs=[smem, vmem, vmem],
        out_specs=vmem,
        cost_estimate=cost(2**28, 2**22),
        compiler_params=small,
    )(place, offsets, range_filter.reshape(2, second, FIRST))
    pieces = [part for four in zip(own, beside, across, diagonal) for part in four]
    tables = [jnp.asarray(t) for t in dft_tables(total)]
    return focus(place, jnp.asarray(turn_table(total)), tables, gain, made, pieces)


def solution(mesh):
    placed = (P(None, "ap", "grp"), P(), P(("grp", "ap")), P(), P())
    return jax.shard_map(
        body, mesh=mesh, in_specs=placed, out_specs=P(None, None, ("grp", "ap")), check_vma=False
    )
```

```python
import functools
import math

import jax
import jax.numpy as jnp
import ml_dtypes
import numpy as np
from jax import lax
from jax.experimental import pallas as pl
from jax.experimental.pallas import tpu as pltpu
from jax.sharding import PartitionSpec as P

A0 = 256
QUAD = 4
LANES = 128
FIRST = 16
TILE = 16


def as_real(matrix):
    top = np.concatenate([matrix.real, -matrix.imag], 1)
    low = np.concatenate([matrix.imag, matrix.real], 1)
    return np.concatenate([top, low], 0).astype(ml_dtypes.bfloat16)


def by_tile(matrix):
    shaped = matrix.reshape(2, -1, TILE, matrix.shape[1])
    return shaped.transpose(1, 0, 2, 3).reshape(matrix.shape)


def root(length, turns):
    return np.exp(-2j * np.pi / length * (turns % length))


def dft_tables(total):
    second = total // FIRST
    one = np.arange(FIRST)
    low = np.arange(TILE)
    k_one = one[:, None, None, None]
    l_row = low[None, :, None, None]
    n_one = one[None, None, :, None]
    l_col = low[None, None, None, :]
    same = l_row == l_col
    forward_one = root(FIRST, k_one * n_one) * root(total, l_row * k_one) * same
    forward_one = forward_one.reshape(FIRST * TILE, FIRST * TILE)
    two = np.arange(second)
    forward_two = root(second, two[:, None] * two[None, :])
    inverse_two = forward_two.conj()
    kept = np.arange(FIRST // QUAD)[:, None, None, None]
    inverse_one = (root(FIRST, kept * n_one) * root(total, l_col * n_one)).conj() * same
    inverse_one = inverse_one.reshape(FIRST // QUAD * TILE, FIRST * TILE)
    one, two, three, four = (
        as_real(t) for t in (forward_one, forward_two, inverse_two, inverse_one)
    )
    return [by_tile(one), by_tile(two), by_tile(by_tile(three).T).T, four]


def turn_table(total):
    chunks = total // FIRST // TILE
    value = root(total, TILE * np.arange(chunks)[:, None] * np.arange(FIRST)[None, :]).conj()
    return np.stack([value.real, value.imag]).astype(np.float32)


def steer_table(angle_count, pulse_count):
    angle_index = np.arange(angle_count)[:, None]
    pulse_index = np.arange(pulse_count)[None, :]
    value = root(angle_count, (angle_index + angle_count // 2) * pulse_index)
    value = (value / math.sqrt(pulse_count)).astype(np.complex64)
    return value.real.astype(ml_dtypes.bfloat16), value.imag.astype(ml_dtypes.bfloat16)


def steer_blocks(pulse_count, child_angles):
    real, imag = steer_table(A0, pulse_count)
    real, imag = real[:child_angles], imag[:child_angles]
    table = np.zeros((2, 2, child_angles, 2, 2, 2, 2, 2, pulse_count), ml_dtypes.bfloat16)
    for pair in range(2):
        for child in range(2):
            spot = (pair, child)
            table[child, 0, :, pair, 0, 0, *spot] = real
            table[child, 0, :, pair, 0, 1, *spot] = -imag
            table[child, 1, :, pair, 0, 0, *spot] = -imag
            table[child, 1, :, pair, 0, 1, *spot] = -real
            table[child, 0, :, pair, 1, 0, *spot] = imag
            table[child, 0, :, pair, 1, 1, *spot] = real
            table[child, 1, :, pair, 1, 0, *spot] = real
            table[child, 1, :, pair, 1, 1, *spot] = -imag
    return table.reshape(4 * child_angles, 32 * pulse_count)


def small_unit(angle):
    square = angle * angle
    cosine = 1.0 + square * (-1 / 2 + square * (1 / 24 + square * (-1 / 720 + square / 40320)))
    sine = angle * (1.0 + square * (-1 / 6 + square * (1 / 120 + square * (-1 / 5040))))
    return cosine, sine


def unit(angle):
    quarter = jnp.floor(angle * (2.0 / math.pi) + 0.5)
    rest = angle - quarter * 1.5703125
    rest = rest - quarter * (math.pi / 2 - 1.5703125)
    cosine, sine = small_unit(rest)
    turn = quarter.astype(jnp.int32)
    odd = (turn & 1) == 1
    first = jnp.where(odd, sine, cosine)
    second = jnp.where(odd, cosine, sine)
    first = jnp.where(((turn + 1) & 2) == 2, -first, first)
    second = jnp.where((turn & 2) == 2, -second, second)
    return first, second


def times(left, right):
    return (
        left[0] * right[0] - left[1] * right[1],
        left[0] * right[1] + left[1] * right[0],
    )


def cut_kernel(place_ref, raw_ref, *outs):
    for step, out in enumerate(outs):
        first = pl.multiple_of((place_ref[0] ^ step) * LANES, LANES)
        out[...] = raw_ref[:, :, pl.ds(first, LANES)]


def phase_rows(ref, rate, start, total):
    size = (LANES, LANES)
    blocks, angles = ref.shape[1], ref.shape[2]
    lane = lax.broadcasted_iota(jnp.int32, size, 1).astype(jnp.float32)
    factor = 1.0 + (lane + start) / total

    @pl.loop(0, angles // LANES)
    def _(part):
        row = lax.broadcasted_iota(jnp.int32, size, 0) + part * LANES
        slope = rate * ((row.astype(jnp.float32) + 0.5) / angles - 0.5)
        value = unit(slope * factor)
        step = small_unit(slope * (LANES / total))
        at = pl.ds(pl.multiple_of(part * LANES, LANES), LANES)
        for block in range(blocks):
            ref[0, block, at, :] = value[0].astype(jnp.bfloat16)
            ref[1, block, at, :] = value[1].astype(jnp.bfloat16)
            if block + 1 < blocks:
                value = times(value, step)


def weight_rows(pulse_count, weight_ref, steer_ref, one_ref, two_ref):
    joined = jnp.concatenate([weight_ref[0, c, part] for c in range(2) for part in range(2)], 1)
    parents = joined.shape[0]
    width = one_ref.shape[2]
    lane = lax.broadcasted_iota(jnp.int32, (parents, width), 1)
    odd_pulse = lane % 2 == 1
    odd_child = lane // pulse_count % 2 == 1
    children = one_ref.shape[1] // 8
    for pair in range(2):
        for part in range(2):
            at = (pair * 2 + part) * width
            value = jnp.dot(
                joined, steer_ref[:, at : at + width], preferred_element_type=jnp.float32
            )
            for turn in range(2):
                turned = jnp.where(odd_pulse, -value, value) if turn else value
                kinds = (turned, jnp.where(odd_child, -turned, turned))
                for kind, rows in enumerate(kinds):
                    rows = rows.astype(jnp.bfloat16)
                    for first in range(0, parents, TILE):
                        block, tile = divmod(first, children)
                        row = (tile // TILE * 8 + pair * 4 + kind * 2 + part) * TILE
                        one_ref[turn * (parents // children) + block, row : row + TILE, :] = rows[
                            first : first + TILE
                        ]
    for child in range(2):
        for tile in range(parents // TILE):
            at = slice(tile * TILE, (tile + 1) * TILE)
            real, imag = weight_ref[1, child, 0, at], weight_ref[1, child, 1, at]
            row = 2 * tile * TILE
            two_ref[child, row : row + TILE] = jnp.concatenate([real, -imag], 1)
            two_ref[child, row + TILE : row + 2 * TILE] = jnp.concatenate([imag, real], 1)


def store_all(held, targets, sems):
    return [
        pltpu.make_async_copy(ref, target, sems.at[spot])
        for spot, (ref, target) in enumerate(zip(held, targets))
    ]


def phase_kernel(total, place_ref, rate_ref, *refs):
    targets, done_ref, held, sems = refs[:2], refs[2], refs[3:5], refs[5]
    stores = store_all(held, targets, sems)
    start = (place_ref[1] * (total // QUAD)).astype(jnp.float32)
    for level in (1, 0):
        phase_rows(held[level], rate_ref[level], start, total)
        stores[level].start()
    done_ref[0] = 1
    for store in stores:
        store.wait()


def weight_kernel(pulse_count, total, place_ref, *refs):
    offset_refs, filter_ref, sources = refs[:QUAD], refs[QUAD], refs[QUAD + 1 : QUAD + 3]
    targets, done_ref = refs[QUAD + 4 : QUAD + 7], refs[QUAD + 7]
    inputs, held, sems = refs[QUAD + 8 : QUAD + 10], refs[QUAD + 10 : QUAD + 13], refs[QUAD + 13]
    stores = store_all(held, targets, sems)
    loads = [
        pltpu.make_async_copy(source, ref, sems.at[spot + 3])
        for spot, (source, ref) in enumerate(zip(sources, inputs))
    ]
    for load in loads:
        load.start()
    gain_rows(total, place_ref, offset_refs, filter_ref, held[0])
    stores[0].start()
    for load in loads:
        load.wait()
    weight_rows(pulse_count, *inputs, *held[1:])
    stores[1].start()
    stores[2].start()
    done_ref[0] = 1
    for store in stores:
        store.wait()


def gain_rows(total, place_ref, offset_refs, filter_ref, out_ref):
    second = total // FIRST
    member = place_ref[1]
    offsets = []
    for owner in range(QUAD):
        value = offset_refs[0][...]
        for rel in range(1, QUAD):
            value = jnp.where((member ^ rel) == owner, offset_refs[rel][...], value)
        offsets.append(value)
    offsets = jnp.concatenate(offsets, 1)
    shift = offsets - place_ref[1] * (total // QUAD)
    scale = -2.0 * math.pi / total

    def ramp(rows, stride):
        k_index = stride * lax.broadcasted_iota(jnp.int32, (rows, LANES), 0)
        return unit(scale * ((k_index * shift) & (total - 1)).astype(jnp.float32))

    low, high = ramp(FIRST, 1), ramp(second, FIRST)
    for k_one in range(FIRST):
        row = (low[0][k_one : k_one + 1] * (1.0 / total), low[1][k_one : k_one + 1] * (1.0 / total))
        column = (filter_ref[0, :, k_one : k_one + 1], filter_ref[1, :, k_one : k_one + 1])
        value = times(times(high, row), column)
        out_ref[0, k_one] = value[0].astype(jnp.bfloat16)
        out_ref[1, k_one] = value[1].astype(jnp.bfloat16)


def kernel(count, total, place_ref, turn_ref, *rest):
    fone_ref, ftwo_ref, itwo_ref, ione_ref = rest[:4]
    sources, pieces, out_ref, rest = rest[4:9], rest[9:-15], rest[-15], rest[-14:]
    held, rest = rest[:5], rest[5:]
    gain_ref, rows_one_ref, rows_two_ref, phase_one_ref, phase_two_ref = held
    samples, partial_ref, folded, compressed, image, ready, load_sems, piece_sem, sems = rest
    loads = [
        pltpu.make_async_copy(source, ref, load_sems.at[spot])
        for spot, (source, ref) in enumerate(zip(sources, held))
    ]
    span = total // count
    second = total // FIRST
    chunks = second // TILE
    kept = FIRST // QUAD
    half = FIRST * TILE
    f32, bf16 = jnp.float32, jnp.bfloat16

    def dot(left, right):
        return jnp.dot(left, right, preferred_element_type=f32)

    def turned(real, imag, chunk, k_one, sign):
        cosine, sine = turn_ref[0, chunk, k_one], turn_ref[1, chunk, k_one] * sign
        return (
            (cosine * real - sine * imag).astype(bf16),
            (cosine * imag + sine * real).astype(bf16),
        )

    index = place_ref[0] * QUAD + place_ref[1]
    per_row = second // span
    arrivals = []
    for number, piece in enumerate(pieces):
        source = index ^ number
        rows = pl.ds(pl.multiple_of(source % per_row * span, TILE), span)
        arrivals.append(
            pltpu.make_async_copy(piece, samples.at[:, source // per_row, rows], piece_sem)
        )
    for copy in arrivals + loads:
        copy.start()
    for copy in arrivals:
        copy.wait()

    @pl.loop(0, chunks // 2, unroll=True)
    def _(pair):
        right = jnp.concatenate(
            [
                samples[:, :, pl.ds((2 * pair + side) * TILE, TILE)].reshape(2 * half, LANES)
                for side in range(2)
            ],
            1,
        )
        result = dot(fone_ref[...], right)
        for side in range(2):
            chunk = 2 * pair + side
            lanes = slice(side * LANES, (side + 1) * LANES)
            for k_one in range(FIRST):
                row = 2 * k_one * TILE
                real = result[row : row + TILE, lanes]
                imag = result[row + TILE : row + 2 * TILE, lanes]
                real, imag = turned(real, imag, chunk, k_one, -1.0)
                partial_ref[k_one, 0, chunk] = real
                partial_ref[k_one, 1, chunk] = imag

    loads[0].wait()

    @pl.loop(0, FIRST // 2, unroll=True)
    def _(pair):
        right = jnp.concatenate(
            [partial_ref[2 * pair + side].reshape(2 * second, LANES) for side in range(2)], 1
        )
        result = dot(ftwo_ref[...], right)
        scaled = []
        for side in range(2):
            k_one = 2 * pair + side
            lanes = slice(side * LANES, (side + 1) * LANES)
            parts = []
            for chunk in range(chunks):
                row = 2 * chunk * TILE
                at = slice(chunk * TILE, (chunk + 1) * TILE)
                real = result[row : row + TILE, lanes]
                imag = result[row + TILE : row + 2 * TILE, lanes]
                gain_real = gain_ref[0, k_one, at].astype(f32)
                gain_imag = gain_ref[1, k_one, at].astype(f32)
                parts.append((real * gain_real - imag * gain_imag).astype(bf16))
                parts.append((real * gain_imag + imag * gain_real).astype(bf16))
            scaled.append(jnp.concatenate(parts, 0))
        result = dot(itwo_ref[...], jnp.concatenate(scaled, 1))
        for side in range(2):
            k_one = 2 * pair + side
            lanes = slice(side * LANES, (side + 1) * LANES)
            for chunk in range(chunks):
                row = 2 * chunk * TILE
                real = result[row : row + TILE, lanes]
                imag = result[row + TILE : row + 2 * TILE, lanes]
                real, imag = turned(real, imag, chunk, k_one, 1.0)
                folded[chunk, 0, k_one] = real
                folded[chunk, 1, k_one] = imag

    for load in loads[1:]:
        load.wait()

    @pl.loop(0, chunks // 2, unroll=True)
    def _(pair):
        right = jnp.concatenate(
            [folded[2 * pair + side].reshape(2 * half, LANES) for side in range(2)], 1
        )
        result = dot(ione_ref[...], right).astype(bf16)
        for side in range(2):
            lanes = slice(side * LANES, (side + 1) * LANES)
            for part in range(2):
                for n_one in range(kept):
                    row = (part * kept + n_one) * TILE
                    compressed[n_one, 2 * pair + side, :, part * LANES : (part + 1) * LANES] = (
                        result[row : row + TILE, lanes]
                    )

    width = image.shape[4]
    blocks = width // LANES
    block_angles = image.shape[3]
    angle_blocks = image.shape[1]
    wide = rows_two_ref.shape[1] // 2
    steps = total // QUAD // width
    per_step = second // width

    def out_copy(step, slot):
        at = pl.ds(pl.multiple_of(step * width, width), width)
        return pltpu.make_async_copy(ready.at[slot], out_ref.at[:, :, at], sems.at[slot])

    @pl.loop(0, steps)
    def _(step):
        slot = step % 2
        tiles_wide = width // TILE
        first_tile = pl.multiple_of(step % per_step * tiles_wide, tiles_wide)
        columns = compressed[step // per_step, pl.ds(first_tile, tiles_wide)].reshape(
            width, 2 * LANES
        )

        def phases(ref, rows):
            return [
                jnp.concatenate(
                    [ref[part, step * blocks + b, rows, :] for b in range(blocks)], 1
                ).astype(f32)
                for part in range(2)
            ]

        for block in range(angle_blocks):
            result = lax.dot_general(
                rows_one_ref[block],
                columns,
                (((1,), (1,)), ((), ())),
                preferred_element_type=f32,
            )
            for tile in range(block_angles // TILE):
                at = slice(tile * TILE, (tile + 1) * TILE)
                cosine, sine = phases(
                    phase_one_ref, pl.ds(block * block_angles + tile * TILE, TILE)
                )
                for pick in range(2):
                    terms = [
                        result[row : row + TILE]
                        for row in [((tile * 2 + pick) * 4 + kind) * TILE for kind in range(4)]
                    ]
                    image[pick, block, 0, at] = (cosine * terms[0] + sine * terms[3]).astype(bf16)
                    image[pick, block, 1, at] = (cosine * terms[1] - sine * terms[2]).astype(bf16)

        @pl.when(step >= 2)
        def _():
            out_copy(step - 2, slot).wait()

        for block in range(angle_blocks):
            lower = dot(rows_two_ref[0], image[0, block].reshape(2 * block_angles, width))
            upper = dot(rows_two_ref[1], image[1, block].reshape(2 * block_angles, width))
            for tile in range(wide // TILE):
                rows = pl.ds(block * wide + tile * TILE, TILE)
                cosine, sine = phases(phase_two_ref, rows)
                real = slice(2 * tile * TILE, (2 * tile + 1) * TILE)
                imag = slice((2 * tile + 1) * TILE, (2 * tile + 2) * TILE)
                ready[slot, 0, rows, :] = cosine * (lower[real] + upper[real]) + sine * (
                    lower[imag] - upper[imag]
                )
                ready[slot, 1, rows, :] = cosine * (lower[imag] + upper[imag]) + sine * (
                    upper[real] - lower[real]
                )
        out_copy(step, slot).start()

    for step in range(max(steps - 2, 0), steps):
        out_copy(step, step % 2).wait()


def hold_kernel(*refs):
    pass


def hold(value, flag, after=None):
    far = pl.BlockSpec(memory_space=pl.ANY)
    others = [] if after is None else [after]
    return pl.pallas_call(
        hold_kernel,
        out_shape=jax.ShapeDtypeStruct(value.shape, value.dtype),
        in_specs=[far, pl.BlockSpec(memory_space=pltpu.SMEM)] + [far] * len(others),
        out_specs=far,
        input_output_aliases={0: 0},
        cost_estimate=pl.CostEstimate(flops=1, bytes_accessed=1, transcendentals=0),
        compiler_params=pltpu.CompilerParams(vmem_limit_bytes=1024 * 1024),
    )(value, flag, *others)


def focus(place, turns, tables, made, pieces):
    _, rows_one, rows_two, phase_one, _ = made
    count = len(pieces)
    total = phase_one.shape[1] * phase_one.shape[3] * QUAD
    second = total // FIRST
    chunks = second // TILE
    step_width = 256
    bf16, f32 = jnp.bfloat16, jnp.float32
    smem = pl.BlockSpec(memory_space=pltpu.SMEM)
    vmem = pl.BlockSpec(memory_space=pltpu.VMEM)
    far = pl.BlockSpec(memory_space=pltpu.HBM)
    parents, children = rows_two.shape[1] // 2, rows_two.shape[2] // 2
    angle_blocks = rows_one.shape[0]
    return pl.pallas_call(
        functools.partial(kernel, count, total),
        out_shape=jax.ShapeDtypeStruct((2, angle_blocks * parents, total // QUAD), f32),
        in_specs=[smem, smem] + [vmem] * 4 + [far] * (len(made) + count),
        out_specs=far,
        scratch_shapes=[pltpu.VMEM(array.shape, bf16) for array in made]
        + [
            pltpu.VMEM((2, FIRST, second, LANES), bf16),
            pltpu.VMEM((FIRST, 2, chunks, TILE, LANES), bf16),
            pltpu.VMEM((chunks, 2, FIRST, TILE, LANES), bf16),
            pltpu.VMEM((FIRST // QUAD, chunks, TILE, 2 * LANES), bf16),
            pltpu.VMEM((2, angle_blocks, 2, children, step_width), bf16),
            pltpu.VMEM((2, 2, angle_blocks * parents, step_width), f32),
            pltpu.SemaphoreType.DMA((5,)),
            pltpu.SemaphoreType.DMA,
            pltpu.SemaphoreType.DMA((2,)),
        ],
        compiler_params=pltpu.CompilerParams(vmem_limit_bytes=46 * 1024 * 1024),
    )(place, turns, *tables, *made, *pieces)


def body(raw_echo, range_filter, range_offsets, interp_weight, phase_rate):
    count = lax.axis_size("ap")
    index = lax.axis_index("ap")
    total = range_filter.shape[1]
    pulse_count = range_offsets.shape[0]
    groups = count // QUAD
    width = total // QUAD
    second = total // FIRST
    f32, bf16 = jnp.float32, jnp.bfloat16
    smem = pl.BlockSpec(memory_space=pltpu.SMEM)
    vmem = pl.BlockSpec(memory_space=pltpu.VMEM)
    place = jnp.stack([index // QUAD, index % QUAD]).astype(jnp.int32)

    def move(value, bits):
        return lax.ppermute(value, "ap", [(i, i ^ bits) for i in range(count)])

    def shape(dims, kind=bf16):
        return jax.ShapeDtypeStruct(dims, kind)

    flag = shape((1,), jnp.int32)
    large = pltpu.CompilerParams(vmem_limit_bytes=52 * 1024 * 1024)
    small = pltpu.CompilerParams(vmem_limit_bytes=2 * 1024 * 1024)

    def cost(flops, moved):
        return pl.CostEstimate(flops=flops, bytes_accessed=moved, transcendentals=0)

    cut = pl.pallas_call(
        cut_kernel,
        out_shape=[shape((2, total // count, LANES))] * groups,
        in_specs=[smem, vmem],
        out_specs=[vmem] * groups,
        compiler_params=small,
    )(place, raw_echo)
    offsets = range_offsets.reshape(1, pulse_count)
    offsets = [offsets] + [move(offsets, rel) for rel in range(1, QUAD)]

    far = pl.BlockSpec(memory_space=pl.ANY)
    child_angles = interp_weight.shape[4]
    steer = jnp.asarray(steer_blocks(pulse_count, child_angles))
    phase_shapes = [
        (2, width // LANES, 2 * A0, LANES),
        (2, width // LANES, 4 * A0, LANES),
    ]
    *phases, phase_flag = pl.pallas_call(
        functools.partial(phase_kernel, total),
        out_shape=[shape(dims) for dims in phase_shapes] + [flag],
        in_specs=[smem, smem],
        out_specs=[far] * 2 + [smem],
        scratch_shapes=[pltpu.VMEM(dims, bf16) for dims in phase_shapes]
        + [pltpu.SemaphoreType.DMA((2,))],
        cost_estimate=cost(2**30, 2**23),
        compiler_params=large,
    )(place, phase_rate)

    own = [cut[0]] + [move(cut[step], QUAD * step) for step in range(1, groups)]
    across = [move(own[0], 2), move(own[1], 2)]
    if groups > 2:
        own[2] = hold(own[2], phase_flag, after=across[1])
    weight_shapes = [
        (2, FIRST, second, LANES),
        (2 * A0 // child_angles, 8 * child_angles, 2 * LANES),
        (2, 2 * interp_weight.shape[3], 2 * child_angles),
    ]
    *weights, weight_flag = pl.pallas_call(
        functools.partial(weight_kernel, pulse_count, total),
        out_shape=[shape(dims) for dims in weight_shapes] + [flag],
        in_specs=[smem] + [vmem] * (QUAD + 1) + [far] * 3,
        out_specs=[far] * 3 + [smem],
        scratch_shapes=[
            pltpu.VMEM(dims, bf16) for dims in [interp_weight.shape, steer.shape, *weight_shapes]
        ]
        + [pltpu.SemaphoreType.DMA((5,))],
        cost_estimate=cost(2**30, 2**22),
        compiler_params=large,
    )(
        place,
        *offsets,
        range_filter.reshape(2, second, FIRST),
        interp_weight,
        steer,
        own[min(2, groups - 1)],
    )
    if groups > 3:
        own[3] = hold(own[3], weight_flag)
    across += [move(piece, 2) for piece in own[2:]]
    beside = [move(piece, 1) for piece in own]
    diagonal = [move(piece, 1) for piece in across]
    pieces = [part for four in zip(own, beside, across, diagonal) for part in four]
    tables = [jnp.asarray(t) for t in dft_tables(total)]
    return focus(place, jnp.asarray(turn_table(total)), tables, [*weights, *phases], pieces)


def solution(mesh):
    placed = (P(None, "ap", "grp"), P(), P(("grp", "ap")), P(), P())
    return jax.shard_map(
        body, mesh=mesh, in_specs=placed, out_specs=P(None, None, ("grp", "ap")), check_vma=False
    )
```

```python
import functools
import math

import jax
import jax.numpy as jnp
import ml_dtypes
import numpy as np
from jax import lax
from jax.experimental import pallas as pl
from jax.experimental.pallas import tpu as pltpu
from jax.sharding import PartitionSpec as P

A0 = 256
QUAD = 4
LANES = 128
FIRST = 16
TILE = 16


def as_real(matrix):
    top = np.concatenate([matrix.real, -matrix.imag], 1)
    low = np.concatenate([matrix.imag, matrix.real], 1)
    return np.concatenate([top, low], 0).astype(ml_dtypes.bfloat16)


def by_tile(matrix):
    shaped = matrix.reshape(2, -1, TILE, matrix.shape[1])
    return shaped.transpose(1, 0, 2, 3).reshape(matrix.shape)


def root(length, turns):
    return np.exp(-2j * np.pi / length * (turns % length))


def dft_tables(total):
    second = total // FIRST
    one = np.arange(FIRST)
    low = np.arange(TILE)
    k_one = one[:, None, None, None]
    l_row = low[None, :, None, None]
    n_one = one[None, None, :, None]
    l_col = low[None, None, None, :]
    same = l_row == l_col
    forward_one = root(FIRST, k_one * n_one) * root(total, l_row * k_one) * same
    forward_one = forward_one.reshape(FIRST * TILE, FIRST * TILE)
    two = np.arange(second)
    forward_two = root(second, two[:, None] * two[None, :])
    inverse_two = forward_two.conj()
    kept = np.arange(FIRST // QUAD)[:, None, None, None]
    inverse_one = (root(FIRST, kept * n_one) * root(total, l_col * n_one)).conj() * same
    inverse_one = inverse_one.reshape(FIRST // QUAD * TILE, FIRST * TILE)
    one, two, three, four = (
        as_real(t) for t in (forward_one, forward_two, inverse_two, inverse_one)
    )
    return [by_tile(one), by_tile(two), by_tile(by_tile(three).T).T, four]


def turn_table(total):
    chunks = total // FIRST // TILE
    value = root(total, TILE * np.arange(chunks)[:, None] * np.arange(FIRST)[None, :]).conj()
    return np.stack([value.real, value.imag]).astype(np.float32)


def steer_table(angle_count, pulse_count):
    angle_index = np.arange(angle_count)[:, None]
    pulse_index = np.arange(pulse_count)[None, :]
    value = root(angle_count, (angle_index + angle_count // 2) * pulse_index)
    value = (value / math.sqrt(pulse_count)).astype(np.complex64)
    return value.real.astype(ml_dtypes.bfloat16), value.imag.astype(ml_dtypes.bfloat16)


def steer_blocks(pulse_count, child_angles):
    real, imag = steer_table(A0, pulse_count)
    real, imag = real[:child_angles], imag[:child_angles]
    table = np.zeros((2, 2, child_angles, 2, 2, 2, 2, 2, pulse_count), ml_dtypes.bfloat16)
    for pair in range(2):
        for child in range(2):
            spot = (pair, child)
            table[child, 0, :, pair, 0, 0, *spot] = real
            table[child, 0, :, pair, 0, 1, *spot] = -imag
            table[child, 1, :, pair, 0, 0, *spot] = -imag
            table[child, 1, :, pair, 0, 1, *spot] = -real
            table[child, 0, :, pair, 1, 0, *spot] = imag
            table[child, 0, :, pair, 1, 1, *spot] = real
            table[child, 1, :, pair, 1, 0, *spot] = real
            table[child, 1, :, pair, 1, 1, *spot] = -imag
    return table.reshape(4 * child_angles, 32 * pulse_count)


def small_unit(angle):
    square = angle * angle
    cosine = 1.0 + square * (-1 / 2 + square * (1 / 24 + square * (-1 / 720 + square / 40320)))
    sine = angle * (1.0 + square * (-1 / 6 + square * (1 / 120 + square * (-1 / 5040))))
    return cosine, sine


def unit(angle):
    quarter = jnp.floor(angle * (2.0 / math.pi) + 0.5)
    rest = angle - quarter * 1.5703125
    rest = rest - quarter * (math.pi / 2 - 1.5703125)
    cosine, sine = small_unit(rest)
    turn = quarter.astype(jnp.int32)
    odd = (turn & 1) == 1
    first = jnp.where(odd, sine, cosine)
    second = jnp.where(odd, cosine, sine)
    first = jnp.where(((turn + 1) & 2) == 2, -first, first)
    second = jnp.where((turn & 2) == 2, -second, second)
    return first, second


def times(left, right):
    return (
        left[0] * right[0] - left[1] * right[1],
        left[0] * right[1] + left[1] * right[0],
    )


def cut_kernel(place_ref, raw_ref, *outs):
    for step, out in enumerate(outs):
        first = pl.multiple_of((place_ref[0] ^ step) * LANES, LANES)
        out[...] = raw_ref[:, :, pl.ds(first, LANES)]


def phase_rows(ref, rate, start, total):
    size = (LANES, LANES)
    blocks, angles = ref.shape[1], ref.shape[2]
    lane = lax.broadcasted_iota(jnp.int32, size, 1).astype(jnp.float32)
    factor = 1.0 + (lane + start) / total

    @pl.loop(0, angles // LANES)
    def _(part):
        row = lax.broadcasted_iota(jnp.int32, size, 0) + part * LANES
        slope = rate * ((row.astype(jnp.float32) + 0.5) / angles - 0.5)
        value = unit(slope * factor)
        step = small_unit(slope * (LANES / total))
        at = pl.ds(pl.multiple_of(part * LANES, LANES), LANES)
        for block in range(blocks):
            ref[0, block, at, :] = value[0].astype(jnp.bfloat16)
            ref[1, block, at, :] = value[1].astype(jnp.bfloat16)
            if block + 1 < blocks:
                value = times(value, step)


def weight_rows(pulse_count, weight_ref, steer_ref, one_ref, two_ref):
    joined = jnp.concatenate([weight_ref[0, c, part] for c in range(2) for part in range(2)], 1)
    parents = joined.shape[0]
    width = one_ref.shape[2]
    lane = lax.broadcasted_iota(jnp.int32, (parents, width), 1)
    odd_pulse = lane % 2 == 1
    odd_child = lane // pulse_count % 2 == 1
    children = one_ref.shape[1] // 8
    for pair in range(2):
        for part in range(2):
            at = (pair * 2 + part) * width
            value = jnp.dot(
                joined, steer_ref[:, at : at + width], preferred_element_type=jnp.float32
            )
            for turn in range(2):
                turned = jnp.where(odd_pulse, -value, value) if turn else value
                kinds = (turned, jnp.where(odd_child, -turned, turned))
                for kind, rows in enumerate(kinds):
                    rows = rows.astype(jnp.bfloat16)
                    for first in range(0, parents, TILE):
                        block, tile = divmod(first, children)
                        row = (tile // TILE * 8 + pair * 4 + kind * 2 + part) * TILE
                        one_ref[turn * (parents // children) + block, row : row + TILE, :] = rows[
                            first : first + TILE
                        ]
    for child in range(2):
        for tile in range(parents // TILE):
            at = slice(tile * TILE, (tile + 1) * TILE)
            real, imag = weight_ref[1, child, 0, at], weight_ref[1, child, 1, at]
            row = 2 * tile * TILE
            two_ref[child, row : row + TILE] = jnp.concatenate([real, -imag], 1)
            two_ref[child, row + TILE : row + 2 * TILE] = jnp.concatenate([imag, real], 1)


def table_kernel(pulse_count, total, place_ref, rate_ref, *refs):
    offset_refs, filter_ref, weight_ref, steer_ref = refs[:QUAD], *refs[QUAD : QUAD + 3]
    gain_ref, one_ref, two_ref, phase_one_ref, phase_two_ref, done_ref = refs[QUAD + 3 :]
    start = (place_ref[1] * (total // QUAD)).astype(jnp.float32)
    done_ref[0] = 1
    phase_rows(phase_one_ref, rate_ref[0], start, total)
    phase_rows(phase_two_ref, rate_ref[1], start, total)
    gain_rows(total, place_ref, offset_refs, filter_ref, gain_ref)
    weight_rows(pulse_count, weight_ref, steer_ref, one_ref, two_ref)


def gain_rows(total, place_ref, offset_refs, filter_ref, out_ref):
    second = total // FIRST
    member = place_ref[1]
    offsets = []
    for owner in range(QUAD):
        value = offset_refs[0][...]
        for rel in range(1, QUAD):
            value = jnp.where((member ^ rel) == owner, offset_refs[rel][...], value)
        offsets.append(value)
    offsets = jnp.concatenate(offsets, 1)
    shift = offsets - place_ref[1] * (total // QUAD)
    scale = -2.0 * math.pi / total

    def ramp(rows, stride):
        k_index = stride * lax.broadcasted_iota(jnp.int32, (rows, LANES), 0)
        return unit(scale * ((k_index * shift) & (total - 1)).astype(jnp.float32))

    low, high = ramp(FIRST, 1), ramp(second, FIRST)
    for k_one in range(FIRST):
        row = (low[0][k_one : k_one + 1] * (1.0 / total), low[1][k_one : k_one + 1] * (1.0 / total))
        column = (filter_ref[0, :, k_one : k_one + 1], filter_ref[1, :, k_one : k_one + 1])
        value = times(times(high, row), column)
        out_ref[0, k_one] = value[0].astype(jnp.bfloat16)
        out_ref[1, k_one] = value[1].astype(jnp.bfloat16)


def kernel(count, total, place_ref, turn_ref, *rest):
    fone_ref, ftwo_ref, itwo_ref, ione_ref = rest[:4]
    gain_ref, rows_one_ref, rows_two_ref, phase_one_ref, phase_two_ref = rest[4:9]
    pieces, out_ref, rest = rest[9:-8], rest[-8], rest[-7:]
    samples, partial_ref, folded, compressed, image, ready, sems = rest
    span = total // count
    second = total // FIRST
    chunks = second // TILE
    kept = FIRST // QUAD
    half = FIRST * TILE
    f32, bf16 = jnp.float32, jnp.bfloat16

    def dot(left, right):
        return jnp.dot(left, right, preferred_element_type=f32)

    def turned(real, imag, chunk, k_one, sign):
        cosine, sine = turn_ref[0, chunk, k_one], turn_ref[1, chunk, k_one] * sign
        return (
            (cosine * real - sine * imag).astype(bf16),
            (cosine * imag + sine * real).astype(bf16),
        )

    index = place_ref[0] * QUAD + place_ref[1]
    per_row = second // span
    for number, piece in enumerate(pieces):
        source = index ^ number
        rows = pl.ds(pl.multiple_of(source % per_row * span, TILE), span)
        samples[:, source // per_row, rows] = piece[...]

    @pl.loop(0, chunks // 2, unroll=True)
    def _(pair):
        right = jnp.concatenate(
            [
                samples[:, :, pl.ds((2 * pair + side) * TILE, TILE)].reshape(2 * half, LANES)
                for side in range(2)
            ],
            1,
        )
        result = dot(fone_ref[...], right)
        for side in range(2):
            chunk = 2 * pair + side
            lanes = slice(side * LANES, (side + 1) * LANES)
            for k_one in range(FIRST):
                row = 2 * k_one * TILE
                real = result[row : row + TILE, lanes]
                imag = result[row + TILE : row + 2 * TILE, lanes]
                real, imag = turned(real, imag, chunk, k_one, -1.0)
                partial_ref[k_one, 0, chunk] = real
                partial_ref[k_one, 1, chunk] = imag

    @pl.loop(0, FIRST // 2, unroll=True)
    def _(pair):
        right = jnp.concatenate(
            [partial_ref[2 * pair + side].reshape(2 * second, LANES) for side in range(2)], 1
        )
        result = dot(ftwo_ref[...], right)
        scaled = []
        for side in range(2):
            k_one = 2 * pair + side
            lanes = slice(side * LANES, (side + 1) * LANES)
            parts = []
            for chunk in range(chunks):
                row = 2 * chunk * TILE
                at = slice(chunk * TILE, (chunk + 1) * TILE)
                real = result[row : row + TILE, lanes]
                imag = result[row + TILE : row + 2 * TILE, lanes]
                gain_real = gain_ref[0, k_one, at].astype(f32)
                gain_imag = gain_ref[1, k_one, at].astype(f32)
                parts.append((real * gain_real - imag * gain_imag).astype(bf16))
                parts.append((real * gain_imag + imag * gain_real).astype(bf16))
            scaled.append(jnp.concatenate(parts, 0))
        result = dot(itwo_ref[...], jnp.concatenate(scaled, 1))
        for side in range(2):
            k_one = 2 * pair + side
            lanes = slice(side * LANES, (side + 1) * LANES)
            for chunk in range(chunks):
                row = 2 * chunk * TILE
                real = result[row : row + TILE, lanes]
                imag = result[row + TILE : row + 2 * TILE, lanes]
                real, imag = turned(real, imag, chunk, k_one, 1.0)
                folded[chunk, 0, k_one] = real
                folded[chunk, 1, k_one] = imag

    @pl.loop(0, chunks // 2, unroll=True)
    def _(pair):
        right = jnp.concatenate(
            [folded[2 * pair + side].reshape(2 * half, LANES) for side in range(2)], 1
        )
        result = dot(ione_ref[...], right).astype(bf16)
        for side in range(2):
            lanes = slice(side * LANES, (side + 1) * LANES)
            for part in range(2):
                for n_one in range(kept):
                    row = (part * kept + n_one) * TILE
                    compressed[n_one, 2 * pair + side, :, part * LANES : (part + 1) * LANES] = (
                        result[row : row + TILE, lanes]
                    )

    width = image.shape[4]
    blocks = width // LANES
    block_angles = image.shape[3]
    angle_blocks = image.shape[1]
    wide = rows_two_ref.shape[1] // 2
    steps = total // QUAD // width
    per_step = second // width

    def out_copy(step, slot):
        at = pl.ds(pl.multiple_of(step * width, width), width)
        return pltpu.make_async_copy(ready.at[slot], out_ref.at[:, :, at], sems.at[slot])

    @pl.loop(0, steps)
    def _(step):
        slot = step % 2
        tiles_wide = width // TILE
        first_tile = pl.multiple_of(step % per_step * tiles_wide, tiles_wide)
        columns = compressed[step // per_step, pl.ds(first_tile, tiles_wide)].reshape(
            width, 2 * LANES
        )

        def phases(ref, rows):
            return [
                jnp.concatenate(
                    [ref[part, step * blocks + b, rows, :] for b in range(blocks)], 1
                ).astype(f32)
                for part in range(2)
            ]

        for block in range(angle_blocks):
            result = lax.dot_general(
                rows_one_ref[block],
                columns,
                (((1,), (1,)), ((), ())),
                preferred_element_type=f32,
            )
            for tile in range(block_angles // TILE):
                at = slice(tile * TILE, (tile + 1) * TILE)
                cosine, sine = phases(
                    phase_one_ref, pl.ds(block * block_angles + tile * TILE, TILE)
                )
                for pick in range(2):
                    terms = [
                        result[row : row + TILE]
                        for row in [((tile * 2 + pick) * 4 + kind) * TILE for kind in range(4)]
                    ]
                    image[pick, block, 0, at] = (cosine * terms[0] + sine * terms[3]).astype(bf16)
                    image[pick, block, 1, at] = (cosine * terms[1] - sine * terms[2]).astype(bf16)

        @pl.when(step >= 2)
        def _():
            out_copy(step - 2, slot).wait()

        for block in range(angle_blocks):
            lower = dot(rows_two_ref[0], image[0, block].reshape(2 * block_angles, width))
            upper = dot(rows_two_ref[1], image[1, block].reshape(2 * block_angles, width))
            for tile in range(wide // TILE):
                rows = pl.ds(block * wide + tile * TILE, TILE)
                cosine, sine = phases(phase_two_ref, rows)
                real = slice(2 * tile * TILE, (2 * tile + 1) * TILE)
                imag = slice((2 * tile + 1) * TILE, (2 * tile + 2) * TILE)
                ready[slot, 0, rows, :] = cosine * (lower[real] + upper[real]) + sine * (
                    lower[imag] - upper[imag]
                )
                ready[slot, 1, rows, :] = cosine * (lower[imag] + upper[imag]) + sine * (
                    upper[real] - lower[real]
                )
        out_copy(step, slot).start()

    for step in range(max(steps - 2, 0), steps):
        out_copy(step, step % 2).wait()


def hold_kernel(*refs):
    pass


def hold(value, flag, after=None):
    far = pl.BlockSpec(memory_space=pl.ANY)
    others = [] if after is None else [after]
    return pl.pallas_call(
        hold_kernel,
        out_shape=jax.ShapeDtypeStruct(value.shape, value.dtype),
        in_specs=[far, pl.BlockSpec(memory_space=pltpu.SMEM)] + [far] * len(others),
        out_specs=far,
        input_output_aliases={0: 0},
        cost_estimate=pl.CostEstimate(flops=1, bytes_accessed=1, transcendentals=0),
        compiler_params=pltpu.CompilerParams(vmem_limit_bytes=1024 * 1024),
    )(value, flag, *others)


def focus(place, turns, tables, made, pieces):
    _, rows_one, rows_two, phase_one, _ = made
    count = len(pieces)
    total = phase_one.shape[1] * phase_one.shape[3] * QUAD
    second = total // FIRST
    chunks = second // TILE
    step_width = 256
    bf16, f32 = jnp.bfloat16, jnp.float32
    smem = pl.BlockSpec(memory_space=pltpu.SMEM)
    vmem = pl.BlockSpec(memory_space=pltpu.VMEM)
    far = pl.BlockSpec(memory_space=pltpu.HBM)
    parents, children = rows_two.shape[1] // 2, rows_two.shape[2] // 2
    angle_blocks = rows_one.shape[0]
    return pl.pallas_call(
        functools.partial(kernel, count, total),
        out_shape=jax.ShapeDtypeStruct((2, angle_blocks * parents, total // QUAD), f32),
        in_specs=[smem, smem] + [vmem] * (9 + count),
        out_specs=far,
        scratch_shapes=[
            pltpu.VMEM((2, FIRST, second, LANES), bf16),
            pltpu.VMEM((FIRST, 2, chunks, TILE, LANES), bf16),
            pltpu.VMEM((chunks, 2, FIRST, TILE, LANES), bf16),
            pltpu.VMEM((FIRST // QUAD, chunks, TILE, 2 * LANES), bf16),
            pltpu.VMEM((2, angle_blocks, 2, children, step_width), bf16),
            pltpu.VMEM((2, 2, angle_blocks * parents, step_width), f32),
            pltpu.SemaphoreType.DMA((2,)),
        ],
        compiler_params=pltpu.CompilerParams(vmem_limit_bytes=24 * 1024 * 1024),
    )(place, turns, *tables, *made, *pieces)


def body(raw_echo, range_filter, range_offsets, interp_weight, phase_rate):
    count = lax.axis_size("ap")
    index = lax.axis_index("ap")
    total = range_filter.shape[1]
    pulse_count = range_offsets.shape[0]
    groups = count // QUAD
    width = total // QUAD
    second = total // FIRST
    f32, bf16 = jnp.float32, jnp.bfloat16
    smem = pl.BlockSpec(memory_space=pltpu.SMEM)
    vmem = pl.BlockSpec(memory_space=pltpu.VMEM)
    place = jnp.stack([index // QUAD, index % QUAD]).astype(jnp.int32)

    def move(value, bits):
        return lax.ppermute(value, "ap", [(i, i ^ bits) for i in range(count)])

    def shape(dims, kind=bf16):
        return jax.ShapeDtypeStruct(dims, kind)

    flag = shape((1,), jnp.int32)
    small = pltpu.CompilerParams(vmem_limit_bytes=2 * 1024 * 1024)

    def cost(flops, moved):
        return pl.CostEstimate(flops=flops, bytes_accessed=moved, transcendentals=0)

    cut = pl.pallas_call(
        cut_kernel,
        out_shape=[shape((2, total // count, LANES))] * groups,
        in_specs=[smem, vmem],
        out_specs=[vmem] * groups,
        compiler_params=small,
    )(place, raw_echo)
    near = jnp.stack([range_offsets, move(range_offsets, 1)])
    joined = [near, move(near, 2)]
    offsets = [joined[rel // 2][rel % 2 : rel % 2 + 1] for rel in range(QUAD)]

    child_angles = interp_weight.shape[4]
    steer = jnp.asarray(steer_blocks(pulse_count, child_angles))
    *made, made_flag = pl.pallas_call(
        functools.partial(table_kernel, pulse_count, total),
        out_shape=[
            shape((2, FIRST, second, LANES)),
            shape((2 * A0 // child_angles, 8 * child_angles, 2 * LANES)),
            shape((2, 2 * interp_weight.shape[3], 2 * child_angles)),
            shape((2, width // LANES, 2 * A0, LANES)),
            shape((2, width // LANES, 4 * A0, LANES)),
            flag,
        ],
        in_specs=[smem, smem] + [vmem] * (QUAD + 3),
        out_specs=[vmem] * 5 + [smem],
        cost_estimate=cost(2**30, 2**23),
        compiler_params=small,
    )(
        place,
        phase_rate,
        *offsets,
        range_filter.reshape(2, second, FIRST),
        interp_weight,
        steer,
    )

    own = [cut[0]] + [move(cut[step], QUAD * step) for step in range(1, groups)]
    first = move(own[1], 2)
    own[2 % groups] = hold(own[2 % groups], made_flag, after=first)
    across = [move(own[0], 2), first] + [move(piece, 2) for piece in own[2:]]
    beside = [move(piece, 1) for piece in own]
    diagonal = [move(piece, 1) for piece in across]
    pieces = [part for four in zip(own, beside, across, diagonal) for part in four]
    tables = [jnp.asarray(t) for t in dft_tables(total)]
    return focus(place, jnp.asarray(turn_table(total)), tables, made, pieces)


def solution(mesh):
    placed = (P(None, "ap", "grp"), P(), P(("grp", "ap")), P(), P())
    return jax.shard_map(
        body, mesh=mesh, in_specs=placed, out_specs=P(None, None, ("grp", "ap")), check_vma=False
    )
```

```python
import functools
import math

import jax
import jax.numpy as jnp
import ml_dtypes
import numpy as np
from jax import lax
from jax.experimental import pallas as pl
from jax.experimental.pallas import tpu as pltpu
from jax.sharding import PartitionSpec as P

A0 = 256
QUAD = 4
LANES = 128
FIRST = 16
TILE = 16


def as_real(matrix):
    top = np.concatenate([matrix.real, -matrix.imag], 1)
    low = np.concatenate([matrix.imag, matrix.real], 1)
    return np.concatenate([top, low], 0).astype(ml_dtypes.bfloat16)


def by_tile(matrix):
    shaped = matrix.reshape(2, -1, TILE, matrix.shape[1])
    return shaped.transpose(1, 0, 2, 3).reshape(matrix.shape)


def root(length, turns):
    return np.exp(-2j * np.pi / length * (turns % length))


def dft_tables(total):
    second = total // FIRST
    one = np.arange(FIRST)
    low = np.arange(TILE)
    k_one = one[:, None, None, None]
    l_row = low[None, :, None, None]
    n_one = one[None, None, :, None]
    l_col = low[None, None, None, :]
    same = l_row == l_col
    forward_one = root(FIRST, k_one * n_one) * root(total, l_row * k_one) * same
    forward_one = forward_one.reshape(FIRST * TILE, FIRST * TILE)
    two = np.arange(second)
    forward_two = root(second, two[:, None] * two[None, :])
    inverse_two = forward_two.conj()
    kept = np.arange(FIRST // QUAD)[:, None, None, None]
    inverse_one = (root(FIRST, kept * n_one) * root(total, l_col * n_one)).conj() * same
    inverse_one = inverse_one.reshape(FIRST // QUAD * TILE, FIRST * TILE)
    one, two, three, four = (
        as_real(t) for t in (forward_one, forward_two, inverse_two, inverse_one)
    )
    return [by_tile(one), by_tile(two), by_tile(by_tile(three).T).T, four]


def turn_table(total):
    chunks = total // FIRST // TILE
    value = root(total, TILE * np.arange(chunks)[:, None] * np.arange(FIRST)[None, :]).conj()
    return np.stack([value.real, value.imag]).astype(np.float32)


def steer_table(angle_count, pulse_count):
    angle_index = np.arange(angle_count)[:, None]
    pulse_index = np.arange(pulse_count)[None, :]
    value = root(angle_count, (angle_index + angle_count // 2) * pulse_index)
    value = (value / math.sqrt(pulse_count)).astype(np.complex64)
    return value.real.astype(ml_dtypes.bfloat16), value.imag.astype(ml_dtypes.bfloat16)


def steer_blocks(pulse_count, child_angles):
    real, imag = steer_table(A0, pulse_count)
    real, imag = real[:child_angles], imag[:child_angles]
    table = np.zeros((2, 2, child_angles, 2, 2, 2, 2, 2, pulse_count), ml_dtypes.bfloat16)
    for pair in range(2):
        for child in range(2):
            spot = (pair, child)
            table[child, 0, :, pair, 0, 0, *spot] = real
            table[child, 0, :, pair, 0, 1, *spot] = -imag
            table[child, 1, :, pair, 0, 0, *spot] = -imag
            table[child, 1, :, pair, 0, 1, *spot] = -real
            table[child, 0, :, pair, 1, 0, *spot] = imag
            table[child, 0, :, pair, 1, 1, *spot] = real
            table[child, 1, :, pair, 1, 0, *spot] = real
            table[child, 1, :, pair, 1, 1, *spot] = -imag
    return table.reshape(4 * child_angles, 32 * pulse_count)


def small_unit(angle):
    square = angle * angle
    cosine = 1.0 + square * (-1 / 2 + square * (1 / 24 + square * (-1 / 720 + square / 40320)))
    sine = angle * (1.0 + square * (-1 / 6 + square * (1 / 120 + square * (-1 / 5040))))
    return cosine, sine


def unit(angle):
    quarter = jnp.floor(angle * (2.0 / math.pi) + 0.5)
    rest = angle - quarter * 1.5703125
    rest = rest - quarter * (math.pi / 2 - 1.5703125)
    cosine, sine = small_unit(rest)
    turn = quarter.astype(jnp.int32)
    odd = (turn & 1) == 1
    first = jnp.where(odd, sine, cosine)
    second = jnp.where(odd, cosine, sine)
    first = jnp.where(((turn + 1) & 2) == 2, -first, first)
    second = jnp.where((turn & 2) == 2, -second, second)
    return first, second


def times(left, right):
    return (
        left[0] * right[0] - left[1] * right[1],
        left[0] * right[1] + left[1] * right[0],
    )


def cut_kernel(place_ref, raw_ref, *outs):
    for step, out in enumerate(outs):
        first = pl.multiple_of((place_ref[0] ^ step) * LANES, LANES)
        out[...] = raw_ref[:, :, pl.ds(first, LANES)]


def phase_rows(ref, rate, start, total):
    size = (LANES, LANES)
    blocks, angles = ref.shape[1], ref.shape[2]
    lane = lax.broadcasted_iota(jnp.int32, size, 1).astype(jnp.float32)
    factor = 1.0 + (lane + start) / total

    @pl.loop(0, angles // LANES)
    def _(part):
        row = lax.broadcasted_iota(jnp.int32, size, 0) + part * LANES
        slope = rate * ((row.astype(jnp.float32) + 0.5) / angles - 0.5)
        value = unit(slope * factor)
        step = small_unit(slope * (LANES / total))
        at = pl.ds(pl.multiple_of(part * LANES, LANES), LANES)
        for block in range(blocks):
            ref[0, block, at, :] = value[0].astype(jnp.bfloat16)
            ref[1, block, at, :] = value[1].astype(jnp.bfloat16)
            if block + 1 < blocks:
                value = times(value, step)


def weight_rows(pulse_count, weight_ref, steer_ref, one_ref, two_ref):
    joined = jnp.concatenate([weight_ref[0, c, part] for c in range(2) for part in range(2)], 1)
    parents = joined.shape[0]
    width = one_ref.shape[2]
    lane = lax.broadcasted_iota(jnp.int32, (parents, width), 1)
    odd_pulse = lane % 2 == 1
    odd_child = lane // pulse_count % 2 == 1
    children = one_ref.shape[1] // 8
    for pair in range(2):
        for part in range(2):
            at = (pair * 2 + part) * width
            value = jnp.dot(
                joined, steer_ref[:, at : at + width], preferred_element_type=jnp.float32
            )
            for turn in range(2):
                turned = jnp.where(odd_pulse, -value, value) if turn else value
                kinds = (turned, jnp.where(odd_child, -turned, turned))
                for kind, rows in enumerate(kinds):
                    rows = rows.astype(jnp.bfloat16)
                    for first in range(0, parents, TILE):
                        block, tile = divmod(first, children)
                        row = (tile // TILE * 8 + pair * 4 + kind * 2 + part) * TILE
                        one_ref[turn * (parents // children) + block, row : row + TILE, :] = rows[
                            first : first + TILE
                        ]
    for child in range(2):
        for tile in range(parents // TILE):
            at = slice(tile * TILE, (tile + 1) * TILE)
            real, imag = weight_ref[1, child, 0, at], weight_ref[1, child, 1, at]
            row = 2 * tile * TILE
            two_ref[child, row : row + TILE] = jnp.concatenate([real, -imag], 1)
            two_ref[child, row + TILE : row + 2 * TILE] = jnp.concatenate([imag, real], 1)


def table_kernel(pulse_count, total, place_ref, rate_ref, *refs):
    offset_refs, filter_ref, weight_ref, steer_ref = refs[:2], *refs[2:5]
    gain_ref, one_ref, two_ref, phase_one_ref, phase_two_ref, done_ref = refs[5:]
    start = (place_ref[1] * (total // QUAD)).astype(jnp.float32)
    done_ref[0] = 1
    phase_rows(phase_one_ref, rate_ref[0], start, total)
    phase_rows(phase_two_ref, rate_ref[1], start, total)
    gain_rows(total, place_ref, offset_refs, filter_ref, gain_ref)
    weight_rows(pulse_count, weight_ref, steer_ref, one_ref, two_ref)


def gain_rows(total, place_ref, offset_refs, filter_ref, out_ref):
    second = total // FIRST
    member = place_ref[1]
    offsets = []
    known = [offset_refs[rel // 2][rel % 2 : rel % 2 + 1, :] for rel in range(QUAD)]
    for owner in range(QUAD):
        value = known[0]
        for rel in range(1, QUAD):
            value = jnp.where((member ^ rel) == owner, known[rel], value)
        offsets.append(value)
    offsets = jnp.concatenate(offsets, 1)
    shift = offsets - place_ref[1] * (total // QUAD)
    scale = -2.0 * math.pi / total

    def ramp(rows, stride):
        k_index = stride * lax.broadcasted_iota(jnp.int32, (rows, LANES), 0)
        return unit(scale * ((k_index * shift) & (total - 1)).astype(jnp.float32))

    low, high = ramp(FIRST, 1), ramp(second, FIRST)
    for k_one in range(FIRST):
        row = (low[0][k_one : k_one + 1] * (1.0 / total), low[1][k_one : k_one + 1] * (1.0 / total))
        column = (filter_ref[0, :, k_one : k_one + 1], filter_ref[1, :, k_one : k_one + 1])
        value = times(times(high, row), column)
        out_ref[0, k_one] = value[0].astype(jnp.bfloat16)
        out_ref[1, k_one] = value[1].astype(jnp.bfloat16)


def kernel(count, total, place_ref, turn_ref, *rest):
    fone_ref, ftwo_ref, itwo_ref, ione_ref = rest[:4]
    gain_ref, rows_one_ref, rows_two_ref, phase_one_ref, phase_two_ref = rest[4:9]
    pieces, out_ref, rest = rest[9:-8], rest[-8], rest[-7:]
    samples, partial_ref, folded, compressed, image, ready, sems = rest
    span = total // count
    second = total // FIRST
    chunks = second // TILE
    kept = FIRST // QUAD
    half = FIRST * TILE
    f32, bf16 = jnp.float32, jnp.bfloat16

    def dot(left, right):
        return jnp.dot(left, right, preferred_element_type=f32)

    def turned(real, imag, chunk, k_one, sign):
        cosine, sine = turn_ref[0, chunk, k_one], turn_ref[1, chunk, k_one] * sign
        return (
            (cosine * real - sine * imag).astype(bf16),
            (cosine * imag + sine * real).astype(bf16),
        )

    index = place_ref[0] * QUAD + place_ref[1]
    per_row = second // span
    order = ((step, rel) for step in (0, 1) for rel in range(QUAD))
    order = sorted(order, key=lambda spot: spot[1])
    order += [(step, rel) for step in range(2, count // QUAD) for rel in range(QUAD)]
    loaded = [piece[spot] for piece in pieces[:QUAD] for spot in range(2)]
    loaded += [piece[...] for piece in pieces[QUAD:]]
    for (step, rel), piece in zip(order, loaded):
        source = index ^ (QUAD * step + rel)
        rows = pl.ds(pl.multiple_of(source % per_row * span, TILE), span)
        samples[:, source // per_row, rows] = piece

    @pl.loop(0, chunks // 2, unroll=True)
    def _(pair):
        right = jnp.concatenate(
            [
                samples[:, :, pl.ds((2 * pair + side) * TILE, TILE)].reshape(2 * half, LANES)
                for side in range(2)
            ],
            1,
        )
        result = dot(fone_ref[...], right)
        for side in range(2):
            chunk = 2 * pair + side
            lanes = slice(side * LANES, (side + 1) * LANES)
            for k_one in range(FIRST):
                row = 2 * k_one * TILE
                real = result[row : row + TILE, lanes]
                imag = result[row + TILE : row + 2 * TILE, lanes]
                real, imag = turned(real, imag, chunk, k_one, -1.0)
                partial_ref[k_one, 0, chunk] = real
                partial_ref[k_one, 1, chunk] = imag

    @pl.loop(0, FIRST // 2, unroll=True)
    def _(pair):
        right = jnp.concatenate(
            [partial_ref[2 * pair + side].reshape(2 * second, LANES) for side in range(2)], 1
        )
        result = dot(ftwo_ref[...], right)
        scaled = []
        for side in range(2):
            k_one = 2 * pair + side
            lanes = slice(side * LANES, (side + 1) * LANES)
            parts = []
            for chunk in range(chunks):
                row = 2 * chunk * TILE
                at = slice(chunk * TILE, (chunk + 1) * TILE)
                real = result[row : row + TILE, lanes]
                imag = result[row + TILE : row + 2 * TILE, lanes]
                gain_real = gain_ref[0, k_one, at].astype(f32)
                gain_imag = gain_ref[1, k_one, at].astype(f32)
                parts.append((real * gain_real - imag * gain_imag).astype(bf16))
                parts.append((real * gain_imag + imag * gain_real).astype(bf16))
            scaled.append(jnp.concatenate(parts, 0))
        result = dot(itwo_ref[...], jnp.concatenate(scaled, 1))
        for side in range(2):
            k_one = 2 * pair + side
            lanes = slice(side * LANES, (side + 1) * LANES)
            for chunk in range(chunks):
                row = 2 * chunk * TILE
                real = result[row : row + TILE, lanes]
                imag = result[row + TILE : row + 2 * TILE, lanes]
                real, imag = turned(real, imag, chunk, k_one, 1.0)
                folded[chunk, 0, k_one] = real
                folded[chunk, 1, k_one] = imag

    @pl.loop(0, chunks // 2, unroll=True)
    def _(pair):
        right = jnp.concatenate(
            [folded[2 * pair + side].reshape(2 * half, LANES) for side in range(2)], 1
        )
        result = dot(ione_ref[...], right).astype(bf16)
        for side in range(2):
            lanes = slice(side * LANES, (side + 1) * LANES)
            for part in range(2):
                for n_one in range(kept):
                    row = (part * kept + n_one) * TILE
                    compressed[n_one, 2 * pair + side, :, part * LANES : (part + 1) * LANES] = (
                        result[row : row + TILE, lanes]
                    )

    width = image.shape[4]
    blocks = width // LANES
    block_angles = image.shape[3]
    angle_blocks = image.shape[1]
    wide = rows_two_ref.shape[1] // 2
    steps = total // QUAD // width
    per_step = second // width

    def out_copy(step, slot):
        at = pl.ds(pl.multiple_of(step * width, width), width)
        return pltpu.make_async_copy(ready.at[slot], out_ref.at[:, :, at], sems.at[slot])

    @pl.loop(0, steps)
    def _(step):
        slot = step % 2
        tiles_wide = width // TILE
        first_tile = pl.multiple_of(step % per_step * tiles_wide, tiles_wide)
        columns = compressed[step // per_step, pl.ds(first_tile, tiles_wide)].reshape(
            width, 2 * LANES
        )

        def phases(ref, rows):
            return [
                jnp.concatenate(
                    [ref[part, step * blocks + b, rows, :] for b in range(blocks)], 1
                ).astype(f32)
                for part in range(2)
            ]

        for block in range(angle_blocks):
            result = lax.dot_general(
                rows_one_ref[block],
                columns,
                (((1,), (1,)), ((), ())),
                preferred_element_type=f32,
            )
            for tile in range(block_angles // TILE):
                at = slice(tile * TILE, (tile + 1) * TILE)
                cosine, sine = phases(
                    phase_one_ref, pl.ds(block * block_angles + tile * TILE, TILE)
                )
                for pick in range(2):
                    terms = [
                        result[row : row + TILE]
                        for row in [((tile * 2 + pick) * 4 + kind) * TILE for kind in range(4)]
                    ]
                    image[pick, block, 0, at] = (cosine * terms[0] + sine * terms[3]).astype(bf16)
                    image[pick, block, 1, at] = (cosine * terms[1] - sine * terms[2]).astype(bf16)

        @pl.when(step >= 2)
        def _():
            out_copy(step - 2, slot).wait()

        for block in range(angle_blocks):
            lower = dot(rows_two_ref[0], image[0, block].reshape(2 * block_angles, width))
            upper = dot(rows_two_ref[1], image[1, block].reshape(2 * block_angles, width))
            for tile in range(wide // TILE):
                rows = pl.ds(block * wide + tile * TILE, TILE)
                cosine, sine = phases(phase_two_ref, rows)
                real = slice(2 * tile * TILE, (2 * tile + 1) * TILE)
                imag = slice((2 * tile + 1) * TILE, (2 * tile + 2) * TILE)
                ready[slot, 0, rows, :] = cosine * (lower[real] + upper[real]) + sine * (
                    lower[imag] - upper[imag]
                )
                ready[slot, 1, rows, :] = cosine * (lower[imag] + upper[imag]) + sine * (
                    upper[real] - lower[real]
                )
        out_copy(step, slot).start()

    for step in range(max(steps - 2, 0), steps):
        out_copy(step, step % 2).wait()


def pack_kernel(*refs):
    for spot in range(refs[-1].shape[0]):
        refs[-1][spot] = refs[spot][...]


def pack(pieces):
    vmem = pl.BlockSpec(memory_space=pltpu.VMEM)
    return pl.pallas_call(
        pack_kernel,
        out_shape=jax.ShapeDtypeStruct((len(pieces), *pieces[0].shape), pieces[0].dtype),
        in_specs=[vmem] * len(pieces),
        out_specs=vmem,
        cost_estimate=pl.CostEstimate(flops=1, bytes_accessed=1, transcendentals=0),
        compiler_params=pltpu.CompilerParams(vmem_limit_bytes=1024 * 1024),
    )(*pieces)


def hold_kernel(*refs):
    pass


def hold(value, flag, after=None):
    far = pl.BlockSpec(memory_space=pl.ANY)
    others = [] if after is None else [after]
    return pl.pallas_call(
        hold_kernel,
        out_shape=jax.ShapeDtypeStruct(value.shape, value.dtype),
        in_specs=[far, pl.BlockSpec(memory_space=pltpu.SMEM)] + [far] * len(others),
        out_specs=far,
        input_output_aliases={0: 0},
        cost_estimate=pl.CostEstimate(flops=1, bytes_accessed=1, transcendentals=0),
        compiler_params=pltpu.CompilerParams(vmem_limit_bytes=1024 * 1024),
    )(value, flag, *others)


def focus(place, turns, tables, made, pieces):
    _, rows_one, rows_two, phase_one, _ = made
    count = len(pieces) + QUAD
    total = phase_one.shape[1] * phase_one.shape[3] * QUAD
    second = total // FIRST
    chunks = second // TILE
    step_width = 256
    bf16, f32 = jnp.bfloat16, jnp.float32
    smem = pl.BlockSpec(memory_space=pltpu.SMEM)
    vmem = pl.BlockSpec(memory_space=pltpu.VMEM)
    far = pl.BlockSpec(memory_space=pltpu.HBM)
    parents, children = rows_two.shape[1] // 2, rows_two.shape[2] // 2
    angle_blocks = rows_one.shape[0]
    return pl.pallas_call(
        functools.partial(kernel, count, total),
        out_shape=jax.ShapeDtypeStruct((2, angle_blocks * parents, total // QUAD), f32),
        in_specs=[smem, smem] + [vmem] * (9 + len(pieces)),
        out_specs=far,
        scratch_shapes=[
            pltpu.VMEM((2, FIRST, second, LANES), bf16),
            pltpu.VMEM((FIRST, 2, chunks, TILE, LANES), bf16),
            pltpu.VMEM((chunks, 2, FIRST, TILE, LANES), bf16),
            pltpu.VMEM((FIRST // QUAD, chunks, TILE, 2 * LANES), bf16),
            pltpu.VMEM((2, angle_blocks, 2, children, step_width), bf16),
            pltpu.VMEM((2, 2, angle_blocks * parents, step_width), f32),
            pltpu.SemaphoreType.DMA((2,)),
        ],
        compiler_params=pltpu.CompilerParams(vmem_limit_bytes=24 * 1024 * 1024),
    )(place, turns, *tables, *made, *pieces)


def body(raw_echo, range_filter, range_offsets, interp_weight, phase_rate):
    count = lax.axis_size("ap")
    index = lax.axis_index("ap")
    total = range_filter.shape[1]
    pulse_count = range_offsets.shape[0]
    groups = count // QUAD
    width = total // QUAD
    second = total // FIRST
    f32, bf16 = jnp.float32, jnp.bfloat16
    smem = pl.BlockSpec(memory_space=pltpu.SMEM)
    vmem = pl.BlockSpec(memory_space=pltpu.VMEM)
    place = jnp.stack([index // QUAD, index % QUAD]).astype(jnp.int32)

    def move(value, bits):
        return lax.ppermute(value, "ap", [(i, i ^ bits) for i in range(count)])

    def shape(dims, kind=bf16):
        return jax.ShapeDtypeStruct(dims, kind)

    flag = shape((1,), jnp.int32)
    small = pltpu.CompilerParams(vmem_limit_bytes=2 * 1024 * 1024)

    def cost(flops, moved):
        return pl.CostEstimate(flops=flops, bytes_accessed=moved, transcendentals=0)

    cut = pl.pallas_call(
        cut_kernel,
        out_shape=[shape((2, total // count, LANES))] * groups,
        in_specs=[smem, vmem],
        out_specs=[vmem] * groups,
        compiler_params=small,
    )(place, raw_echo)
    near = jnp.stack([range_offsets, move(range_offsets, 1)])
    offsets = [near, move(near, 2)]

    child_angles = interp_weight.shape[4]
    steer = jnp.asarray(steer_blocks(pulse_count, child_angles))
    *made, made_flag = pl.pallas_call(
        functools.partial(table_kernel, pulse_count, total),
        out_shape=[
            shape((2, FIRST, second, LANES)),
            shape((2 * A0 // child_angles, 8 * child_angles, 2 * LANES)),
            shape((2, 2 * interp_weight.shape[3], 2 * child_angles)),
            shape((2, width // LANES, 2 * A0, LANES)),
            shape((2, width // LANES, 4 * A0, LANES)),
            flag,
        ],
        in_specs=[smem, smem] + [vmem] * 5,
        out_specs=[vmem] * 5 + [smem],
        cost_estimate=cost(2**30, 2**23),
        compiler_params=small,
    )(
        place,
        phase_rate,
        *offsets,
        range_filter.reshape(2, second, FIRST),
        interp_weight,
        steer,
    )

    own = [cut[0]] + [move(cut[step], QUAD * step) for step in range(1, groups)]
    sent = [pack(own[:2])]
    across = [move(sent[0], 2)]
    if groups > 2:
        own[2] = hold(own[2], made_flag, after=across[0])
    sent += own[2:]
    across += [move(piece, 2) for piece in own[2:]]
    beside = [move(piece, 1) for piece in sent]
    diagonal = [move(piece, 1) for piece in across]
    pieces = [part for four in zip(sent, beside, across, diagonal) for part in four]
    tables = [jnp.asarray(t) for t in dft_tables(total)]
    return focus(place, jnp.asarray(turn_table(total)), tables, made, pieces)


def solution(mesh):
    placed = (P(None, "ap", "grp"), P(), P(("grp", "ap")), P(), P())
    return jax.shard_map(
        body, mesh=mesh, in_specs=placed, out_specs=P(None, None, ("grp", "ap")), check_vma=False
    )
```

```python
import functools
import math

import jax
import jax.numpy as jnp
import ml_dtypes
import numpy as np
from jax import lax
from jax.experimental import pallas as pl
from jax.experimental.pallas import tpu as pltpu
from jax.sharding import PartitionSpec as P

A0 = 256
QUAD = 4
LANES = 128
FIRST = 16
TILE = 16


def as_real(matrix):
    top = np.concatenate([matrix.real, -matrix.imag], 1)
    low = np.concatenate([matrix.imag, matrix.real], 1)
    return np.concatenate([top, low], 0).astype(ml_dtypes.bfloat16)


def by_tile(matrix):
    shaped = matrix.reshape(2, -1, TILE, matrix.shape[1])
    return shaped.transpose(1, 0, 2, 3).reshape(matrix.shape)


def root(length, turns):
    return np.exp(-2j * np.pi / length * (turns % length))


def dft_tables(total):
    second = total // FIRST
    one = np.arange(FIRST)
    low = np.arange(TILE)
    k_one = one[:, None, None, None]
    l_row = low[None, :, None, None]
    n_one = one[None, None, :, None]
    l_col = low[None, None, None, :]
    same = l_row == l_col
    forward_one = root(FIRST, k_one * n_one) * root(total, l_row * k_one) * same
    forward_one = forward_one.reshape(FIRST * TILE, FIRST * TILE)
    two = np.arange(second)
    forward_two = root(second, two[:, None] * two[None, :])
    inverse_two = forward_two.conj()
    kept = np.arange(FIRST // QUAD)[:, None, None, None]
    inverse_one = (root(FIRST, kept * n_one) * root(total, l_col * n_one)).conj() * same
    inverse_one = inverse_one.reshape(FIRST // QUAD * TILE, FIRST * TILE)
    one, two, three, four = (
        as_real(t) for t in (forward_one, forward_two, inverse_two, inverse_one)
    )
    return [by_tile(one), by_tile(two), by_tile(by_tile(three).T).T, four]


def turn_table(total):
    chunks = total // FIRST // TILE
    value = root(total, TILE * np.arange(chunks)[:, None] * np.arange(FIRST)[None, :]).conj()
    return np.stack([value.real, value.imag]).astype(np.float32)


def steer_tiles(pulse_count, child_angles):
    size = (child_angles, LANES)
    lane = lax.broadcasted_iota(jnp.int32, size, 1)
    angle = lax.broadcasted_iota(jnp.int32, size, 0) + A0 // 2
    turn = (angle * (lane % pulse_count)) & (A0 - 1)
    real, imag = unit(turn.astype(jnp.float32) * (-2.0 * math.pi / A0))
    real, imag = real / math.sqrt(pulse_count), imag / math.sqrt(pulse_count)
    owner = lane // pulse_count
    rows = (((real, -imag), (-imag, -real)), ((imag, real), (real, -imag)))

    def tiles(pair, part):
        blocks = []
        for child in range(2):
            mine = owner == 2 * pair + child
            for piece in rows[part]:
                blocks.append(
                    jnp.concatenate([jnp.where(mine, side, 0.0) for side in piece], 1)
                )
        return jnp.concatenate(blocks, 0).astype(jnp.bfloat16)

    return tiles


def small_unit(angle):
    square = angle * angle
    cosine = 1.0 + square * (-1 / 2 + square * (1 / 24 + square * (-1 / 720 + square / 40320)))
    sine = angle * (1.0 + square * (-1 / 6 + square * (1 / 120 + square * (-1 / 5040))))
    return cosine, sine


def unit(angle):
    quarter = jnp.floor(angle * (2.0 / math.pi) + 0.5)
    rest = angle - quarter * 1.5703125
    rest = rest - quarter * (math.pi / 2 - 1.5703125)
    cosine, sine = small_unit(rest)
    turn = quarter.astype(jnp.int32)
    odd = (turn & 1) == 1
    first = jnp.where(odd, sine, cosine)
    second = jnp.where(odd, cosine, sine)
    first = jnp.where(((turn + 1) & 2) == 2, -first, first)
    second = jnp.where((turn & 2) == 2, -second, second)
    return first, second


def times(left, right):
    return (
        left[0] * right[0] - left[1] * right[1],
        left[0] * right[1] + left[1] * right[0],
    )


def cut_kernel(place_ref, raw_ref, *outs):
    for step, out in enumerate(outs):
        first = pl.multiple_of((place_ref[0] ^ step) * LANES, LANES)
        out[...] = raw_ref[:, :, pl.ds(first, LANES)]


def phase_rows(ref, rate, start, total):
    size = (LANES, LANES)
    blocks, angles = ref.shape[1], ref.shape[2]
    lane = lax.broadcasted_iota(jnp.int32, size, 1).astype(jnp.float32)
    factor = 1.0 + (lane + start) / total

    @pl.loop(0, angles // LANES)
    def _(part):
        row = lax.broadcasted_iota(jnp.int32, size, 0) + part * LANES
        slope = rate * ((row.astype(jnp.float32) + 0.5) / angles - 0.5)
        value = unit(slope * factor)
        step = small_unit(slope * (LANES / total))
        at = pl.ds(pl.multiple_of(part * LANES, LANES), LANES)
        for block in range(blocks):
            ref[0, block, at, :] = value[0].astype(jnp.bfloat16)
            ref[1, block, at, :] = value[1].astype(jnp.bfloat16)
            if block + 1 < blocks:
                value = times(value, step)


def weight_rows(pulse_count, weight_ref, one_ref, two_ref):
    steer = steer_tiles(pulse_count, weight_ref.shape[4])
    joined = jnp.concatenate([weight_ref[0, c, part] for c in range(2) for part in range(2)], 1)
    parents = joined.shape[0]
    width = one_ref.shape[2]
    lane = lax.broadcasted_iota(jnp.int32, (parents, width), 1)
    odd_pulse = lane % 2 == 1
    odd_child = lane // pulse_count % 2 == 1
    children = one_ref.shape[1] // 8
    for pair in range(2):
        for part in range(2):
            value = jnp.dot(
                joined, steer(pair, part), preferred_element_type=jnp.float32
            )
            for turn in range(2):
                turned = jnp.where(odd_pulse, -value, value) if turn else value
                kinds = (turned, jnp.where(odd_child, -turned, turned))
                for kind, rows in enumerate(kinds):
                    rows = rows.astype(jnp.bfloat16)
                    for first in range(0, parents, TILE):
                        block, tile = divmod(first, children)
                        row = (tile // TILE * 8 + pair * 4 + kind * 2 + part) * TILE
                        one_ref[turn * (parents // children) + block, row : row + TILE, :] = rows[
                            first : first + TILE
                        ]
    for child in range(2):
        for tile in range(parents // TILE):
            at = slice(tile * TILE, (tile + 1) * TILE)
            real, imag = weight_ref[1, child, 0, at], weight_ref[1, child, 1, at]
            row = 2 * tile * TILE
            two_ref[child, row : row + TILE] = jnp.concatenate([real, -imag], 1)
            two_ref[child, row + TILE : row + 2 * TILE] = jnp.concatenate([imag, real], 1)


def table_kernel(pulse_count, total, place_ref, rate_ref, *refs):
    offset_refs, filter_ref, weight_ref = refs[:2], *refs[2:4]
    gain_ref, one_ref, two_ref, phase_one_ref, phase_two_ref, done_ref = refs[4:]
    start = (place_ref[1] * (total // QUAD)).astype(jnp.float32)
    done_ref[0] = 1
    phase_rows(phase_one_ref, rate_ref[0], start, total)
    phase_rows(phase_two_ref, rate_ref[1], start, total)
    gain_rows(total, place_ref, offset_refs, filter_ref, gain_ref)
    weight_rows(pulse_count, weight_ref, one_ref, two_ref)


def gain_rows(total, place_ref, offset_refs, filter_ref, out_ref):
    second = total // FIRST
    member = place_ref[1]
    offsets = []
    known = [ref[row : row + 1, :] for ref in offset_refs for row in range(2)]
    for owner in range(QUAD):
        value = known[0]
        for rel in range(1, QUAD):
            value = jnp.where((member ^ rel) == owner, known[rel], value)
        offsets.append(value)
    offsets = jnp.concatenate(offsets, 1)
    shift = offsets - place_ref[1] * (total // QUAD)
    scale = -2.0 * math.pi / total

    def ramp(rows, stride):
        k_index = stride * lax.broadcasted_iota(jnp.int32, (rows, LANES), 0)
        return unit(scale * ((k_index * shift) & (total - 1)).astype(jnp.float32))

    low, high = ramp(FIRST, 1), ramp(second, FIRST)
    for k_one in range(FIRST):
        row = (low[0][k_one : k_one + 1] * (1.0 / total), low[1][k_one : k_one + 1] * (1.0 / total))
        column = (filter_ref[0, :, k_one : k_one + 1], filter_ref[1, :, k_one : k_one + 1])
        value = times(times(high, row), column)
        out_ref[0, k_one] = value[0].astype(jnp.bfloat16)
        out_ref[1, k_one] = value[1].astype(jnp.bfloat16)


def kernel(count, total, place_ref, turn_ref, *rest):
    fone_ref, ftwo_ref, itwo_ref, ione_ref = rest[:4]
    gain_ref, rows_one_ref, rows_two_ref, phase_one_ref, phase_two_ref = rest[4:9]
    pieces, out_ref, rest = rest[9:-8], rest[-8], rest[-7:]
    samples, partial_ref, folded, compressed, image, ready, sems = rest
    span = total // count
    second = total // FIRST
    chunks = second // TILE
    kept = FIRST // QUAD
    half = FIRST * TILE
    f32, bf16 = jnp.float32, jnp.bfloat16

    def dot(left, right):
        return jnp.dot(left, right, preferred_element_type=f32)

    def turned(real, imag, chunk, k_one, sign):
        cosine, sine = turn_ref[0, chunk, k_one], turn_ref[1, chunk, k_one] * sign
        return (
            (cosine * real - sine * imag).astype(bf16),
            (cosine * imag + sine * real).astype(bf16),
        )

    index = place_ref[0] * QUAD + place_ref[1]
    per_row = second // span
    for number, piece in enumerate(pieces):
        source = index ^ number
        rows = pl.ds(pl.multiple_of(source % per_row * span, TILE), span)
        samples[:, source // per_row, rows] = piece[...]

    @pl.loop(0, chunks // 2, unroll=True)
    def _(pair):
        right = jnp.concatenate(
            [
                samples[:, :, pl.ds((2 * pair + side) * TILE, TILE)].reshape(2 * half, LANES)
                for side in range(2)
            ],
            1,
        )
        result = dot(fone_ref[...], right)
        for side in range(2):
            chunk = 2 * pair + side
            lanes = slice(side * LANES, (side + 1) * LANES)
            for k_one in range(FIRST):
                row = 2 * k_one * TILE
                real = result[row : row + TILE, lanes]
                imag = result[row + TILE : row + 2 * TILE, lanes]
                real, imag = turned(real, imag, chunk, k_one, -1.0)
                partial_ref[k_one, 0, chunk] = real
                partial_ref[k_one, 1, chunk] = imag

    @pl.loop(0, FIRST // 2, unroll=True)
    def _(pair):
        right = jnp.concatenate(
            [partial_ref[2 * pair + side].reshape(2 * second, LANES) for side in range(2)], 1
        )
        result = dot(ftwo_ref[...], right)
        scaled = []
        for side in range(2):
            k_one = 2 * pair + side
            lanes = slice(side * LANES, (side + 1) * LANES)
            parts = []
            for chunk in range(chunks):
                row = 2 * chunk * TILE
                at = slice(chunk * TILE, (chunk + 1) * TILE)
                real = result[row : row + TILE, lanes]
                imag = result[row + TILE : row + 2 * TILE, lanes]
                gain_real = gain_ref[0, k_one, at].astype(f32)
                gain_imag = gain_ref[1, k_one, at].astype(f32)
                parts.append((real * gain_real - imag * gain_imag).astype(bf16))
                parts.append((real * gain_imag + imag * gain_real).astype(bf16))
            scaled.append(jnp.concatenate(parts, 0))
        result = dot(itwo_ref[...], jnp.concatenate(scaled, 1))
        for side in range(2):
            k_one = 2 * pair + side
            lanes = slice(side * LANES, (side + 1) * LANES)
            for chunk in range(chunks):
                row = 2 * chunk * TILE
                real = result[row : row + TILE, lanes]
                imag = result[row + TILE : row + 2 * TILE, lanes]
                real, imag = turned(real, imag, chunk, k_one, 1.0)
                folded[chunk, 0, k_one] = real
                folded[chunk, 1, k_one] = imag

    @pl.loop(0, chunks // 2, unroll=True)
    def _(pair):
        right = jnp.concatenate(
            [folded[2 * pair + side].reshape(2 * half, LANES) for side in range(2)], 1
        )
        result = dot(ione_ref[...], right).astype(bf16)
        for side in range(2):
            lanes = slice(side * LANES, (side + 1) * LANES)
            for part in range(2):
                for n_one in range(kept):
                    row = (part * kept + n_one) * TILE
                    compressed[n_one, 2 * pair + side, :, part * LANES : (part + 1) * LANES] = (
                        result[row : row + TILE, lanes]
                    )

    width = image.shape[4]
    blocks = width // LANES
    block_angles = image.shape[3]
    angle_blocks = image.shape[1]
    wide = rows_two_ref.shape[1] // 2
    steps = total // QUAD // width
    per_step = second // width

    def out_copy(step, slot):
        at = pl.ds(pl.multiple_of(step * width, width), width)
        return pltpu.make_async_copy(ready.at[slot], out_ref.at[:, :, at], sems.at[slot])

    @pl.loop(0, steps)
    def _(step):
        slot = step % 2
        tiles_wide = width // TILE
        first_tile = pl.multiple_of(step % per_step * tiles_wide, tiles_wide)
        columns = compressed[step // per_step, pl.ds(first_tile, tiles_wide)].reshape(
            width, 2 * LANES
        )

        def phases(ref, rows):
            return [
                jnp.concatenate(
                    [ref[part, step * blocks + b, rows, :] for b in range(blocks)], 1
                ).astype(f32)
                for part in range(2)
            ]

        for block in range(angle_blocks):
            result = lax.dot_general(
                rows_one_ref[block],
                columns,
                (((1,), (1,)), ((), ())),
                preferred_element_type=f32,
            )
            for tile in range(block_angles // TILE):
                at = slice(tile * TILE, (tile + 1) * TILE)
                cosine, sine = phases(
                    phase_one_ref, pl.ds(block * block_angles + tile * TILE, TILE)
                )
                for pick in range(2):
                    terms = [
                        result[row : row + TILE]
                        for row in [((tile * 2 + pick) * 4 + kind) * TILE for kind in range(4)]
                    ]
                    image[pick, block, 0, at] = (cosine * terms[0] + sine * terms[3]).astype(bf16)
                    image[pick, block, 1, at] = (cosine * terms[1] - sine * terms[2]).astype(bf16)

        @pl.when(step >= 2)
        def _():
            out_copy(step - 2, slot).wait()

        for block in range(angle_blocks):
            lower = dot(rows_two_ref[0], image[0, block].reshape(2 * block_angles, width))
            upper = dot(rows_two_ref[1], image[1, block].reshape(2 * block_angles, width))
            for tile in range(wide // TILE):
                rows = pl.ds(block * wide + tile * TILE, TILE)
                cosine, sine = phases(phase_two_ref, rows)
                real = slice(2 * tile * TILE, (2 * tile + 1) * TILE)
                imag = slice((2 * tile + 1) * TILE, (2 * tile + 2) * TILE)
                ready[slot, 0, rows, :] = cosine * (lower[real] + upper[real]) + sine * (
                    lower[imag] - upper[imag]
                )
                ready[slot, 1, rows, :] = cosine * (lower[imag] + upper[imag]) + sine * (
                    upper[real] - lower[real]
                )
        out_copy(step, slot).start()

    for step in range(max(steps - 2, 0), steps):
        out_copy(step, step % 2).wait()


def hold_kernel(*refs):
    pass


def hold(value, flag, after=None):
    far = pl.BlockSpec(memory_space=pl.ANY)
    others = [] if after is None else [after]
    return pl.pallas_call(
        hold_kernel,
        out_shape=jax.ShapeDtypeStruct(value.shape, value.dtype),
        in_specs=[far, pl.BlockSpec(memory_space=pltpu.SMEM)] + [far] * len(others),
        out_specs=far,
        input_output_aliases={0: 0},
        cost_estimate=pl.CostEstimate(flops=1, bytes_accessed=1, transcendentals=0),
        compiler_params=pltpu.CompilerParams(vmem_limit_bytes=1024 * 1024),
    )(value, flag, *others)


def focus(place, turns, tables, made, pieces):
    _, rows_one, rows_two, phase_one, _ = made
    count = len(pieces)
    total = phase_one.shape[1] * phase_one.shape[3] * QUAD
    second = total // FIRST
    chunks = second // TILE
    step_width = 256
    bf16, f32 = jnp.bfloat16, jnp.float32
    smem = pl.BlockSpec(memory_space=pltpu.SMEM)
    vmem = pl.BlockSpec(memory_space=pltpu.VMEM)
    far = pl.BlockSpec(memory_space=pltpu.HBM)
    parents, children = rows_two.shape[1] // 2, rows_two.shape[2] // 2
    angle_blocks = rows_one.shape[0]
    return pl.pallas_call(
        functools.partial(kernel, count, total),
        out_shape=jax.ShapeDtypeStruct((2, angle_blocks * parents, total // QUAD), f32),
        in_specs=[smem, smem] + [vmem] * (9 + count),
        out_specs=far,
        scratch_shapes=[
            pltpu.VMEM((2, FIRST, second, LANES), bf16),
            pltpu.VMEM((FIRST, 2, chunks, TILE, LANES), bf16),
            pltpu.VMEM((chunks, 2, FIRST, TILE, LANES), bf16),
            pltpu.VMEM((FIRST // QUAD, chunks, TILE, 2 * LANES), bf16),
            pltpu.VMEM((2, angle_blocks, 2, children, step_width), bf16),
            pltpu.VMEM((2, 2, angle_blocks * parents, step_width), f32),
            pltpu.SemaphoreType.DMA((2,)),
        ],
        compiler_params=pltpu.CompilerParams(vmem_limit_bytes=24 * 1024 * 1024),
    )(place, turns, *tables, *made, *pieces)


def body(raw_echo, range_filter, range_offsets, interp_weight, phase_rate):
    count = lax.axis_size("ap")
    index = lax.axis_index("ap")
    total = range_filter.shape[1]
    pulse_count = range_offsets.shape[0]
    groups = count // QUAD
    width = total // QUAD
    second = total // FIRST
    f32, bf16 = jnp.float32, jnp.bfloat16
    smem = pl.BlockSpec(memory_space=pltpu.SMEM)
    vmem = pl.BlockSpec(memory_space=pltpu.VMEM)
    place = jnp.stack([index // QUAD, index % QUAD]).astype(jnp.int32)

    def move(value, bits):
        return lax.ppermute(value, "ap", [(i, i ^ bits) for i in range(count)])

    def shape(dims, kind=bf16):
        return jax.ShapeDtypeStruct(dims, kind)

    flag = shape((1,), jnp.int32)
    small = pltpu.CompilerParams(vmem_limit_bytes=2 * 1024 * 1024)

    def cost(flops, moved):
        return pl.CostEstimate(flops=flops, bytes_accessed=moved, transcendentals=0)

    cut = pl.pallas_call(
        cut_kernel,
        out_shape=[shape((2, total // count, LANES))] * groups,
        in_specs=[smem, vmem],
        out_specs=[vmem] * groups,
        compiler_params=small,
    )(place, raw_echo)
    near = jnp.stack([range_offsets, move(range_offsets, 1)])
    offsets = [near, move(near, 2)]

    child_angles = interp_weight.shape[4]
    *made, made_flag = pl.pallas_call(
        functools.partial(table_kernel, pulse_count, total),
        out_shape=[
            shape((2, FIRST, second, LANES)),
            shape((2 * A0 // child_angles, 8 * child_angles, 2 * LANES)),
            shape((2, 2 * interp_weight.shape[3], 2 * child_angles)),
            shape((2, width // LANES, 2 * A0, LANES)),
            shape((2, width // LANES, 4 * A0, LANES)),
            flag,
        ],
        in_specs=[smem, smem] + [vmem] * 4,
        out_specs=[vmem] * 5 + [smem],
        cost_estimate=cost(2**30, 2**23),
        compiler_params=small,
    )(
        place,
        phase_rate,
        *offsets,
        range_filter.reshape(2, second, FIRST),
        interp_weight,
    )

    own = [cut[0]] + [move(cut[step], QUAD * step) for step in range(1, groups)]
    first = move(own[1], 2)
    own[2 % groups] = hold(own[2 % groups], made_flag, after=first)
    across = [move(own[0], 2), first] + [move(piece, 2) for piece in own[2:]]
    beside = [move(piece, 1) for piece in own]
    diagonal = [move(piece, 1) for piece in across]
    pieces = [part for four in zip(own, beside, across, diagonal) for part in four]
    tables = [jnp.asarray(t) for t in dft_tables(total)]
    return focus(place, jnp.asarray(turn_table(total)), tables, made, pieces)


def solution(mesh):
    placed = (P(None, "ap", "grp"), P(), P(("grp", "ap")), P(), P())
    return jax.shard_map(
        body, mesh=mesh, in_specs=placed, out_specs=P(None, None, ("grp", "ap")), check_vma=False
    )
```

```python
import functools
import math

import jax
import jax.numpy as jnp
import ml_dtypes
import numpy as np
from jax import lax
from jax.experimental import pallas as pl
from jax.experimental.pallas import tpu as pltpu
from jax.sharding import PartitionSpec as P

A0 = 256
QUAD = 4
LANES = 128
FIRST = 16
TILE = 16


def as_real(matrix):
    top = np.concatenate([matrix.real, -matrix.imag], 1)
    low = np.concatenate([matrix.imag, matrix.real], 1)
    return np.concatenate([top, low], 0).astype(ml_dtypes.bfloat16)


def by_tile(matrix):
    shaped = matrix.reshape(2, -1, TILE, matrix.shape[1])
    return shaped.transpose(1, 0, 2, 3).reshape(matrix.shape)


def root(length, turns):
    return np.exp(-2j * np.pi / length * (turns % length))


def dft_tables(total):
    second = total // FIRST
    one = np.arange(FIRST)
    low = np.arange(TILE)
    k_one = one[:, None, None, None]
    l_row = low[None, :, None, None]
    n_one = one[None, None, :, None]
    l_col = low[None, None, None, :]
    same = l_row == l_col
    forward_one = root(FIRST, k_one * n_one) * root(total, l_row * k_one) * same
    forward_one = forward_one.reshape(FIRST * TILE, FIRST * TILE)
    two = np.arange(second)
    forward_two = root(second, two[:, None] * two[None, :])
    inverse_two = forward_two.conj()
    kept = np.arange(FIRST // QUAD)[:, None, None, None]
    inverse_one = (root(FIRST, kept * n_one) * root(total, l_col * n_one)).conj() * same
    inverse_one = inverse_one.reshape(FIRST // QUAD * TILE, FIRST * TILE)
    one, two, three, four = (
        as_real(t) for t in (forward_one, forward_two, inverse_two, inverse_one)
    )
    return [by_tile(one), by_tile(two), by_tile(by_tile(three).T).T, four]


def turn_table(total):
    chunks = total // FIRST // TILE
    value = root(total, TILE * np.arange(chunks)[:, None] * np.arange(FIRST)[None, :]).conj()
    return np.stack([value.real, value.imag]).astype(np.float32)


def steer_tiles(pulse_count, child_angles):
    size = (child_angles, LANES)
    lane = lax.broadcasted_iota(jnp.int32, size, 1)
    angle = lax.broadcasted_iota(jnp.int32, size, 0) + A0 // 2
    turn = (angle * (lane % pulse_count)) & (A0 - 1)
    real, imag = unit(turn.astype(jnp.float32) * (-2.0 * math.pi / A0))
    real, imag = real / math.sqrt(pulse_count), imag / math.sqrt(pulse_count)
    owner = lane // pulse_count
    rows = (((real, -imag), (-imag, -real)), ((imag, real), (real, -imag)))

    def tiles(pair, part):
        blocks = []
        for child in range(2):
            mine = owner == 2 * pair + child
            for piece in rows[part]:
                blocks.append(
                    jnp.concatenate([jnp.where(mine, side, 0.0) for side in piece], 1)
                )
        return jnp.concatenate(blocks, 0).astype(jnp.bfloat16)

    return tiles


def small_unit(angle):
    square = angle * angle
    cosine = 1.0 + square * (-1 / 2 + square * (1 / 24 + square * (-1 / 720 + square / 40320)))
    sine = angle * (1.0 + square * (-1 / 6 + square * (1 / 120 + square * (-1 / 5040))))
    return cosine, sine


def unit(angle):
    quarter = jnp.floor(angle * (2.0 / math.pi) + 0.5)
    rest = angle - quarter * 1.5703125
    rest = rest - quarter * (math.pi / 2 - 1.5703125)
    cosine, sine = small_unit(rest)
    turn = quarter.astype(jnp.int32)
    odd = (turn & 1) == 1
    first = jnp.where(odd, sine, cosine)
    second = jnp.where(odd, cosine, sine)
    first = jnp.where(((turn + 1) & 2) == 2, -first, first)
    second = jnp.where((turn & 2) == 2, -second, second)
    return first, second


def times(left, right):
    return (
        left[0] * right[0] - left[1] * right[1],
        left[0] * right[1] + left[1] * right[0],
    )


def cut_kernel(place_ref, raw_ref, *outs):
    for step, out in enumerate(outs):
        first = pl.multiple_of((place_ref[0] ^ step) * LANES, LANES)
        out[...] = raw_ref[:, :, pl.ds(first, LANES)]


def phase_rows(ref, rate, start, total):
    size = (LANES, LANES)
    blocks, angles = ref.shape[1], ref.shape[2]
    lane = lax.broadcasted_iota(jnp.int32, size, 1).astype(jnp.float32)
    factor = 1.0 + (lane + start) / total

    @pl.loop(0, angles // LANES)
    def _(part):
        row = lax.broadcasted_iota(jnp.int32, size, 0) + part * LANES
        slope = rate * ((row.astype(jnp.float32) + 0.5) / angles - 0.5)
        value = unit(slope * factor)
        step = small_unit(slope * (LANES / total))
        at = pl.ds(pl.multiple_of(part * LANES, LANES), LANES)
        for block in range(blocks):
            ref[0, block, at, :] = value[0].astype(jnp.bfloat16)
            ref[1, block, at, :] = value[1].astype(jnp.bfloat16)
            if block + 1 < blocks:
                value = times(value, step)


def weight_rows(pulse_count, weight_ref, one_ref, two_ref):
    steer = steer_tiles(pulse_count, weight_ref.shape[4])
    joined = jnp.concatenate([weight_ref[0, c, part] for c in range(2) for part in range(2)], 1)
    parents = joined.shape[0]
    width = one_ref.shape[2]
    lane = lax.broadcasted_iota(jnp.int32, (parents, width), 1)
    odd_pulse = lane % 2 == 1
    odd_child = lane // pulse_count % 2 == 1
    children = one_ref.shape[1] // 8
    for pair in range(2):
        for part in range(2):
            value = jnp.dot(
                joined, steer(pair, part), preferred_element_type=jnp.float32
            )
            for turn in range(2):
                turned = jnp.where(odd_pulse, -value, value) if turn else value
                kinds = (turned, jnp.where(odd_child, -turned, turned))
                for kind, rows in enumerate(kinds):
                    rows = rows.astype(jnp.bfloat16)
                    for first in range(0, parents, TILE):
                        block, tile = divmod(first, children)
                        row = (tile // TILE * 8 + pair * 4 + kind * 2 + part) * TILE
                        one_ref[turn * (parents // children) + block, row : row + TILE, :] = rows[
                            first : first + TILE
                        ]
    for child in range(2):
        for tile in range(parents // TILE):
            at = slice(tile * TILE, (tile + 1) * TILE)
            real, imag = weight_ref[1, child, 0, at], weight_ref[1, child, 1, at]
            row = 2 * tile * TILE
            two_ref[child, row : row + TILE] = jnp.concatenate([real, -imag], 1)
            two_ref[child, row + TILE : row + 2 * TILE] = jnp.concatenate([imag, real], 1)


def table_kernel(pulse_count, total, place_ref, rate_ref, *refs):
    offset_refs, filter_ref, weight_ref = refs[:2], *refs[2:4]
    gain_ref, one_ref, two_ref, phase_one_ref, phase_two_ref, done_ref = refs[4:]
    start = (place_ref[1] * (total // QUAD)).astype(jnp.float32)
    done_ref[0] = 1
    phase_rows(phase_one_ref, rate_ref[0], start, total)
    phase_rows(phase_two_ref, rate_ref[1], start, total)
    gain_rows(total, place_ref, offset_refs, filter_ref, gain_ref)
    weight_rows(pulse_count, weight_ref, one_ref, two_ref)


def gain_rows(total, place_ref, offset_refs, filter_ref, out_ref):
    second = total // FIRST
    member = place_ref[1]
    offsets = []
    known = [ref[row : row + 1, :] for row in range(2) for ref in offset_refs]
    for owner in range(QUAD):
        value = known[0]
        for rel in range(1, QUAD):
            value = jnp.where((member ^ rel) == owner, known[rel], value)
        offsets.append(value)
    offsets = jnp.concatenate(offsets, 1)
    shift = offsets - place_ref[1] * (total // QUAD)
    scale = -2.0 * math.pi / total

    def ramp(rows, stride):
        k_index = stride * lax.broadcasted_iota(jnp.int32, (rows, LANES), 0)
        return unit(scale * ((k_index * shift) & (total - 1)).astype(jnp.float32))

    low, high = ramp(FIRST, 1), ramp(second, FIRST)
    for k_one in range(FIRST):
        row = (low[0][k_one : k_one + 1] * (1.0 / total), low[1][k_one : k_one + 1] * (1.0 / total))
        column = (filter_ref[0, :, k_one : k_one + 1], filter_ref[1, :, k_one : k_one + 1])
        value = times(times(high, row), column)
        out_ref[0, k_one] = value[0].astype(jnp.bfloat16)
        out_ref[1, k_one] = value[1].astype(jnp.bfloat16)


def kernel(count, total, place_ref, turn_ref, *rest):
    fone_ref, ftwo_ref, itwo_ref, ione_ref = rest[:4]
    gain_ref, rows_one_ref, rows_two_ref, phase_one_ref, phase_two_ref = rest[4:9]
    pieces, out_ref, rest = rest[9:-8], rest[-8], rest[-7:]
    samples, partial_ref, folded, compressed, image, ready, sems = rest
    span = total // count
    second = total // FIRST
    chunks = second // TILE
    kept = FIRST // QUAD
    half = FIRST * TILE
    f32, bf16 = jnp.float32, jnp.bfloat16

    def dot(left, right):
        return jnp.dot(left, right, preferred_element_type=f32)

    def turned(real, imag, chunk, k_one, sign):
        cosine, sine = turn_ref[0, chunk, k_one], turn_ref[1, chunk, k_one] * sign
        return (
            (cosine * real - sine * imag).astype(bf16),
            (cosine * imag + sine * real).astype(bf16),
        )

    index = place_ref[0] * QUAD + place_ref[1]
    per_row = second // span
    for number, piece in enumerate(pieces):
        source = index ^ number
        rows = pl.ds(pl.multiple_of(source % per_row * span, TILE), span)
        samples[:, source // per_row, rows] = piece[...]

    @pl.loop(0, chunks // 2, unroll=True)
    def _(pair):
        right = jnp.concatenate(
            [
                samples[:, :, pl.ds((2 * pair + side) * TILE, TILE)].reshape(2 * half, LANES)
                for side in range(2)
            ],
            1,
        )
        result = dot(fone_ref[...], right)
        for side in range(2):
            chunk = 2 * pair + side
            lanes = slice(side * LANES, (side + 1) * LANES)
            for k_one in range(FIRST):
                row = 2 * k_one * TILE
                real = result[row : row + TILE, lanes]
                imag = result[row + TILE : row + 2 * TILE, lanes]
                real, imag = turned(real, imag, chunk, k_one, -1.0)
                partial_ref[k_one, 0, chunk] = real
                partial_ref[k_one, 1, chunk] = imag

    @pl.loop(0, FIRST // 2, unroll=True)
    def _(pair):
        right = jnp.concatenate(
            [partial_ref[2 * pair + side].reshape(2 * second, LANES) for side in range(2)], 1
        )
        result = dot(ftwo_ref[...], right)
        scaled = []
        for side in range(2):
            k_one = 2 * pair + side
            lanes = slice(side * LANES, (side + 1) * LANES)
            parts = []
            for chunk in range(chunks):
                row = 2 * chunk * TILE
                at = slice(chunk * TILE, (chunk + 1) * TILE)
                real = result[row : row + TILE, lanes]
                imag = result[row + TILE : row + 2 * TILE, lanes]
                gain_real = gain_ref[0, k_one, at].astype(f32)
                gain_imag = gain_ref[1, k_one, at].astype(f32)
                parts.append((real * gain_real - imag * gain_imag).astype(bf16))
                parts.append((real * gain_imag + imag * gain_real).astype(bf16))
            scaled.append(jnp.concatenate(parts, 0))
        result = dot(itwo_ref[...], jnp.concatenate(scaled, 1))
        for side in range(2):
            k_one = 2 * pair + side
            lanes = slice(side * LANES, (side + 1) * LANES)
            for chunk in range(chunks):
                row = 2 * chunk * TILE
                real = result[row : row + TILE, lanes]
                imag = result[row + TILE : row + 2 * TILE, lanes]
                real, imag = turned(real, imag, chunk, k_one, 1.0)
                folded[chunk, 0, k_one] = real
                folded[chunk, 1, k_one] = imag

    @pl.loop(0, chunks // 2, unroll=True)
    def _(pair):
        right = jnp.concatenate(
            [folded[2 * pair + side].reshape(2 * half, LANES) for side in range(2)], 1
        )
        result = dot(ione_ref[...], right).astype(bf16)
        for side in range(2):
            lanes = slice(side * LANES, (side + 1) * LANES)
            for part in range(2):
                for n_one in range(kept):
                    row = (part * kept + n_one) * TILE
                    compressed[n_one, 2 * pair + side, :, part * LANES : (part + 1) * LANES] = (
                        result[row : row + TILE, lanes]
                    )

    width = image.shape[4]
    blocks = width // LANES
    block_angles = image.shape[3]
    angle_blocks = image.shape[1]
    wide = rows_two_ref.shape[1] // 2
    steps = total // QUAD // width
    per_step = second // width

    def out_copy(step, slot):
        at = pl.ds(pl.multiple_of(step * width, width), width)
        return pltpu.make_async_copy(ready.at[slot], out_ref.at[:, :, at], sems.at[slot])

    @pl.loop(0, steps)
    def _(step):
        slot = step % 2
        tiles_wide = width // TILE
        first_tile = pl.multiple_of(step % per_step * tiles_wide, tiles_wide)
        columns = compressed[step // per_step, pl.ds(first_tile, tiles_wide)].reshape(
            width, 2 * LANES
        )

        def phases(ref, rows):
            return [
                jnp.concatenate(
                    [ref[part, step * blocks + b, rows, :] for b in range(blocks)], 1
                ).astype(f32)
                for part in range(2)
            ]

        for block in range(angle_blocks):
            result = lax.dot_general(
                rows_one_ref[block],
                columns,
                (((1,), (1,)), ((), ())),
                preferred_element_type=f32,
            )
            for tile in range(block_angles // TILE):
                at = slice(tile * TILE, (tile + 1) * TILE)
                cosine, sine = phases(
                    phase_one_ref, pl.ds(block * block_angles + tile * TILE, TILE)
                )
                for pick in range(2):
                    terms = [
                        result[row : row + TILE]
                        for row in [((tile * 2 + pick) * 4 + kind) * TILE for kind in range(4)]
                    ]
                    image[pick, block, 0, at] = (cosine * terms[0] + sine * terms[3]).astype(bf16)
                    image[pick, block, 1, at] = (cosine * terms[1] - sine * terms[2]).astype(bf16)

        @pl.when(step >= 2)
        def _():
            out_copy(step - 2, slot).wait()

        for block in range(angle_blocks):
            lower = dot(rows_two_ref[0], image[0, block].reshape(2 * block_angles, width))
            upper = dot(rows_two_ref[1], image[1, block].reshape(2 * block_angles, width))
            for tile in range(wide // TILE):
                rows = pl.ds(block * wide + tile * TILE, TILE)
                cosine, sine = phases(phase_two_ref, rows)
                real = slice(2 * tile * TILE, (2 * tile + 1) * TILE)
                imag = slice((2 * tile + 1) * TILE, (2 * tile + 2) * TILE)
                ready[slot, 0, rows, :] = cosine * (lower[real] + upper[real]) + sine * (
                    lower[imag] - upper[imag]
                )
                ready[slot, 1, rows, :] = cosine * (lower[imag] + upper[imag]) + sine * (
                    upper[real] - lower[real]
                )
        out_copy(step, slot).start()

    for step in range(max(steps - 2, 0), steps):
        out_copy(step, step % 2).wait()


def hold_kernel(*refs):
    pass


def hold(value, flag, after=None):
    far = pl.BlockSpec(memory_space=pl.ANY)
    others = [] if after is None else [after]
    return pl.pallas_call(
        hold_kernel,
        out_shape=jax.ShapeDtypeStruct(value.shape, value.dtype),
        in_specs=[far, pl.BlockSpec(memory_space=pltpu.SMEM)] + [far] * len(others),
        out_specs=far,
        input_output_aliases={0: 0},
        cost_estimate=pl.CostEstimate(flops=1, bytes_accessed=1, transcendentals=0),
        compiler_params=pltpu.CompilerParams(vmem_limit_bytes=1024 * 1024),
    )(value, flag, *others)


def focus(place, turns, tables, made, pieces):
    _, rows_one, rows_two, phase_one, _ = made
    count = len(pieces)
    total = phase_one.shape[1] * phase_one.shape[3] * QUAD
    second = total // FIRST
    chunks = second // TILE
    step_width = 256
    bf16, f32 = jnp.bfloat16, jnp.float32
    smem = pl.BlockSpec(memory_space=pltpu.SMEM)
    vmem = pl.BlockSpec(memory_space=pltpu.VMEM)
    far = pl.BlockSpec(memory_space=pltpu.HBM)
    parents, children = rows_two.shape[1] // 2, rows_two.shape[2] // 2
    angle_blocks = rows_one.shape[0]
    return pl.pallas_call(
        functools.partial(kernel, count, total),
        out_shape=jax.ShapeDtypeStruct((2, angle_blocks * parents, total // QUAD), f32),
        in_specs=[smem, smem] + [vmem] * (9 + count),
        out_specs=far,
        scratch_shapes=[
            pltpu.VMEM((2, FIRST, second, LANES), bf16),
            pltpu.VMEM((FIRST, 2, chunks, TILE, LANES), bf16),
            pltpu.VMEM((chunks, 2, FIRST, TILE, LANES), bf16),
            pltpu.VMEM((FIRST // QUAD, chunks, TILE, 2 * LANES), bf16),
            pltpu.VMEM((2, angle_blocks, 2, children, step_width), bf16),
            pltpu.VMEM((2, 2, angle_blocks * parents, step_width), f32),
            pltpu.SemaphoreType.DMA((2,)),
        ],
        compiler_params=pltpu.CompilerParams(vmem_limit_bytes=24 * 1024 * 1024),
    )(place, turns, *tables, *made, *pieces)


def body(raw_echo, range_filter, range_offsets, interp_weight, phase_rate):
    count = lax.axis_size("ap")
    index = lax.axis_index("ap")
    total = range_filter.shape[1]
    pulse_count = range_offsets.shape[0]
    groups = count // QUAD
    width = total // QUAD
    second = total // FIRST
    f32, bf16 = jnp.float32, jnp.bfloat16
    smem = pl.BlockSpec(memory_space=pltpu.SMEM)
    vmem = pl.BlockSpec(memory_space=pltpu.VMEM)
    place = jnp.stack([index // QUAD, index % QUAD]).astype(jnp.int32)

    def move(value, bits):
        return lax.ppermute(value, "ap", [(i, i ^ bits) for i in range(count)])

    def shape(dims, kind=bf16):
        return jax.ShapeDtypeStruct(dims, kind)

    flag = shape((1,), jnp.int32)
    small = pltpu.CompilerParams(vmem_limit_bytes=2 * 1024 * 1024)

    def cost(flops, moved):
        return pl.CostEstimate(flops=flops, bytes_accessed=moved, transcendentals=0)

    cut = pl.pallas_call(
        cut_kernel,
        out_shape=[shape((2, total // count, LANES))] * groups,
        in_specs=[smem, vmem],
        out_specs=[vmem] * groups,
        compiler_params=small,
    )(place, raw_echo)
    column = jnp.stack([range_offsets, move(range_offsets, 2)])
    offsets = [column, move(column, 1)]

    child_angles = interp_weight.shape[4]
    *made, made_flag = pl.pallas_call(
        functools.partial(table_kernel, pulse_count, total),
        out_shape=[
            shape((2, FIRST, second, LANES)),
            shape((2 * A0 // child_angles, 8 * child_angles, 2 * LANES)),
            shape((2, 2 * interp_weight.shape[3], 2 * child_angles)),
            shape((2, width // LANES, 2 * A0, LANES)),
            shape((2, width // LANES, 4 * A0, LANES)),
            flag,
        ],
        in_specs=[smem, smem] + [vmem] * 4,
        out_specs=[vmem] * 5 + [smem],
        cost_estimate=cost(2**30, 2**23),
        compiler_params=small,
    )(
        place,
        phase_rate,
        *offsets,
        range_filter.reshape(2, second, FIRST),
        interp_weight,
    )

    own = [cut[0]] + [move(cut[step], QUAD * step) for step in range(1, groups)]
    first = move(own[1], 2)
    own[2 % groups] = hold(own[2 % groups], made_flag, after=first)
    across = [move(own[0], 2), first] + [move(piece, 2) for piece in own[2:]]
    beside = [move(piece, 1) for piece in own]
    diagonal = [move(piece, 1) for piece in across]
    pieces = [part for four in zip(own, beside, across, diagonal) for part in four]
    tables = [jnp.asarray(t) for t in dft_tables(total)]
    return focus(place, jnp.asarray(turn_table(total)), tables, made, pieces)


def solution(mesh):
    placed = (P(None, "ap", "grp"), P(), P(("grp", "ap")), P(), P())
    return jax.shard_map(
        body, mesh=mesh, in_specs=placed, out_specs=P(None, None, ("grp", "ap")), check_vma=False
    )
```
